32 devices in a mesh: clu: 8 (over z, y), col: 4 (over x, core).
Axes of the slice: x: 2, y: 2, z: 4, core: 2. Of those that a mesh axis runs over, the one named last changes fastest.
Arguments:
- features: bfloat16 [8192, 2048], P('clu', 'col'), may hold values from -6 to 6
- weight: bfloat16 [2048, 2048], P(None, 'col'), may hold values from -0.125 to 0.125
- layer_bias: bfloat16 [2048], P('col'), may hold values from -3 to 3
- cotangent: bfloat16 [8192, 2048], P('clu', 'col'), may hold values from -24 to 24
- self_weight: float32 [8192], P('clu'), may hold values from 0.1 to 0.4
- local_index: int32 [8192, 16], P('clu'), may hold values from 0 to 1023
- local_weight: float32 [8192, 16], P('clu'), may hold values from 0.1 to 0.4
- send_index: int32 [8, 8, 64], P('clu'), may hold values from -1 to 1023, as said below
- remote_slot: int32 [8192, 8], P('clu'), may hold values from 0 to 511, as said below
- remote_weight: float32 [8192, 8], P('clu'), may hold values from 0.1 to 0.4
Outputs:
- activations: bfloat16 [8192, 2048], P('clu')
- input_grad: bfloat16 [8192, 2048], P('clu', 'col')
- weight_grad: float32 [2048, 2048], P(None, 'col')
- bias_grad: float32 [2048], P('col')
The draws below stay inside these ranges and needn't reach their ends.
Inputs may be any that keep to these rules, and one draw needn't show every extreme that they name: Entries send_index[s, t, j] for j below a count n(s, t) are row numbers of cluster s read by cluster t; the rest are -1. n(s, s) = 0; otherwise 1 <= n(s, t) <= 64, and every cluster sends 64 rows to one other cluster and receives 64 rows from one other cluster. remote_slot[i, k] = s * 64 + j names a slot j < n(s, t) of a cluster s different from i's cluster t, so it always holds a sent row.
All inputs are finite; a program needn't handle non-finite values.
Results may differ from the reference program's by a relative error of at most 0.015.
Values may be sent and summed in bfloat16 or wider, within the bound.
A program may use at most 128 MiB of HBM per device.

```python
import math
import jax
import jax.numpy as jnp
from jax import lax

WIDTH = 2048
ROWS = 1024
SLOTS = 64
LOCAL_EDGES = 16
REMOTE_EDGES = 8
CLUSTERS = 8
NODES = 8192


def pair_counts(key):
    key = jax.random.fold_in(key, 101)
    first, second, third = jax.random.split(key, 3)
    draw_one = jax.random.randint(first, (CLUSTERS, CLUSTERS), 1, SLOTS + 1)
    draw_two = jax.random.randint(second, (CLUSTERS, CLUSTERS), 1, SLOTS + 1)
    counts = jnp.maximum(draw_one, draw_two)
    offset = jax.random.randint(third, (), 1, CLUSTERS)
    source = jnp.arange(CLUSTERS, dtype=jnp.int32)[:, None]
    target = jnp.arange(CLUSTERS, dtype=jnp.int32)[None, :]
    counts = jnp.where(target == (source + offset) % CLUSTERS, SLOTS, counts)
    counts = jnp.where(source == target, 0, counts)
    return (counts.astype(jnp.int32), offset.astype(jnp.int32))


def draw_send_index(key, part):
    counts, shift_by = pair_counts(key)
    key = jax.random.fold_in(key, 7)
    picked = jax.random.randint(key, (CLUSTERS, CLUSTERS, SLOTS), 0, ROWS)
    position = jnp.arange(SLOTS, dtype=jnp.int32)[None, None, :]
    return jnp.where(position < counts[:, :, None], picked, -1).astype(jnp.int32)


def draw_remote_slot(key, part):
    counts, shift_by = pair_counts(key)
    key = jax.random.fold_in(key, 11)
    first, second = jax.random.split(key)
    offset = jax.random.randint(first, (NODES, REMOTE_EDGES), 0, CLUSTERS - 1)
    target = (jnp.arange(NODES, dtype=jnp.int32) // ROWS)[:, None]
    source = (target + 1 + offset) % CLUSTERS
    limit = counts[source, target]
    raw = jax.random.randint(second, (NODES, REMOTE_EDGES), 0, 1 << 20)
    slots = (source * SLOTS + raw % limit).astype(jnp.int32)
    full_target = (CLUSTERS - 1 + shift_by) % CLUSTERS
    slots = slots.at[full_target * ROWS, 0].set(CLUSTERS * SLOTS - 1)
    slots = slots.at[ROWS + 1, 0].set(0)
    return slots.astype(jnp.int32)


def draw_cotangent(key, part):
    key = jax.random.fold_in(key, 23)
    first = jax.random.fold_in(key, 0)
    cluster = (jnp.arange(NODES) // ROWS).astype(jnp.float32)
    rising = 1.0 + 2.0 * cluster / (CLUSTERS - 1)
    base = jnp.clip(jax.random.normal(first, (NODES, WIDTH), jnp.float32), -6.0, 6.0)
    return (base * rising[:, None]).astype(jnp.bfloat16)


def set_ends(values, key, smallest, top_value):
    shape = values.shape
    spot = [jax.random.randint(jax.random.fold_in(key, axis), (), 0, shape[axis]) for axis in range(len(shape))]
    values = values.at[tuple(spot)].set(smallest)
    longest = shape.index(max(shape))
    spot[longest] = (spot[longest] + 1) % shape[longest]
    return values.at[tuple(spot)].set(top_value)


def block_scale(own_key, dims, pieces, least, top_value):
    factor_of = 1.0
    for axis_at, parts in pieces:
        draws = jax.random.uniform(jax.random.fold_in(jax.random.fold_in(own_key, 6), axis_at), (parts,), jnp.float32, least / len(pieces), top_value / len(pieces))
        factor_of = factor_of * jnp.repeat(jnp.exp(draws), dims[axis_at] // parts).reshape((-1,) + (1,) * (len(dims) - 1 - axis_at))
    return factor_of


def bell_draw(key, extent, deviation, bound, cuts=(), kind=jnp.bfloat16):
    level = block_scale(key, extent, cuts, -0.22, 0.18) if cuts else 1.0
    drawn = jax.random.normal(key, extent, jnp.float32) * deviation * level
    return jnp.minimum(jnp.maximum(drawn, -bound), bound).astype(kind)


def setup_inputs(seed: int = 0) -> dict:
    seeds = jax.random.split(jax.random.key(seed), 11)
    features = bell_draw(seeds[0], (NODES, WIDTH), 1.0, 6.0, ((0, 8), (1, 4)))
    weight = bell_draw(seeds[1], (WIDTH, WIDTH), WIDTH ** -0.5, 0.125, ((1, 4),))
    layer_bias = bell_draw(seeds[2], (WIDTH,), 0.5, 3.0, ((0, 4),))
    cotangent = draw_cotangent(jax.random.fold_in(seeds[10], 71), 0)
    self_weight = jnp.clip(jnp.exp(math.log(0.4) - 1.3862944 * jax.random.uniform(seeds[4], (NODES,), jnp.float32) ** block_scale(seeds[4], (NODES,), ((0, 8),), -0.2, 0.2)), 0.1, 0.4)
    local_index = set_ends(jax.random.randint(seeds[5], (NODES, LOCAL_EDGES), 0, ROWS), jax.random.fold_in(seeds[5], 1), 0, ROWS - 1).astype(jnp.int32)
    local_weight = jnp.clip(jnp.exp(math.log(0.4) - 1.3862944 * jax.random.uniform(seeds[6], (NODES, LOCAL_EDGES), jnp.float32) ** block_scale(seeds[6], (NODES, LOCAL_EDGES), ((0, 8),), -0.2, 0.2)), 0.1, 0.4)
    send_index = draw_send_index(jax.random.fold_in(seeds[10], 71), 0)
    remote_slot = draw_remote_slot(jax.random.fold_in(seeds[10], 71), 0)
    remote_weight = jnp.clip(jnp.exp(math.log(0.4) - 1.3862944 * jax.random.uniform(seeds[9], (NODES, REMOTE_EDGES), jnp.float32) ** block_scale(seeds[9], (NODES, REMOTE_EDGES), ((0, 8),), -0.2, 0.2)), 0.1, 0.4)
    return dict(features=features, weight=weight, layer_bias=layer_bias, cotangent=cotangent, self_weight=self_weight, local_index=local_index, local_weight=local_weight, send_index=send_index, remote_slot=remote_slot, remote_weight=remote_weight)


enhance = 1.0

@jax.custom_vjp
def low(v):
    return lax.optimization_barrier(v.astype(jnp.bfloat16)).astype(jnp.float32)

@jax.custom_vjp
def low_back(v):
    return v

def low_keep(v):
    return (low(v), None)

def low_pass(kept, grad):
    return (grad,)

def back_keep(v):
    return (v, None)

def back_low(kept, grad):
    return (low(grad),)
low.defvjp(low_keep, low_pass)
low_back.defvjp(back_keep, back_low)

def reference(features, weight, layer_bias, cotangent, self_weight, local_index, local_weight, send_index, remote_slot, remote_weight):
    inputs = features.astype(jnp.float32)
    matrix = weight.astype(jnp.float32)
    offset = layer_bias.astype(jnp.float32)

    def forward(inputs, matrix, offset):

        def aggregate_one(cluster):
            start = cluster * ROWS
            own = lax.dynamic_slice_in_dim(inputs, start, ROWS, 0)
            neighbours = lax.dynamic_slice_in_dim(local_index, start, ROWS, 0)
            near_weight = lax.dynamic_slice_in_dim(local_weight, start, ROWS, 0)
            diagonal = lax.dynamic_slice_in_dim(self_weight, start, ROWS, 0)
            far_slots = lax.dynamic_slice_in_dim(remote_slot, start, ROWS, 0)
            far_weight = lax.dynamic_slice_in_dim(remote_weight, start, ROWS, 0)
            send_plan = lax.dynamic_index_in_dim(send_index, cluster, 1, keepdims=False)
            anchor = jnp.arange(CLUSTERS, dtype=jnp.int32)[:, None] * ROWS + jnp.maximum(send_plan, 0).astype(jnp.int32)
            pooled = jnp.where((send_plan >= 0)[:, :, None], inputs[anchor], 0.0)
            pooled = low_back(pooled.reshape(CLUSTERS * SLOTS, WIDTH))
            near = jnp.einsum('rk,rkf->rf', near_weight, own[neighbours], precision=lax.Precision.HIGHEST)
            far = jnp.einsum('rk,rkf->rf', far_weight, pooled[far_slots], precision=lax.Precision.HIGHEST)
            return (1.0 + enhance) * diagonal[:, None] * own + near + far
        gathered = lax.map(jax.checkpoint(aggregate_one), jnp.arange(CLUSTERS, dtype=jnp.int32))
        gathered = gathered.reshape(NODES, WIDTH)
        linear = jnp.dot(low(gathered), matrix, precision=lax.Precision.HIGHEST, preferred_element_type=jnp.float32)
        preact = low_back(linear + offset)
        return jax.nn.gelu(preact, approximate=False)
    result, backward = jax.vjp(forward, inputs, matrix, offset)
    grad_input, grad_matrix, grad_offset = backward(cotangent.astype(jnp.float32))
    return (result.astype(jnp.bfloat16), grad_input.astype(jnp.bfloat16), grad_matrix, grad_offset)
```

```python
import functools
import math

import jax
import jax.numpy as jnp
from jax import lax
from jax.experimental import pallas as pl
from jax.experimental.pallas import tpu as pltpu
from jax.sharding import PartitionSpec as P

enhance = 1.0
f32, bf16, i32 = jnp.float32, jnp.bfloat16, jnp.int32
MESH = pl.DeviceIdType.MESH
BLOCKS = 4
HALVES = 2
UNROLL = 8


def tn(a, b):
    return lax.dot_general(a, b, (((0,), (0,)), ((), ())), preferred_element_type=f32)


def nt(a, b):
    return lax.dot_general(a, b, (((1,), (1,)), ((), ())), preferred_element_type=f32)


def nn(a, b):
    return jnp.dot(a, b, preferred_element_type=f32)


def layer(
    feat, weight_in, bias, cot_in, selfw, lidx, lwgt, send, ridx, rwgt,
    act_out, ig_out, wg_out, bg_out,
    w_v, cot_v, sel, near, far, edge_pos, edge_w, outg, incg, wide, merged, act, glow, keep_own, keep_far,
    csend, crecv, xsend, xrecv, gm, wacc, ysend, yrecv, zsend, zrecv, wfin, bsend, brecv, ret,
    load_s, in_s, in_r, tab_s, tab_r, mx_s, mx_r, mc_s, mc_r, mf_s, mf_r, rc_s, rc_r, rx_s, rx_r,
    y_s, y_r, z_s, z_r, zg_s, zg_r, yg_s, yg_r, b_s, b_r, ret_s, ret_r, ax_s, ax_r, ac_s, ac_r, af_s, af_r, out_s,
    *, n, ncol,
):
    rows, part = feat.shape
    half = part // HALVES
    rb = rows // BLOCKS
    slots = send.shape[1]
    gd = min(8, n)
    groups = n // gd
    gs = gd * slots
    depth = n // 2
    kb = wacc.shape[0] // n

    me = lax.axis_index("clu")
    col = lax.axis_index("col")
    zz, yy = lax.div(me, 2), lax.rem(me, 2)
    core = lax.rem(col, 2)
    pair = col + 1 - 2 * core
    xcol = lax.rem(col + ncol // 2, ncol)
    dcol = lax.rem(pair + ncol // 2, ncol)
    ypeer = (me + 1 - 2 * yy, col)
    pending = []

    def put(src, dst, ss, rs, dev):
        copy = pltpu.make_async_remote_copy(
            src_ref=src, dst_ref=dst, send_sem=ss, recv_sem=rs, device_id=dev, device_id_type=MESH
        )
        copy.start()
        pending.append(copy)

    def got(dst, rs):
        pltpu.make_async_remote_copy(
            src_ref=dst, dst_ref=dst, send_sem=rs, recv_sem=rs, device_id=(me, pair), device_id_type=MESH
        ).wait_recv()

    def sent(src, ss):
        pltpu.make_async_remote_copy(
            src_ref=src, dst_ref=src, send_sem=ss, recv_sem=ss, device_id=(me, pair), device_id_type=MESH
        ).wait_send()

    def peers(step):
        def body(k, carry):
            step(lax.rem(me + k, n))
            return carry

        lax.fori_loop(1, n, body, 0)

    load_w = pltpu.make_async_copy(weight_in, w_v, load_s.at[0])
    load_c = pltpu.make_async_copy(cot_in, cot_v, load_s.at[1])
    load_w.start()
    load_c.start()
    barrier = pltpu.get_barrier_semaphore()
    peers(lambda t: pl.semaphore_signal(barrier, inc=1, device_id=(t, col), device_id_type=MESH))
    for other in (pair, xcol):
        pl.semaphore_signal(barrier, inc=1, device_id=(me, other), device_id_type=MESH)

    lane = lax.broadcasted_iota(i32, (slots, rows), 1)

    def put_selector(g):
        ids = send[g * gd : (g + 1) * gd, :].T
        for d in range(gd):
            sel[d * slots : (d + 1) * slots, :] = jnp.where(ids[:, d : d + 1] == lane, 1.0, 0.0).astype(bf16)

    def in_copy(h, t):
        pltpu.make_async_remote_copy(
            src_ref=outg.at[h, t], dst_ref=incg.at[h, me], send_sem=in_s.at[h, t], recv_sem=in_r.at[h, me],
            device_id=(t, col), device_id_type=MESH,
        ).start()

    for h in range(HALVES):
        for g in range(groups):
            if groups > 1 or h == 0:
                put_selector(g)
            rows_out = nn(sel[...], feat[:, h * half : (h + 1) * half]).astype(bf16)
            outg[h, g * gd : (g + 1) * gd] = rows_out.reshape(gd, slots, half)
        if h == 0:
            pl.semaphore_wait(barrier, n + 1)
        peers(functools.partial(in_copy, h))
        incg[h, me] = jnp.zeros((slots, half), bf16)

    local_edges, far_edges = lidx.shape[1], ridx.shape[1]
    first_far = local_edges + 1

    def put_edges(at, idx, w):
        for k in range(idx.shape[0]):
            edge_pos[at + k] = jnp.broadcast_to(idx[k : k + 1, :], (8, rows))
            edge_w[at + k] = jnp.broadcast_to(w[k : k + 1, :], (8, rows))

    put_edges(0, lidx[...].T, lwgt[...].T)
    put_edges(local_edges, lax.broadcasted_iota(i32, (1, rows), 1), (1.0 + enhance) * selfw[...])
    put_edges(first_far, ridx[...].T, rwgt[...].T)
    sub = lax.broadcasted_iota(i32, (8, 128), 0)

    def table(dst, first, count, base, edge_from, edge_to):
        tall = 16 * UNROLL

        def lanes(l, carry):
            ls = pl.ds(pl.multiple_of(l * 128, 128), 128)

            def step(b, carry):
                r0 = first + b * tall
                places = [sub + (base + r0 + 8 * u) for u in range(2 * UNROLL)]
                sums = [jnp.zeros((8, 128), f32)] * (2 * UNROLL)
                for k in range(edge_from, edge_to):
                    at, w = edge_pos[k, :, ls], edge_w[k, :, ls]
                    sums = [s + jnp.where(at == p, w, 0.0) for s, p in zip(sums, places)]
                dst[pl.ds(pl.multiple_of(r0, 16), tall), ls] = jnp.concatenate(sums, 0).astype(bf16)
                return carry

            return lax.fori_loop(0, count // tall, step, carry)

        lax.fori_loop(0, rows // 128, lanes, 0)

    def shared_table(dst, which, edge_from, edge_to):
        count = dst.shape[0] // 2
        table(dst, core * count, count, 0, edge_from, edge_to)
        mine = dst.at[pl.ds(pl.multiple_of(core * count, count), count)]
        put(mine, mine, tab_s.at[which], tab_r.at[which], (me, pair))

    def wait_table(dst, which):
        count = dst.shape[0] // 2
        got(dst.at[pl.ds(pl.multiple_of((1 - core) * count, count), count)], tab_r.at[which])

    def far_group(g):
        table(far, 0, gs, g * gs, first_far, first_far + far_edges)

    shared_table(near, 0, 0, first_far)
    if groups == 1:
        shared_table(far, 1, first_far, first_far + far_edges)
    wait_table(near, 0)
    for r in range(BLOCKS):
        rs = slice(r * rb, (r + 1) * rb)
        wide[rs, :] = tn(near[:, rs], feat[...])
    if groups == 1:
        wait_table(far, 1)

    def arrived(h):
        peers(lambda s: got(incg.at[h, s], in_r.at[h, s]))

    def send_merged(h, r):
        piece = merged.at[col, h, pl.ds(r * rb, rb)]
        put(piece, piece, mx_s.at[h, r], mx_r.at[h, r], (me, xcol))
        put(piece, piece, mc_s.at[h, r], mc_r.at[h, r], (me, pair))

    if groups == 1:
        for h in range(HALVES):
            hs = slice(h * half, (h + 1) * half)
            arrived(h)
            pooled = incg[h].reshape(gs, half)
            for r in range(BLOCKS):
                rs = slice(r * rb, (r + 1) * rb)
                merged[col, h, rs] = (wide[rs, hs] + tn(far[:, rs], pooled)).astype(bf16)
                send_merged(h, r)
    else:
        for h in range(HALVES):
            arrived(h)
        for g in range(groups):
            far_group(g)
            for h in range(HALVES):
                hs = slice(h * half, (h + 1) * half)
                pooled = incg[h, g * gd : (g + 1) * gd].reshape(gs, half)
                for r in range(BLOCKS):
                    rs = slice(r * rb, (r + 1) * rb)
                    wide[rs, hs] += tn(far[:, rs], pooled)
        for h in range(HALVES):
            hs = slice(h * half, (h + 1) * half)
            for r in range(BLOCKS):
                rs = slice(r * rb, (r + 1) * rb)
                merged[col, h, rs] = wide[rs, hs].astype(bf16)
                send_merged(h, r)

    load_w.wait()
    load_c.wait()

    def cross(h, r):
        piece = merged.at[xcol, h, pl.ds(r * rb, rb)]
        got(piece, mx_r.at[h, r])
        put(piece, piece, mf_s.at[h, r], mf_r.at[h, r], (me, pair))

    def whole_rows(h, r):
        got(merged.at[pair, h, pl.ds(r * rb, rb)], mc_r.at[h, r])
        got(merged.at[dcol, h, pl.ds(r * rb, rb)], mf_r.at[h, r])

    def products(h, r):
        total = None
        for q in range(ncol):
            k0 = q * part + h * half
            term = nn(merged[q, h, r * rb : (r + 1) * rb, :], w_v[k0 : k0 + half, :])
            total = term if total is None else total + term
        return total

    def first_half(r):
        whole_rows(0, r)
        wide[r * rb : (r + 1) * rb, :] = products(0, r) + bias[...]

    def second_half(r):
        whole_rows(1, r)
        wide[r * rb : (r + 1) * rb, :] += products(1, r)

    tall = 32

    def smooth(r, total):
        def step(b, total):
            rs = pl.ds(pl.multiple_of(r * rb + b * tall, tall), tall)
            v = wide[rs, :]
            cdf = 0.5 + 0.5 * lax.erf(v * (1.0 / math.sqrt(2.0)))
            act[col, rs, :] = (v * cdf).astype(bf16)
            density = jnp.exp(v * v * -0.5) * (1.0 / math.sqrt(2.0 * math.pi))
            low = (cot_v[rs, :].astype(f32) * (cdf + v * density)).astype(bf16)
            glow[rs, :] = low
            return total + jnp.sum(low.astype(f32).reshape(tall // 8, 8, part), axis=0)

        return lax.fori_loop(0, rb // tall, step, total)

    def grads(r):
        rs = slice(r * rb, (r + 1) * rb)
        low = glow[rs, :]

        def term(q):
            return nt(low, w_v[pl.ds(pl.multiple_of(q * part, part), part), :])

        csend[r, 0] = term(pair).astype(bf16)
        csend[r, 1] = term(dcol).astype(bf16)
        put(csend.at[r], crecv.at[r], rc_s.at[r], rc_r.at[r], (me, pair))
        keep_own[rs, :] = term(col)
        keep_far[rs, :] = term(xcol)

    def grads_over(r):
        rs = slice(r * rb, (r + 1) * rb)
        got(crecv.at[r], rc_r.at[r])
        xsend[r] = (keep_far[rs, :] + crecv[r, 1].astype(f32)).astype(bf16)
        put(xsend.at[r], xrecv.at[r], rx_s.at[r], rx_r.at[r], (me, xcol))
        keep_own[rs, :] += crecv[r, 0].astype(f32)

    def grads_in(r):
        rs = slice(r * rb, (r + 1) * rb)
        got(xrecv.at[r], rx_r.at[r])
        gm[rs, :] = (keep_own[rs, :] + xrecv[r].astype(f32)).astype(bf16)

    for r in range(BLOCKS):
        cross(0, r)
        if r:
            first_half(r - 1)
    total = jnp.zeros((8, part), f32)
    for r in range(BLOCKS):
        cross(1, r)
        if r == 0:
            first_half(BLOCKS - 1)
        else:
            grads_over(r - 1)
        second_half(r)
        total = smooth(r, total)
        grads(r)

    bsend[...] = total

    def weight_chunk(chunk):
        q, h = lax.div(chunk, HALVES), lax.rem(chunk, HALVES)
        return tn(merged[q, h], glow[...])

    fine = kb == half
    if not fine:
        for chunk in range(ncol * HALVES):
            wacc[chunk * half : (chunk + 1) * half, :] = tn(merged[chunk // HALVES, chunk % HALVES], glow[...])

    def block_rows(b):
        return pl.ds(pl.multiple_of(b * kb, kb), kb)

    def place(k):
        return lax.rem(zz + k, depth)

    def weight_out(k):
        z = place(k)
        theirs, mine = z * 2 + 1 - yy, z * 2 + yy
        if fine:
            ysend[z] = weight_chunk(theirs).astype(bf16)
        else:
            ysend[z] = wacc[block_rows(theirs), :].astype(bf16)
        put(ysend.at[z], yrecv.at[z], y_s.at[z], y_r.at[z], ypeer)
        if fine:
            wacc[block_rows(mine), :] = weight_chunk(mine)

    def weight_pass(k):
        z = place(k)
        got(yrecv.at[z], y_r.at[z])
        summed = wacc[block_rows(z * 2 + yy), :] + yrecv[z].astype(f32)
        if k:
            zsend[z] = summed.astype(bf16)
            put(zsend.at[z], zrecv.at[zz], z_s.at[z], z_r.at[zz], (z * 2 + yy, col))
        else:
            wacc[block_rows(me), :] = summed

    order = list(range(1, depth)) + [0]
    for at, k in enumerate(order):
        weight_out(k)
        if at == 0:
            grads_over(BLOCKS - 1)

    def bias_copy(t):
        pltpu.make_async_remote_copy(
            src_ref=bsend, dst_ref=brecv.at[me], send_sem=b_s.at[t], recv_sem=b_r.at[me],
            device_id=(t, col), device_id_type=MESH,
        ).start()

    peers(bias_copy)

    def act_over(r):
        piece = act.at[col, pl.ds(r * rb, rb)]
        put(piece, piece, ax_s.at[r], ax_r.at[r], (me, xcol))

    own_act = act.at[col]
    put(own_act, own_act, ac_s.at[0], ac_r.at[0], (me, pair))
    columns = lambda q: pl.ds(pl.multiple_of(q * part, part), part)
    saves = [pltpu.make_async_copy(own_act, act_out.at[:, columns(col)], out_s.at[0])]
    saves[0].start()

    for k in order[: depth - 3]:
        weight_pass(k)
    grads_in(0)
    grads_in(1)
    weight_pass(order[depth - 3])
    grads_in(2)
    act_over(0)
    weight_pass(order[depth - 2])
    grads_in(3)
    for r in range(1, BLOCKS):
        act_over(r)

    def sent_in(h):
        peers(lambda t: sent(outg.at[h, t], in_s.at[h, t]))

    for h in range(HALVES):
        sent_in(h)

    def back_copy(h, t):
        pltpu.make_async_remote_copy(
            src_ref=outg.at[h, t], dst_ref=ret.at[h, me], send_sem=ret_s.at[h, t], recv_sem=ret_r.at[h, me],
            device_id=(t, col), device_id_type=MESH,
        ).start()

    for g in range(groups):
        if groups > 1:
            far_group(g)
        pool_grad = nn(far[...], gm[...]).astype(bf16)
        for h in range(HALVES):
            outg[h, g * gd : (g + 1) * gd] = pool_grad[:, h * half : (h + 1) * half].reshape(gd, slots, half)
    for h in range(HALVES):
        peers(functools.partial(back_copy, h))
        ret[h, me] = jnp.zeros((slots, half), bf16)
    weight_pass(0)
    for r in range(BLOCKS):
        rs = slice(r * rb, (r + 1) * rb)
        wide[rs, :] = nn(near[rs, :], gm[...])

    mine = wacc[block_rows(me), :]
    for k in range(1, depth):
        z = place(k)
        got(zrecv.at[z], z_r.at[z])
        mine = mine + zrecv[z].astype(f32)
    wfin[me] = mine.astype(bf16)
    block = wfin.at[me]
    for k in range(1, depth):
        z = place(k)
        put(block, block, zg_s.at[z], zg_r.at[zz], (z * 2 + yy, col))
    put(block, block, yg_s.at[zz], yg_r.at[zz], ypeer)

    for h in range(HALVES):
        hs = slice(h * half, (h + 1) * half)
        peers(lambda s: got(ret.at[h, s], ret_r.at[h, s]))
        for g in range(groups):
            if groups > 1:
                put_selector(g)
            back = ret[h, g * gd : (g + 1) * gd].reshape(gs, half)
            for r in range(BLOCKS):
                rs = slice(r * rb, (r + 1) * rb)
                wide[rs, hs] += tn(sel[:, rs], back)
        ig_out[:, hs] = wide[:, hs].astype(bf16)

    for k in range(1, depth):
        z = place(k)
        block = wfin.at[z * 2 + yy]
        got(block, zg_r.at[z])
        put(block, block, yg_s.at[z], yg_r.at[z], ypeer)
    for r in range(BLOCKS):
        piece = act.at[xcol, pl.ds(r * rb, rb)]
        got(piece, ax_r.at[r])
        put(piece, piece, af_s.at[r], af_r.at[r], (me, pair))
    got(act.at[pair], ac_r.at[0])
    for at, q in enumerate((pair, xcol)):
        saves.append(pltpu.make_async_copy(act.at[q], act_out.at[:, columns(q)], out_s.at[1 + at]))
        saves[-1].start()
    peers(lambda s: got(brecv.at[s], b_r.at[s]))
    brecv[me] = bsend[...]
    bg_out[...] = jnp.sum(brecv[...].reshape(n * 8, part), axis=0, keepdims=True)
    for r in range(BLOCKS):
        got(act.at[dcol, pl.ds(r * rb, rb)], af_r.at[r])
    saves.append(pltpu.make_async_copy(act.at[dcol], act_out.at[:, columns(dcol)], out_s.at[3]))
    saves[-1].start()
    for k in range(depth):
        z = place(k)
        got(wfin.at[z * 2 + 1 - yy], yg_r.at[z])
    saves.append(pltpu.make_async_copy(wfin, wg_out, out_s.at[4]))
    saves[-1].start()

    peers(lambda t: sent(bsend, b_s.at[t]))
    for h in range(HALVES):
        peers(lambda t: sent(outg.at[h, t], ret_s.at[h, t]))
    for copy in pending:
        copy.wait_send()
    for save in saves:
        save.wait()


def local(
    features, weight, layer_bias, cotangent, self_weight, local_index, local_weight, send_index, remote_slot, remote_weight,
    *, n, ncol,
):
    rows, part = features.shape
    width = weight.shape[0]
    slots = send_index.shape[2]
    half, rb = part // HALVES, rows // BLOCKS
    gs = min(8, n) * slots
    depth, kb = n // 2, width // n
    edges = local_index.shape[1] + 1 + remote_slot.shape[1]
    vmem = pl.BlockSpec(memory_space=pltpu.VMEM)
    hbm = pl.BlockSpec(memory_space=pl.ANY)
    V = pltpu.VMEM
    S = lambda *shape: pltpu.SemaphoreType.DMA(shape)
    buffers = [
        V((width, part), bf16), V((rows, part), bf16), V((gs, rows), bf16), V((rows, rows), bf16), V((gs, rows), bf16),
        V((edges, 8, rows), i32), V((edges, 8, rows), f32),
        V((HALVES, n, slots, half), bf16), V((HALVES, n, slots, half), bf16), V((rows, part), f32),
        V((ncol, HALVES, rows, half), bf16), V((ncol, rows, part), bf16), V((rows, part), bf16),
        V((rows, part), f32), V((rows, part), f32),
        V((BLOCKS, 2, rb, part), bf16), V((BLOCKS, 2, rb, part), bf16), V((BLOCKS, rb, part), bf16), V((BLOCKS, rb, part), bf16),
        V((rows, part), bf16), V((width, part), f32),
        V((depth, kb, part), bf16), V((depth, kb, part), bf16), V((depth, kb, part), bf16), V((depth, kb, part), bf16),
        V((n, kb, part), bf16), V((8, part), f32), V((n, 8, part), f32), V((HALVES, n, slots, half), bf16),
    ]
    semaphores = [
        S(2), S(HALVES, n), S(HALVES, n), S(2), S(2),
        S(HALVES, BLOCKS), S(HALVES, BLOCKS), S(HALVES, BLOCKS), S(HALVES, BLOCKS), S(HALVES, BLOCKS), S(HALVES, BLOCKS),
        S(BLOCKS), S(BLOCKS), S(BLOCKS), S(BLOCKS),
        S(depth), S(depth), S(depth), S(depth), S(depth), S(depth), S(depth), S(depth),
        S(n), S(n), S(HALVES, n), S(HALVES, n),
        S(BLOCKS), S(BLOCKS), S(1), S(1), S(BLOCKS), S(BLOCKS), S(5),
    ]
    act, ig, wg, bg = pl.pallas_call(
        functools.partial(layer, n=n, ncol=ncol),
        out_shape=(
            jax.ShapeDtypeStruct((rows, ncol * part), bf16),
            jax.ShapeDtypeStruct((rows, part), bf16),
            jax.ShapeDtypeStruct((n, kb, part), bf16),
            jax.ShapeDtypeStruct((1, part), f32),
        ),
        in_specs=[vmem, hbm, vmem, hbm, vmem, vmem, vmem, vmem, vmem, vmem],
        out_specs=(hbm, vmem, hbm, vmem),
        scratch_shapes=buffers + semaphores,
        compiler_params=pltpu.CompilerParams(
            collective_id=0, has_side_effects=True, vmem_limit_bytes=62 << 20
        ),
        cost_estimate=pl.CostEstimate(flops=11 << 30, bytes_accessed=16 << 20, transcendentals=1 << 20),
    )(
        features, weight, layer_bias.astype(f32)[None, :], cotangent, self_weight[None, :], local_index, local_weight,
        send_index[0], remote_slot, remote_weight,
    )
    return act, ig, wg.reshape(width, part).astype(f32), bg[0]


def solution(mesh):
    placed = (
        P("clu", "col"),
        P(None, "col"),
        P("col"),
        P("clu", "col"),
        P("clu"),
        P("clu", None),
        P("clu", None),
        P("clu", None, None),
        P("clu", None),
        P("clu", None),
    )
    return jax.shard_map(
        functools.partial(local, n=mesh.shape["clu"], ncol=mesh.shape["col"]),
        mesh=mesh,
        in_specs=placed,
        out_specs=(P("clu", None), P("clu", "col"), P(None, "col"), P("col")),
        check_vma=False,
    )
```

```python
import functools
import math

import jax
import jax.numpy as jnp
from jax import lax
from jax.experimental import pallas as pl
from jax.experimental.pallas import tpu as pltpu
from jax.sharding import PartitionSpec as P

enhance = 1.0
f32, bf16, i32 = jnp.float32, jnp.bfloat16, jnp.int32
MESH = pl.DeviceIdType.MESH
BLOCKS = 4
HALVES = 2
UNROLL = 8


def tn(a, b):
    return lax.dot_general(a, b, (((0,), (0,)), ((), ())), preferred_element_type=f32)


def nt(a, b):
    return lax.dot_general(a, b, (((1,), (1,)), ((), ())), preferred_element_type=f32)


def nn(a, b):
    return jnp.dot(a, b, preferred_element_type=f32)


def layer(
    feat, weight_in, bias, cot_in, selfw, lidx, lwgt, send, ridx, rwgt,
    act, ig_out, wfin, bg_out,
    w_v, cot_v, sel, near, far, edge_pos, edge_w, outg, incg, wide, merged, glow, keep_own, keep_far,
    csend, crecv, xsend, xrecv, gm, wacc, ysend, yrecv, zsend, zrecv, bsend, brecv, ret,
    load_s, in_s, in_r, tab_s, tab_r, mx_s, mx_r, mc_s, mc_r, mf_s, mf_r, rc_s, rc_r, rx_s, rx_r,
    y_s, y_r, z_s, z_r, zg_s, zg_r, yg_s, yg_r, b_s, b_r, ret_s, ret_r, ax_s, ax_r, ac_s, ac_r, af_s, af_r,
    *, n, ncol,
):
    rows, part = feat.shape
    half = part // HALVES
    rb = rows // BLOCKS
    slots = send.shape[1]
    gd = min(8, n)
    groups = n // gd
    gs = gd * slots
    depth = n // 2
    kb = wacc.shape[0] // n

    me = lax.axis_index("clu")
    col = lax.axis_index("col")
    zz, yy = lax.div(me, 2), lax.rem(me, 2)
    core = lax.rem(col, 2)
    pair = col + 1 - 2 * core
    xcol = lax.rem(col + ncol // 2, ncol)
    dcol = lax.rem(pair + ncol // 2, ncol)
    ypeer = (me + 1 - 2 * yy, col)
    pending = []

    def put(src, dst, ss, rs, dev):
        copy = pltpu.make_async_remote_copy(
            src_ref=src, dst_ref=dst, send_sem=ss, recv_sem=rs, device_id=dev, device_id_type=MESH
        )
        copy.start()
        pending.append(copy)

    def got(dst, rs):
        pltpu.make_async_remote_copy(
            src_ref=dst, dst_ref=dst, send_sem=rs, recv_sem=rs, device_id=(me, pair), device_id_type=MESH
        ).wait_recv()

    def sent(src, ss):
        pltpu.make_async_remote_copy(
            src_ref=src, dst_ref=src, send_sem=ss, recv_sem=ss, device_id=(me, pair), device_id_type=MESH
        ).wait_send()

    def peers(step):
        def body(k, carry):
            step(lax.rem(me + k, n))
            return carry

        lax.fori_loop(1, n, body, 0)

    load_w = pltpu.make_async_copy(weight_in, w_v, load_s.at[0])
    load_c = pltpu.make_async_copy(cot_in, cot_v, load_s.at[1])
    load_w.start()
    load_c.start()
    barrier = pltpu.get_barrier_semaphore()
    peers(lambda t: pl.semaphore_signal(barrier, inc=1, device_id=(t, col), device_id_type=MESH))
    for other in (pair, xcol):
        pl.semaphore_signal(barrier, inc=1, device_id=(me, other), device_id_type=MESH)

    lane = lax.broadcasted_iota(i32, (slots, rows), 1)

    def put_selector(g):
        ids = send[g * gd : (g + 1) * gd, :].T
        for d in range(gd):
            sel[d * slots : (d + 1) * slots, :] = jnp.where(ids[:, d : d + 1] == lane, 1.0, 0.0).astype(bf16)

    def in_copy(h, t):
        pltpu.make_async_remote_copy(
            src_ref=outg.at[h, t], dst_ref=incg.at[h, me], send_sem=in_s.at[h, t], recv_sem=in_r.at[h, me],
            device_id=(t, col), device_id_type=MESH,
        ).start()

    for h in range(HALVES):
        for g in range(groups):
            if groups > 1 or h == 0:
                put_selector(g)
            rows_out = nn(sel[...], feat[:, h * half : (h + 1) * half]).astype(bf16)
            outg[h, g * gd : (g + 1) * gd] = rows_out.reshape(gd, slots, half)
        if h == 0:
            pl.semaphore_wait(barrier, n + 1)
        peers(functools.partial(in_copy, h))
        incg[h, me] = jnp.zeros((slots, half), bf16)

    local_edges, far_edges = lidx.shape[0], ridx.shape[0]
    first_far = local_edges + 1

    def put_edges(at, idx, w):
        for k in range(idx.shape[0]):
            edge_pos[at + k] = jnp.broadcast_to(idx[k : k + 1, :], (8, rows))
            edge_w[at + k] = jnp.broadcast_to(w[k : k + 1, :], (8, rows))

    put_edges(0, lidx[...], lwgt[...])
    put_edges(local_edges, lax.broadcasted_iota(i32, (1, rows), 1), (1.0 + enhance) * selfw[...])
    put_edges(first_far, ridx[...], rwgt[...])
    sub = lax.broadcasted_iota(i32, (8, 128), 0)

    def table(dst, first, count, base, edge_from, edge_to):
        tall = 16 * UNROLL

        def lanes(l, carry):
            ls = pl.ds(pl.multiple_of(l * 128, 128), 128)

            def step(b, carry):
                r0 = first + b * tall
                places = [sub + (base + r0 + 8 * u) for u in range(2 * UNROLL)]
                sums = [jnp.zeros((8, 128), f32)] * (2 * UNROLL)
                for k in range(edge_from, edge_to):
                    at, w = edge_pos[k, :, ls], edge_w[k, :, ls]
                    sums = [s + jnp.where(at == p, w, 0.0) for s, p in zip(sums, places)]
                dst[pl.ds(pl.multiple_of(r0, 16), tall), ls] = jnp.concatenate(sums, 0).astype(bf16)
                return carry

            return lax.fori_loop(0, count // tall, step, carry)

        lax.fori_loop(0, rows // 128, lanes, 0)

    def shared_table(dst, which, edge_from, edge_to):
        count = dst.shape[0] // 2
        table(dst, core * count, count, 0, edge_from, edge_to)
        mine = dst.at[pl.ds(pl.multiple_of(core * count, count), count)]
        put(mine, mine, tab_s.at[which], tab_r.at[which], (me, pair))

    def wait_table(dst, which):
        count = dst.shape[0] // 2
        got(dst.at[pl.ds(pl.multiple_of((1 - core) * count, count), count)], tab_r.at[which])

    def far_group(g):
        table(far, 0, gs, g * gs, first_far, first_far + far_edges)

    shared_table(near, 0, 0, first_far)
    if groups == 1:
        shared_table(far, 1, first_far, first_far + far_edges)
    wait_table(near, 0)
    for r in range(BLOCKS):
        rs = slice(r * rb, (r + 1) * rb)
        wide[rs, :] = tn(near[:, rs], feat[...])
    if groups == 1:
        wait_table(far, 1)

    def arrived(h):
        peers(lambda s: got(incg.at[h, s], in_r.at[h, s]))

    def send_merged(h, r):
        piece = merged.at[col, h, pl.ds(r * rb, rb)]
        put(piece, piece, mx_s.at[h, r], mx_r.at[h, r], (me, xcol))
        put(piece, piece, mc_s.at[h, r], mc_r.at[h, r], (me, pair))

    if groups == 1:
        for h in range(HALVES):
            hs = slice(h * half, (h + 1) * half)
            arrived(h)
            pooled = incg[h].reshape(gs, half)
            for r in range(BLOCKS):
                rs = slice(r * rb, (r + 1) * rb)
                merged[col, h, rs] = (wide[rs, hs] + tn(far[:, rs], pooled)).astype(bf16)
                send_merged(h, r)
    else:
        for h in range(HALVES):
            arrived(h)
        for g in range(groups):
            far_group(g)
            for h in range(HALVES):
                hs = slice(h * half, (h + 1) * half)
                pooled = incg[h, g * gd : (g + 1) * gd].reshape(gs, half)
                for r in range(BLOCKS):
                    rs = slice(r * rb, (r + 1) * rb)
                    wide[rs, hs] += tn(far[:, rs], pooled)
        for h in range(HALVES):
            hs = slice(h * half, (h + 1) * half)
            for r in range(BLOCKS):
                rs = slice(r * rb, (r + 1) * rb)
                merged[col, h, rs] = wide[rs, hs].astype(bf16)
                send_merged(h, r)

    load_w.wait()
    load_c.wait()

    def cross(h, r):
        piece = merged.at[xcol, h, pl.ds(r * rb, rb)]
        got(piece, mx_r.at[h, r])
        put(piece, piece, mf_s.at[h, r], mf_r.at[h, r], (me, pair))

    def whole_rows(h, r):
        got(merged.at[pair, h, pl.ds(r * rb, rb)], mc_r.at[h, r])
        got(merged.at[dcol, h, pl.ds(r * rb, rb)], mf_r.at[h, r])

    def products(h, r):
        total = None
        for q in range(ncol):
            k0 = q * part + h * half
            term = nn(merged[q, h, r * rb : (r + 1) * rb, :], w_v[k0 : k0 + half, :])
            total = term if total is None else total + term
        return total

    def first_half(r):
        whole_rows(0, r)
        wide[r * rb : (r + 1) * rb, :] = products(0, r) + bias[...].astype(f32)

    def second_half(r):
        whole_rows(1, r)
        wide[r * rb : (r + 1) * rb, :] += products(1, r)

    tall = 32

    def smooth(r, total):
        def step(b, total):
            rs = pl.ds(pl.multiple_of(r * rb + b * tall, tall), tall)
            v = wide[rs, :]
            cdf = 0.5 + 0.5 * lax.erf(v * (1.0 / math.sqrt(2.0)))
            act[col, rs, :] = (v * cdf).astype(bf16)
            density = jnp.exp(v * v * -0.5) * (1.0 / math.sqrt(2.0 * math.pi))
            low = (cot_v[rs, :].astype(f32) * (cdf + v * density)).astype(bf16)
            glow[rs, :] = low
            return total + jnp.sum(low.astype(f32).reshape(tall // 8, 8, part), axis=0)

        return lax.fori_loop(0, rb // tall, step, total)

    def grads(r):
        rs = slice(r * rb, (r + 1) * rb)
        low = glow[rs, :]

        def term(q):
            return nt(low, w_v[pl.ds(pl.multiple_of(q * part, part), part), :])

        csend[r, 0] = term(pair).astype(bf16)
        csend[r, 1] = term(dcol).astype(bf16)
        put(csend.at[r], crecv.at[r], rc_s.at[r], rc_r.at[r], (me, pair))
        keep_own[rs, :] = term(col)
        keep_far[rs, :] = term(xcol)

    def grads_over(r):
        rs = slice(r * rb, (r + 1) * rb)
        got(crecv.at[r], rc_r.at[r])
        xsend[r] = (keep_far[rs, :] + crecv[r, 1].astype(f32)).astype(bf16)
        put(xsend.at[r], xrecv.at[r], rx_s.at[r], rx_r.at[r], (me, xcol))
        keep_own[rs, :] += crecv[r, 0].astype(f32)

    def grads_in(r):
        rs = slice(r * rb, (r + 1) * rb)
        got(xrecv.at[r], rx_r.at[r])
        gm[rs, :] = (keep_own[rs, :] + xrecv[r].astype(f32)).astype(bf16)

    for r in range(BLOCKS):
        cross(0, r)
        if r:
            first_half(r - 1)
    total = jnp.zeros((8, part), f32)
    for r in range(BLOCKS):
        cross(1, r)
        if r == 0:
            first_half(BLOCKS - 1)
        else:
            grads_over(r - 1)
        second_half(r)
        total = smooth(r, total)
        grads(r)

    bsend[...] = total

    def weight_chunk(chunk):
        q, h = lax.div(chunk, HALVES), lax.rem(chunk, HALVES)
        return tn(merged[q, h], glow[...])

    fine = kb == half
    if not fine:
        for chunk in range(ncol * HALVES):
            wacc[chunk * half : (chunk + 1) * half, :] = tn(merged[chunk // HALVES, chunk % HALVES], glow[...])

    def block_rows(b):
        return pl.ds(pl.multiple_of(b * kb, kb), kb)

    def place(k):
        return lax.rem(zz + k, depth)

    def weight_out(k):
        z = place(k)
        theirs, mine = z * 2 + 1 - yy, z * 2 + yy
        if fine:
            ysend[z] = weight_chunk(theirs).astype(bf16)
        else:
            ysend[z] = wacc[block_rows(theirs), :].astype(bf16)
        put(ysend.at[z], yrecv.at[z], y_s.at[z], y_r.at[z], ypeer)
        if fine:
            wacc[block_rows(mine), :] = weight_chunk(mine)

    def weight_pass(k):
        z = place(k)
        got(yrecv.at[z], y_r.at[z])
        summed = wacc[block_rows(z * 2 + yy), :] + yrecv[z].astype(f32)
        if k:
            zsend[z] = summed.astype(bf16)
            put(zsend.at[z], zrecv.at[zz], z_s.at[z], z_r.at[zz], (z * 2 + yy, col))
        else:
            wacc[block_rows(me), :] = summed

    order = list(range(1, depth)) + [0]
    for at, k in enumerate(order):
        weight_out(k)
        if at == 0:
            grads_over(BLOCKS - 1)

    def bias_copy(t):
        pltpu.make_async_remote_copy(
            src_ref=bsend, dst_ref=brecv.at[me], send_sem=b_s.at[t], recv_sem=b_r.at[me],
            device_id=(t, col), device_id_type=MESH,
        ).start()

    peers(bias_copy)

    def act_over(r):
        piece = act.at[col, pl.ds(r * rb, rb)]
        put(piece, piece, ax_s.at[r], ax_r.at[r], (me, xcol))

    own_act = act.at[col]
    put(own_act, own_act, ac_s.at[0], ac_r.at[0], (me, pair))

    for k in order[: depth - 3]:
        weight_pass(k)
    grads_in(0)
    grads_in(1)
    weight_pass(order[depth - 3])
    grads_in(2)
    act_over(0)
    weight_pass(order[depth - 2])
    grads_in(3)
    for r in range(1, BLOCKS):
        act_over(r)

    def sent_in(h):
        peers(lambda t: sent(outg.at[h, t], in_s.at[h, t]))

    for h in range(HALVES):
        sent_in(h)

    def back_copy(h, t):
        pltpu.make_async_remote_copy(
            src_ref=outg.at[h, t], dst_ref=ret.at[h, me], send_sem=ret_s.at[h, t], recv_sem=ret_r.at[h, me],
            device_id=(t, col), device_id_type=MESH,
        ).start()

    for g in range(groups):
        if groups > 1:
            far_group(g)
        pool_grad = nn(far[...], gm[...]).astype(bf16)
        for h in range(HALVES):
            outg[h, g * gd : (g + 1) * gd] = pool_grad[:, h * half : (h + 1) * half].reshape(gd, slots, half)
    for h in range(HALVES):
        peers(functools.partial(back_copy, h))
        ret[h, me] = jnp.zeros((slots, half), bf16)
    weight_pass(0)
    for r in range(BLOCKS):
        rs = slice(r * rb, (r + 1) * rb)
        wide[rs, :] = nn(near[rs, :], gm[...])

    mine = wacc[block_rows(me), :]
    for k in range(1, depth):
        z = place(k)
        got(zrecv.at[z], z_r.at[z])
        mine = mine + zrecv[z].astype(f32)
    wfin[me] = mine.astype(bf16)
    block = wfin.at[me]
    for k in range(1, depth):
        z = place(k)
        put(block, block, zg_s.at[z], zg_r.at[zz], (z * 2 + yy, col))
    put(block, block, yg_s.at[zz], yg_r.at[zz], ypeer)

    for h in range(HALVES):
        hs = slice(h * half, (h + 1) * half)
        peers(lambda s: got(ret.at[h, s], ret_r.at[h, s]))
        for g in range(groups):
            if groups > 1:
                put_selector(g)
            back = ret[h, g * gd : (g + 1) * gd].reshape(gs, half)
            for r in range(BLOCKS):
                rs = slice(r * rb, (r + 1) * rb)
                wide[rs, hs] += tn(sel[:, rs], back)
        ig_out[:, hs] = wide[:, hs].astype(bf16)

    for k in range(1, depth):
        z = place(k)
        block = wfin.at[z * 2 + yy]
        got(block, zg_r.at[z])
        put(block, block, yg_s.at[z], yg_r.at[z], ypeer)
    for r in range(BLOCKS):
        piece = act.at[xcol, pl.ds(r * rb, rb)]
        got(piece, ax_r.at[r])
        put(piece, piece, af_s.at[r], af_r.at[r], (me, pair))
    got(act.at[pair], ac_r.at[0])
    peers(lambda s: got(brecv.at[s], b_r.at[s]))
    brecv[me] = bsend[...]
    bg_out[...] = jnp.sum(brecv[...].reshape(n * 8, part), axis=0, keepdims=True)
    for r in range(BLOCKS):
        got(act.at[dcol, pl.ds(r * rb, rb)], af_r.at[r])
    for k in range(depth):
        z = place(k)
        got(wfin.at[z * 2 + 1 - yy], yg_r.at[z])

    peers(lambda t: sent(bsend, b_s.at[t]))
    for h in range(HALVES):
        peers(lambda t: sent(outg.at[h, t], ret_s.at[h, t]))
    for copy in pending:
        copy.wait_send()


WRITES = 8


def store(act, ig, wg, bg, act_out, ig_out, wg_out, bg_out, wide, some_s, wg_s):
    ncol, part = act.shape[0], act.shape[2]
    copies = []
    for q in range(ncol):
        copies.append(pltpu.make_async_copy(act.at[q], act_out.at[:, q * part : (q + 1) * part], some_s.at[q]))
        copies[-1].start()
    copies.append(pltpu.make_async_copy(ig, ig_out, some_s.at[ncol]))
    copies[-1].start()
    tall = wide.shape[0] // WRITES
    group = wg.shape[0] // WRITES
    for p in range(WRITES):
        rs = slice(p * tall, (p + 1) * tall)
        wide[rs, :] = wg[p * group : (p + 1) * group].reshape(tall, part).astype(f32)
        copies.append(pltpu.make_async_copy(wide.at[rs], wg_out.at[rs], wg_s.at[p]))
        copies[-1].start()
    bg_out[...] = bg[...]
    for copy in copies:
        copy.wait()


def local(
    features, weight, layer_bias, cotangent, self_weight, local_index, local_weight, send_index, remote_slot, remote_weight,
    *, n, ncol,
):
    rows, part = features.shape
    width = weight.shape[0]
    slots = send_index.shape[2]
    half, rb = part // HALVES, rows // BLOCKS
    gs = min(8, n) * slots
    depth, kb = n // 2, width // n
    edges = local_index.shape[1] + 1 + remote_slot.shape[1]
    vmem = pl.BlockSpec(memory_space=pltpu.VMEM)
    hbm = pl.BlockSpec(memory_space=pl.ANY)
    V = pltpu.VMEM
    S = lambda *shape: pltpu.SemaphoreType.DMA(shape)
    buffers = [
        V((width, part), bf16), V((rows, part), bf16), V((gs, rows), bf16), V((rows, rows), bf16), V((gs, rows), bf16),
        V((edges, 8, rows), i32), V((edges, 8, rows), f32),
        V((HALVES, n, slots, half), bf16), V((HALVES, n, slots, half), bf16), V((rows, part), f32),
        V((ncol, HALVES, rows, half), bf16), V((rows, part), bf16),
        V((rows, part), f32), V((rows, part), f32),
        V((BLOCKS, 2, rb, part), bf16), V((BLOCKS, 2, rb, part), bf16), V((BLOCKS, rb, part), bf16), V((BLOCKS, rb, part), bf16),
        V((rows, part), bf16), V((width, part), f32),
        V((depth, kb, part), bf16), V((depth, kb, part), bf16), V((depth, kb, part), bf16), V((depth, kb, part), bf16),
        V((8, part), f32), V((n, 8, part), f32), V((HALVES, n, slots, half), bf16),
    ]
    semaphores = [
        S(2), S(HALVES, n), S(HALVES, n), S(2), S(2),
        S(HALVES, BLOCKS), S(HALVES, BLOCKS), S(HALVES, BLOCKS), S(HALVES, BLOCKS), S(HALVES, BLOCKS), S(HALVES, BLOCKS),
        S(BLOCKS), S(BLOCKS), S(BLOCKS), S(BLOCKS),
        S(depth), S(depth), S(depth), S(depth), S(depth), S(depth), S(depth), S(depth),
        S(n), S(n), S(HALVES, n), S(HALVES, n),
        S(BLOCKS), S(BLOCKS), S(1), S(1), S(BLOCKS), S(BLOCKS),
    ]
    results = pl.pallas_call(
        functools.partial(layer, n=n, ncol=ncol),
        out_shape=(
            V((ncol, rows, part), bf16),
            V((rows, part), bf16),
            V((n, kb, part), bf16),
            V((1, part), f32),
        ),
        in_specs=[vmem, hbm, vmem, hbm, vmem, vmem, vmem, vmem, vmem, vmem],
        out_specs=(vmem,) * 4,
        scratch_shapes=buffers + semaphores,
        compiler_params=pltpu.CompilerParams(
            collective_id=0, has_side_effects=True, vmem_limit_bytes=50 << 20
        ),
        cost_estimate=pl.CostEstimate(flops=11 << 30, bytes_accessed=16 << 20, transcendentals=1 << 20),
    )(
        features, weight, layer_bias[None, :], cotangent, self_weight[None, :], local_index.T, local_weight.T,
        send_index[0], remote_slot.T, remote_weight.T,
    )
    output, input_grad, weight_grad, bias_grad = pl.pallas_call(
        store,
        out_shape=(
            jax.ShapeDtypeStruct((rows, ncol * part), bf16),
            jax.ShapeDtypeStruct((rows, part), bf16),
            jax.ShapeDtypeStruct((width, part), f32),
            jax.ShapeDtypeStruct((1, part), f32),
        ),
        in_specs=[vmem] * 4,
        out_specs=(hbm, hbm, hbm, vmem),
        scratch_shapes=[V((width, part), f32), S(ncol + 1), S(WRITES)],
        compiler_params=pltpu.CompilerParams(vmem_limit_bytes=6 << 20),
        cost_estimate=pl.CostEstimate(flops=0, bytes_accessed=10 << 20, transcendentals=0),
    )(*results)
    return output, input_grad, weight_grad, bias_grad[0]


def solution(mesh):
    placed = (
        P("clu", "col"),
        P(None, "col"),
        P("col"),
        P("clu", "col"),
        P("clu"),
        P("clu", None),
        P("clu", None),
        P("clu", None, None),
        P("clu", None),
        P("clu", None),
    )
    return jax.shard_map(
        functools.partial(local, n=mesh.shape["clu"], ncol=mesh.shape["col"]),
        mesh=mesh,
        in_specs=placed,
        out_specs=(P("clu", None), P("clu", "col"), P(None, "col"), P("col")),
        check_vma=False,
    )
```

```python
import functools
import math

import jax
import jax.numpy as jnp
from jax import lax
from jax.experimental import pallas as pl
from jax.experimental.pallas import tpu as pltpu
from jax.sharding import PartitionSpec as P

enhance = 1.0
f32, bf16, i32 = jnp.float32, jnp.bfloat16, jnp.int32
MESH = pl.DeviceIdType.MESH
BLOCKS = 4
HALVES = 2
UNROLL = 8


def tn(a, b):
    return lax.dot_general(a, b, (((0,), (0,)), ((), ())), preferred_element_type=f32)


def nt(a, b):
    return lax.dot_general(a, b, (((1,), (1,)), ((), ())), preferred_element_type=f32)


def nn(a, b):
    return jnp.dot(a, b, preferred_element_type=f32)


def layer(
    feat, weight_in, bias, cot_in, selfw, lidx, lwgt, send, ridx, rwgt,
    act, ig_out, wfin, bg_out,
    w_v, cot_v, sel, near, far, edge_pos, edge_w, outg, incg, wide, merged, glow, keep_own, keep_far,
    csend, crecv, xsend, xrecv, gm, wacc, ysend, yrecv, zsend, from_before, from_after, bsend, brecv, ret,
    load_s, in_s, in_r, tab_s, tab_r, mx_s, mx_r, mc_s, mc_r, mf_s, mf_r, rc_s, rc_r, rx_s, rx_r,
    y_s, y_r, z_s, fb_r, fa_r, zu_s, zd_s, zg_r, yg_s, yg_r, b_s, b_r, ret_s, ret_r, ax_s, ax_r, ac_s, ac_r, af_s, af_r,
    *, n, ncol,
):
    rows, part = feat.shape
    half = part // HALVES
    rb = rows // BLOCKS
    slots = send.shape[1]
    gd = min(8, n)
    groups = n // gd
    gs = gd * slots
    depth = n // 2
    kb = wacc.shape[0] // n

    me = lax.axis_index("clu")
    col = lax.axis_index("col")
    zz, yy = lax.div(me, 2), lax.rem(me, 2)
    core = lax.rem(col, 2)
    pair = col + 1 - 2 * core
    xcol = lax.rem(col + ncol // 2, ncol)
    dcol = lax.rem(pair + ncol // 2, ncol)
    ypeer = (me + 1 - 2 * yy, col)
    pending = []

    def start(src, dst, ss, rs, dev):
        copy = pltpu.make_async_remote_copy(
            src_ref=src, dst_ref=dst, send_sem=ss, recv_sem=rs, device_id=dev, device_id_type=MESH
        )
        copy.start()
        return copy

    def put(*args):
        pending.append(start(*args))

    def got(dst, rs):
        pltpu.make_async_remote_copy(
            src_ref=dst, dst_ref=dst, send_sem=rs, recv_sem=rs, device_id=(me, pair), device_id_type=MESH
        ).wait_recv()

    def sent(src, ss):
        pltpu.make_async_remote_copy(
            src_ref=src, dst_ref=src, send_sem=ss, recv_sem=ss, device_id=(me, pair), device_id_type=MESH
        ).wait_send()

    def peers(step):
        def body(k, carry):
            step(lax.rem(me + k, n))
            return carry

        lax.fori_loop(1, n, body, 0)

    load_w = pltpu.make_async_copy(weight_in, w_v, load_s.at[0])
    load_c = pltpu.make_async_copy(cot_in, cot_v, load_s.at[1])
    load_w.start()
    load_c.start()
    barrier = pltpu.get_barrier_semaphore()
    peers(lambda t: pl.semaphore_signal(barrier, inc=1, device_id=(t, col), device_id_type=MESH))
    for other in (pair, xcol):
        pl.semaphore_signal(barrier, inc=1, device_id=(me, other), device_id_type=MESH)

    lane = lax.broadcasted_iota(i32, (slots, rows), 1)

    def put_selector(g):
        ids = send[g * gd : (g + 1) * gd, :].T
        for d in range(gd):
            sel[d * slots : (d + 1) * slots, :] = jnp.where(ids[:, d : d + 1] == lane, 1.0, 0.0).astype(bf16)

    def in_copy(h, t):
        pltpu.make_async_remote_copy(
            src_ref=outg.at[h, t], dst_ref=incg.at[h, me], send_sem=in_s.at[h, t], recv_sem=in_r.at[h, me],
            device_id=(t, col), device_id_type=MESH,
        ).start()

    for h in range(HALVES):
        for g in range(groups):
            if groups > 1 or h == 0:
                put_selector(g)
            rows_out = nn(sel[...], feat[:, h * half : (h + 1) * half]).astype(bf16)
            outg[h, g * gd : (g + 1) * gd] = rows_out.reshape(gd, slots, half)
        if h == 0:
            pl.semaphore_wait(barrier, n + 1)
        peers(functools.partial(in_copy, h))
        incg[h, me] = jnp.zeros((slots, half), bf16)

    local_edges, far_edges = lidx.shape[0], ridx.shape[0]
    first_far = local_edges + 1

    def put_edges(at, idx, w):
        for k in range(idx.shape[0]):
            edge_pos[at + k] = jnp.broadcast_to(idx[k : k + 1, :], (8, rows))
            edge_w[at + k] = jnp.broadcast_to(w[k : k + 1, :], (8, rows))

    put_edges(0, lidx[...], lwgt[...])
    put_edges(local_edges, lax.broadcasted_iota(i32, (1, rows), 1), (1.0 + enhance) * selfw[...])
    put_edges(first_far, ridx[...], rwgt[...])
    sub = lax.broadcasted_iota(i32, (8, 128), 0)

    def table(dst, first, count, base, edge_from, edge_to):
        tall = 16 * UNROLL

        def lanes(l, carry):
            ls = pl.ds(pl.multiple_of(l * 128, 128), 128)

            def step(b, carry):
                r0 = first + b * tall
                places = [sub + (base + r0 + 8 * u) for u in range(2 * UNROLL)]
                sums = [jnp.zeros((8, 128), f32)] * (2 * UNROLL)
                for k in range(edge_from, edge_to):
                    at, w = edge_pos[k, :, ls], edge_w[k, :, ls]
                    sums = [s + jnp.where(at == p, w, 0.0) for s, p in zip(sums, places)]
                dst[pl.ds(pl.multiple_of(r0, 16), tall), ls] = jnp.concatenate(sums, 0).astype(bf16)
                return carry

            return lax.fori_loop(0, count // tall, step, carry)

        lax.fori_loop(0, rows // 128, lanes, 0)

    def shared_table(dst, which, edge_from, edge_to):
        count = dst.shape[0] // 2
        table(dst, core * count, count, 0, edge_from, edge_to)
        mine = dst.at[pl.ds(pl.multiple_of(core * count, count), count)]
        put(mine, mine, tab_s.at[which], tab_r.at[which], (me, pair))

    def wait_table(dst, which):
        count = dst.shape[0] // 2
        got(dst.at[pl.ds(pl.multiple_of((1 - core) * count, count), count)], tab_r.at[which])

    def far_group(g):
        table(far, 0, gs, g * gs, first_far, first_far + far_edges)

    shared_table(near, 0, 0, first_far)
    if groups == 1:
        shared_table(far, 1, first_far, first_far + far_edges)
    wait_table(near, 0)
    for r in range(BLOCKS):
        rs = slice(r * rb, (r + 1) * rb)
        wide[rs, :] = tn(near[:, rs], feat[...])
    if groups == 1:
        wait_table(far, 1)

    def arrived(h):
        peers(lambda s: got(incg.at[h, s], in_r.at[h, s]))

    def send_merged(h, r):
        piece = merged.at[col, h, pl.ds(r * rb, rb)]
        put(piece, piece, mx_s.at[h, r], mx_r.at[h, r], (me, xcol))
        put(piece, piece, mc_s.at[h, r], mc_r.at[h, r], (me, pair))

    if groups == 1:
        for h in range(HALVES):
            hs = slice(h * half, (h + 1) * half)
            arrived(h)
            pooled = incg[h].reshape(gs, half)
            for r in range(BLOCKS):
                rs = slice(r * rb, (r + 1) * rb)
                merged[col, h, rs] = (wide[rs, hs] + tn(far[:, rs], pooled)).astype(bf16)
                send_merged(h, r)
    else:
        for h in range(HALVES):
            arrived(h)
        for g in range(groups):
            far_group(g)
            for h in range(HALVES):
                hs = slice(h * half, (h + 1) * half)
                pooled = incg[h, g * gd : (g + 1) * gd].reshape(gs, half)
                for r in range(BLOCKS):
                    rs = slice(r * rb, (r + 1) * rb)
                    wide[rs, hs] += tn(far[:, rs], pooled)
        for h in range(HALVES):
            hs = slice(h * half, (h + 1) * half)
            for r in range(BLOCKS):
                rs = slice(r * rb, (r + 1) * rb)
                merged[col, h, rs] = wide[rs, hs].astype(bf16)
                send_merged(h, r)

    load_w.wait()
    load_c.wait()

    def cross(h, r):
        piece = merged.at[xcol, h, pl.ds(r * rb, rb)]
        got(piece, mx_r.at[h, r])
        put(piece, piece, mf_s.at[h, r], mf_r.at[h, r], (me, pair))

    def whole_rows(h, r):
        got(merged.at[pair, h, pl.ds(r * rb, rb)], mc_r.at[h, r])
        got(merged.at[dcol, h, pl.ds(r * rb, rb)], mf_r.at[h, r])

    def products(h, r):
        total = None
        for q in range(ncol):
            k0 = q * part + h * half
            term = nn(merged[q, h, r * rb : (r + 1) * rb, :], w_v[k0 : k0 + half, :])
            total = term if total is None else total + term
        return total

    def first_half(r):
        whole_rows(0, r)
        wide[r * rb : (r + 1) * rb, :] = products(0, r) + bias[...].astype(f32)

    def second_half(r):
        whole_rows(1, r)
        wide[r * rb : (r + 1) * rb, :] += products(1, r)

    tall = 32

    def smooth(r, total):
        def step(b, total):
            rs = pl.ds(pl.multiple_of(r * rb + b * tall, tall), tall)
            v = wide[rs, :]
            cdf = 0.5 + 0.5 * lax.erf(v * (1.0 / math.sqrt(2.0)))
            act[col, rs, :] = (v * cdf).astype(bf16)
            density = jnp.exp(v * v * -0.5) * (1.0 / math.sqrt(2.0 * math.pi))
            low = (cot_v[rs, :].astype(f32) * (cdf + v * density)).astype(bf16)
            glow[rs, :] = low
            return total + jnp.sum(low.astype(f32).reshape(tall // 8, 8, part), axis=0)

        return lax.fori_loop(0, rb // tall, step, total)

    def grads(r):
        rs = slice(r * rb, (r + 1) * rb)
        low = glow[rs, :]

        def term(q):
            return nt(low, w_v[pl.ds(pl.multiple_of(q * part, part), part), :])

        csend[r, 0] = term(pair).astype(bf16)
        csend[r, 1] = term(dcol).astype(bf16)
        put(csend.at[r], crecv.at[r], rc_s.at[r], rc_r.at[r], (me, pair))
        keep_own[rs, :] = term(col)
        keep_far[rs, :] = term(xcol)

    def grads_over(r):
        rs = slice(r * rb, (r + 1) * rb)
        got(crecv.at[r], rc_r.at[r])
        xsend[r] = (keep_far[rs, :] + crecv[r, 1].astype(f32)).astype(bf16)
        put(xsend.at[r], xrecv.at[r], rx_s.at[r], rx_r.at[r], (me, xcol))
        keep_own[rs, :] += crecv[r, 0].astype(f32)

    def grads_in(r):
        rs = slice(r * rb, (r + 1) * rb)
        got(xrecv.at[r], rx_r.at[r])
        gm[rs, :] = (keep_own[rs, :] + xrecv[r].astype(f32)).astype(bf16)

    for r in range(BLOCKS):
        cross(0, r)
        if r:
            first_half(r - 1)
    total = jnp.zeros((8, part), f32)
    for r in range(BLOCKS):
        cross(1, r)
        if r == 0:
            first_half(BLOCKS - 1)
        else:
            grads_over(r - 1)
        second_half(r)
        total = smooth(r, total)
        grads(r)

    bsend[...] = total

    def cols(h):
        return slice(h * half, (h + 1) * half)

    def weight_chunk(chunk, h):
        return tn(merged[lax.div(chunk, HALVES), lax.rem(chunk, HALVES)], glow[:, cols(h)])

    fine = kb == half
    if not fine:
        for chunk in range(ncol * HALVES):
            wacc[chunk * half : (chunk + 1) * half, :] = tn(merged[chunk // HALVES, chunk % HALVES], glow[...])

    def block_rows(b):
        return pl.ds(pl.multiple_of(b * kb, kb), kb)

    low = zz < depth // 2
    ahead = jnp.where(low, depth - 1 - zz, zz)

    def place(k):
        up = jnp.where(k < ahead, depth - 1 - k, k - ahead)
        return jnp.where(low, up, depth - 1 - up)

    def weight_out(h, k):
        z = place(k)
        theirs, mine = z * 2 + 1 - yy, z * 2 + yy
        if fine:
            ysend[h, z] = weight_chunk(theirs, h).astype(bf16)
        else:
            ysend[h, z] = wacc[block_rows(theirs), cols(h)].astype(bf16)
        put(ysend.at[h, z], yrecv.at[h, z], y_s.at[h, z], y_r.at[h, z], ypeer)
        if fine:
            wacc[block_rows(mine), cols(h)] = weight_chunk(mine, h)

    before, after = me - 2, me + 2

    def weight_sum(h, k):
        z = place(k)
        got(yrecv.at[h, z], y_r.at[h, z])
        total = wacc[block_rows(z * 2 + yy), cols(h)] + yrecv[h, z].astype(f32)
        if k == depth - 1:
            wacc[block_rows(me), cols(h)] = total

            @pl.when(zz > 0)
            def _():
                got(from_before.at[h, zz], fb_r.at[h, zz])
                wacc[block_rows(me), cols(h)] += from_before[h, zz].astype(f32)

            @pl.when(zz < depth - 1)
            def _():
                got(from_after.at[h, zz], fa_r.at[h, zz])
                wacc[block_rows(me), cols(h)] += from_after[h, zz].astype(f32)

            wfin[h, me] = wacc[block_rows(me), cols(h)].astype(bf16)
            weight_share(h, me)
            return
        zsend[h, z] = total.astype(bf16)

        @pl.when(z > zz)
        def _():
            @pl.when(zz > 0)
            def _():
                got(from_before.at[h, z], fb_r.at[h, z])
                zsend[h, z] = (total + from_before[h, z].astype(f32)).astype(bf16)

            start(zsend.at[h, z], from_before.at[h, z], z_s.at[h, z], fb_r.at[h, z], (after, col))

        @pl.when(z < zz)
        def _():
            @pl.when(zz < depth - 1)
            def _():
                got(from_after.at[h, z], fa_r.at[h, z])
                zsend[h, z] = (total + from_after[h, z].astype(f32)).astype(bf16)

            start(zsend.at[h, z], from_after.at[h, z], z_s.at[h, z], fa_r.at[h, z], (before, col))

    def weight_share(h, b, up=True, down=True):
        z = lax.div(b, 2)
        block = wfin.at[h, b]
        if up:
            @pl.when(zz < depth - 1)
            def _():
                start(block, block, zu_s.at[h, z], zg_r.at[h, z], (after, col))
        if down:
            @pl.when(zz > 0)
            def _():
                start(block, block, zd_s.at[h, z], zg_r.at[h, z], (before, col))
        start(block, block, yg_s.at[h, z], yg_r.at[h, z], ypeer)

    def weight_on(h, d):
        @pl.when(zz >= d)
        def _():
            got(wfin.at[h, me - 2 * d], zg_r.at[h, zz - d])
            weight_share(h, me - 2 * d, down=False)

        @pl.when(zz + d < depth)
        def _():
            got(wfin.at[h, me + 2 * d], zg_r.at[h, zz + d])
            weight_share(h, me + 2 * d, up=False)

    def weight_end(h):
        for z in range(depth):
            got(wfin.at[h, z * 2 + 1 - yy], yg_r.at[h, z])
            sent(wfin.at[h, z * 2 + yy], yg_s.at[h, z])

            @pl.when(z != zz)
            def _():
                sent(zsend.at[h, z], z_s.at[h, z])

            @pl.when((z <= zz) & (zz < depth - 1))
            def _():
                sent(wfin.at[h, z * 2 + yy], zu_s.at[h, z])

            @pl.when((z >= zz) & (zz > 0))
            def _():
                sent(wfin.at[h, z * 2 + yy], zd_s.at[h, z])

    for h in range(HALVES):
        for k in range(depth):
            weight_out(h, k)
            if h == 0 and k == 0:
                grads_over(BLOCKS - 1)

    def bias_copy(t):
        pltpu.make_async_remote_copy(
            src_ref=bsend, dst_ref=brecv.at[me], send_sem=b_s.at[t], recv_sem=b_r.at[me],
            device_id=(t, col), device_id_type=MESH,
        ).start()

    peers(bias_copy)

    def act_over(r):
        piece = act.at[col, pl.ds(r * rb, rb)]
        put(piece, piece, ax_s.at[r], ax_r.at[r], (me, xcol))

    own_act = act.at[col]
    put(own_act, own_act, ac_s.at[0], ac_r.at[0], (me, pair))

    steps = [functools.partial(weight_sum, h, k) for h in range(HALVES) for k in range(depth)]
    steps.pop(0)()
    grads_in(0)
    steps.pop(0)()
    grads_in(1)
    for _ in range(depth - 2):
        steps.pop(0)()
    grads_in(2)
    act_over(0)
    steps.pop(0)()
    grads_in(3)
    for r in range(1, BLOCKS):
        act_over(r)

    def sent_in(h):
        peers(lambda t: sent(outg.at[h, t], in_s.at[h, t]))

    for h in range(HALVES):
        sent_in(h)

    def back_copy(h, t):
        pltpu.make_async_remote_copy(
            src_ref=outg.at[h, t], dst_ref=ret.at[h, me], send_sem=ret_s.at[h, t], recv_sem=ret_r.at[h, me],
            device_id=(t, col), device_id_type=MESH,
        ).start()

    for g in range(groups):
        if groups > 1:
            far_group(g)
        pool_grad = nn(far[...], gm[...]).astype(bf16)
        for h in range(HALVES):
            outg[h, g * gd : (g + 1) * gd] = pool_grad[:, h * half : (h + 1) * half].reshape(gd, slots, half)
    for h in range(HALVES):
        peers(functools.partial(back_copy, h))
        ret[h, me] = jnp.zeros((slots, half), bf16)
    for k in range(1, depth - 1):
        steps.pop(0)()
        weight_on(0, k)
    for r in range(BLOCKS):
        rs = slice(r * rb, (r + 1) * rb)
        wide[rs, :] = nn(near[rs, :], gm[...])
    steps.pop(0)()
    weight_on(0, depth - 1)
    weight_on(1, 1)

    for h in range(HALVES):
        hs = slice(h * half, (h + 1) * half)
        peers(lambda s: got(ret.at[h, s], ret_r.at[h, s]))
        for g in range(groups):
            if groups > 1:
                put_selector(g)
            back = ret[h, g * gd : (g + 1) * gd].reshape(gs, half)
            for r in range(BLOCKS):
                rs = slice(r * rb, (r + 1) * rb)
                wide[rs, hs] += tn(sel[:, rs], back)
        ig_out[:, hs] = wide[:, hs].astype(bf16)

    for d in range(2, depth):
        weight_on(1, d)
    for r in range(BLOCKS):
        piece = act.at[xcol, pl.ds(r * rb, rb)]
        got(piece, ax_r.at[r])
        put(piece, piece, af_s.at[r], af_r.at[r], (me, pair))
    got(act.at[pair], ac_r.at[0])
    peers(lambda s: got(brecv.at[s], b_r.at[s]))
    brecv[me] = bsend[...]
    bg_out[...] = jnp.sum(brecv[...].reshape(n * 8, part), axis=0, keepdims=True)
    for r in range(BLOCKS):
        got(act.at[dcol, pl.ds(r * rb, rb)], af_r.at[r])
    for h in range(HALVES):
        weight_end(h)

    peers(lambda t: sent(bsend, b_s.at[t]))
    for h in range(HALVES):
        peers(lambda t: sent(outg.at[h, t], ret_s.at[h, t]))
    for copy in pending:
        copy.wait_send()


WRITES = 8


def store(act, ig, wg, bg, act_out, ig_out, wg_out, bg_out, wide, some_s, wg_s):
    ncol, part = act.shape[0], act.shape[2]
    copies = []
    for q in range(ncol):
        copies.append(pltpu.make_async_copy(act.at[q], act_out.at[:, q * part : (q + 1) * part], some_s.at[q]))
        copies[-1].start()
    copies.append(pltpu.make_async_copy(ig, ig_out, some_s.at[ncol]))
    copies[-1].start()
    tall = wide.shape[0] // WRITES
    group, half = wg.shape[1] // WRITES, wg.shape[3]
    for p in range(WRITES):
        rs = slice(p * tall, (p + 1) * tall)
        for h in range(HALVES):
            wide[rs, h * half : (h + 1) * half] = wg[h, p * group : (p + 1) * group].reshape(tall, half).astype(f32)
        copies.append(pltpu.make_async_copy(wide.at[rs], wg_out.at[rs], wg_s.at[p]))
        copies[-1].start()
    bg_out[...] = bg[...]
    for copy in copies:
        copy.wait()


def local(
    features, weight, layer_bias, cotangent, self_weight, local_index, local_weight, send_index, remote_slot, remote_weight,
    *, n, ncol,
):
    rows, part = features.shape
    width = weight.shape[0]
    slots = send_index.shape[2]
    half, rb = part // HALVES, rows // BLOCKS
    gs = min(8, n) * slots
    depth, kb = n // 2, width // n
    edges = local_index.shape[1] + 1 + remote_slot.shape[1]
    vmem = pl.BlockSpec(memory_space=pltpu.VMEM)
    hbm = pl.BlockSpec(memory_space=pl.ANY)
    V = pltpu.VMEM
    S = lambda *shape: pltpu.SemaphoreType.DMA(shape)
    buffers = [
        V((width, part), bf16), V((rows, part), bf16), V((gs, rows), bf16), V((rows, rows), bf16), V((gs, rows), bf16),
        V((edges, 8, rows), i32), V((edges, 8, rows), f32),
        V((HALVES, n, slots, half), bf16), V((HALVES, n, slots, half), bf16), V((rows, part), f32),
        V((ncol, HALVES, rows, half), bf16), V((rows, part), bf16),
        V((rows, part), f32), V((rows, part), f32),
        V((BLOCKS, 2, rb, part), bf16), V((BLOCKS, 2, rb, part), bf16), V((BLOCKS, rb, part), bf16), V((BLOCKS, rb, part), bf16),
        V((rows, part), bf16), V((width, part), f32),
        *[V((HALVES, depth, kb, half), bf16) for _ in range(5)],
        V((8, part), f32), V((n, 8, part), f32), V((HALVES, n, slots, half), bf16),
    ]
    semaphores = [
        S(2), S(HALVES, n), S(HALVES, n), S(2), S(2),
        S(HALVES, BLOCKS), S(HALVES, BLOCKS), S(HALVES, BLOCKS), S(HALVES, BLOCKS), S(HALVES, BLOCKS), S(HALVES, BLOCKS),
        S(BLOCKS), S(BLOCKS), S(BLOCKS), S(BLOCKS),
        *[S(HALVES, depth) for _ in range(10)],
        S(n), S(n), S(HALVES, n), S(HALVES, n),
        S(BLOCKS), S(BLOCKS), S(1), S(1), S(BLOCKS), S(BLOCKS),
    ]
    results = pl.pallas_call(
        functools.partial(layer, n=n, ncol=ncol),
        out_shape=(
            V((ncol, rows, part), bf16),
            V((rows, part), bf16),
            V((HALVES, n, kb, half), bf16),
            V((1, part), f32),
        ),
        in_specs=[vmem, hbm, vmem, hbm, vmem, vmem, vmem, vmem, vmem, vmem],
        out_specs=(vmem,) * 4,
        scratch_shapes=buffers + semaphores,
        compiler_params=pltpu.CompilerParams(
            collective_id=0, has_side_effects=True, vmem_limit_bytes=54 << 20
        ),
        cost_estimate=pl.CostEstimate(flops=11 << 30, bytes_accessed=16 << 20, transcendentals=1 << 20),
    )(
        features, weight, layer_bias[None, :], cotangent, self_weight[None, :], local_index.T, local_weight.T,
        send_index[0], remote_slot.T, remote_weight.T,
    )
    output, input_grad, weight_grad, bias_grad = pl.pallas_call(
        store,
        out_shape=(
            jax.ShapeDtypeStruct((rows, ncol * part), bf16),
            jax.ShapeDtypeStruct((rows, part), bf16),
            jax.ShapeDtypeStruct((width, part), f32),
            jax.ShapeDtypeStruct((1, part), f32),
        ),
        in_specs=[vmem] * 4,
        out_specs=(hbm, hbm, hbm, vmem),
        scratch_shapes=[V((width, part), f32), S(ncol + 1), S(WRITES)],
        compiler_params=pltpu.CompilerParams(vmem_limit_bytes=6 << 20),
        cost_estimate=pl.CostEstimate(flops=0, bytes_accessed=10 << 20, transcendentals=0),
    )(*results)
    return output, input_grad, weight_grad, bias_grad[0]


def solution(mesh):
    placed = (
        P("clu", "col"),
        P(None, "col"),
        P("col"),
        P("clu", "col"),
        P("clu"),
        P("clu", None),
        P("clu", None),
        P("clu", None, None),
        P("clu", None),
        P("clu", None),
    )
    return jax.shard_map(
        functools.partial(local, n=mesh.shape["clu"], ncol=mesh.shape["col"]),
        mesh=mesh,
        in_specs=placed,
        out_specs=(P("clu", None), P("clu", "col"), P(None, "col"), P("col")),
        check_vma=False,
    )
```

```python
import functools
import math

import jax
import jax.numpy as jnp
from jax import lax
from jax.experimental import pallas as pl
from jax.experimental.pallas import tpu as pltpu
from jax.sharding import PartitionSpec as P

enhance = 1.0
f32, bf16, i32 = jnp.float32, jnp.bfloat16, jnp.int32
MESH = pl.DeviceIdType.MESH
BLOCKS = 4
HALVES = 2
QUARTERS = 4
UNROLL = 8
ORDER = (
    (0, 0), (0, 1), (1, 0), (1, 1), (0, 2), (1, 2), (2, 0), (2, 1), (2, 2),
    (3, 0), (0, 3), (3, 1), (1, 3), (3, 2), (2, 3), (3, 3),
)


def tn(a, b):
    return lax.dot_general(a, b, (((0,), (0,)), ((), ())), preferred_element_type=f32)


def nt(a, b):
    return lax.dot_general(a, b, (((1,), (1,)), ((), ())), preferred_element_type=f32)


def nn(a, b):
    return jnp.dot(a, b, preferred_element_type=f32)


def layer(
    feat, weight_in, bias, cot_in, selfw, lidx, lwgt, send, ridx, rwgt,
    act, ig_out, wfin, bg_out,
    w_v, cot_v, sel, near, far, turned, edge_pos, edge_w, outg, incg, wide, merged, glow, keep_own, keep_far,
    csend, crecv, xsend, xrecv, gm, wacc, ysend, yrecv, zsend, from_before, from_after, bsend, brecv, ret,
    load_s, in_s, in_r, tab_s, tab_r, mx_s, mx_r, mc_s, mc_r, mf_s, mf_r, rc_s, rc_r, rx_s, rx_r,
    y_s, y_r, z_s, fb_r, fa_r, zu_s, zd_s, zg_r, yg_s, yg_r, b_s, b_r, ret_s, ret_r, ax_s, ax_r, ac_s, ac_r, af_s, af_r,
    *, n, ncol,
):
    rows, part = feat.shape
    half, quarter = part // HALVES, part // QUARTERS
    per_half = QUARTERS // HALVES
    rb = rows // BLOCKS
    slots = send.shape[1]
    gd = min(8, n)
    groups = n // gd
    gs = gd * slots
    depth = n // 2
    kb = wacc.shape[0] // n

    me = lax.axis_index("clu")
    col = lax.axis_index("col")
    zz, yy = lax.div(me, 2), lax.rem(me, 2)
    core = lax.rem(col, 2)
    pair = col + 1 - 2 * core
    xcol = lax.rem(col + ncol // 2, ncol)
    dcol = lax.rem(pair + ncol // 2, ncol)
    ypeer = (me + 1 - 2 * yy, col)
    pending = []

    def start(src, dst, ss, rs, dev):
        copy = pltpu.make_async_remote_copy(
            src_ref=src, dst_ref=dst, send_sem=ss, recv_sem=rs, device_id=dev, device_id_type=MESH
        )
        copy.start()
        return copy

    def put(*args):
        pending.append(start(*args))

    def got(dst, rs):
        pltpu.make_async_remote_copy(
            src_ref=dst, dst_ref=dst, send_sem=rs, recv_sem=rs, device_id=(me, pair), device_id_type=MESH
        ).wait_recv()

    def sent(src, ss):
        pltpu.make_async_remote_copy(
            src_ref=src, dst_ref=src, send_sem=ss, recv_sem=ss, device_id=(me, pair), device_id_type=MESH
        ).wait_send()

    def peers(step):
        def body(k, carry):
            step(lax.rem(me + k, n))
            return carry

        lax.fori_loop(1, n, body, 0)

    load_w = pltpu.make_async_copy(weight_in, w_v, load_s.at[0])
    load_c = pltpu.make_async_copy(cot_in, cot_v, load_s.at[1])
    load_w.start()
    load_c.start()
    barrier = pltpu.get_barrier_semaphore()
    peers(lambda t: pl.semaphore_signal(barrier, inc=1, device_id=(t, col), device_id_type=MESH))
    for other in (pair, xcol):
        pl.semaphore_signal(barrier, inc=1, device_id=(me, other), device_id_type=MESH)

    lane = lax.broadcasted_iota(i32, (slots, rows), 1)

    def put_selector(g):
        ids = send[g * gd : (g + 1) * gd, :].T
        for d in range(gd):
            sel[d * slots : (d + 1) * slots, :] = jnp.where(ids[:, d : d + 1] == lane, 1.0, 0.0).astype(bf16)

    def half_of(ref, h, *at):
        return jnp.concatenate([ref[(h * per_half + p, *at)] for p in range(per_half)], axis=-1)

    def in_copy(q, t):
        pltpu.make_async_remote_copy(
            src_ref=outg.at[q, t], dst_ref=incg.at[q, me], send_sem=in_s.at[q, t], recv_sem=in_r.at[q, me],
            device_id=(t, col), device_id_type=MESH,
        ).start()

    for q in range(QUARTERS):
        if q % per_half == 0:
            for g in range(groups):
                if groups > 1 or q == 0:
                    put_selector(g)
                at = q // per_half * half
                rows_out = nn(sel[...], feat[:, at : at + half]).astype(bf16)
                for p in range(per_half):
                    piece = rows_out[:, p * quarter : (p + 1) * quarter].reshape(gd, slots, quarter)
                    outg[q // per_half * per_half + p, g * gd : (g + 1) * gd] = piece
        if q == 0:
            pl.semaphore_wait(barrier, n + 1)
        peers(functools.partial(in_copy, q))
        incg[q, me] = jnp.zeros((slots, quarter), bf16)

    local_edges, far_edges = lidx.shape[0], ridx.shape[0]
    first_far = local_edges + 1

    def put_edges(at, idx, w):
        for k in range(idx.shape[0]):
            edge_pos[at + k] = jnp.broadcast_to(idx[k : k + 1, :], (8, rows))
            edge_w[at + k] = jnp.broadcast_to(w[k : k + 1, :], (8, rows))

    put_edges(0, lidx[...], lwgt[...])
    put_edges(local_edges, lax.broadcasted_iota(i32, (1, rows), 1), (1.0 + enhance) * selfw[...])
    put_edges(first_far, ridx[...], rwgt[...])
    sub = lax.broadcasted_iota(i32, (8, 128), 0)

    def table(dst, block, first, count, base, edge_from, edge_to):
        tall = 16 * UNROLL

        def lanes(l, carry):
            ls = pl.ds(pl.multiple_of(l * 128, 128), 128)

            def step(b, carry):
                r0 = first + b * tall
                places = [sub + (base + r0 + 8 * u) for u in range(2 * UNROLL)]
                sums = [jnp.zeros((8, 128), f32)] * (2 * UNROLL)
                for k in range(edge_from, edge_to):
                    at, w = edge_pos[k, :, ls], edge_w[k, :, ls]
                    sums = [s + jnp.where(at == p, w, 0.0) for s, p in zip(sums, places)]
                inner = pl.ds(pl.multiple_of(l * 128 - block * rb, 128), 128)
                dst[block, pl.ds(pl.multiple_of(r0, 16), tall), inner] = jnp.concatenate(sums, 0).astype(bf16)
                return carry

            return lax.fori_loop(0, count // tall, step, carry)

        lax.fori_loop(block * rb // 128, (block + 1) * rb // 128, lanes, 0)

    def shared_part(dst, r, whose):
        count = dst.shape[1] // 2
        return dst.at[r, pl.ds(pl.multiple_of(whose * count, count), count)]

    def shared_table(dst, which, r, edge_from, edge_to):
        count = dst.shape[1] // 2
        table(dst, r, core * count, count, 0, edge_from, edge_to)
        piece = shared_part(dst, r, core)
        put(piece, piece, tab_s.at[which, r], tab_r.at[which, r], (me, pair))

    def far_group(g):
        for r in range(BLOCKS):
            table(far, r, 0, gs, g * gs, first_far, first_far + far_edges)

    def build(r):
        shared_table(near, 0, r, 0, first_far)
        if groups == 1:
            shared_table(far, 1, r, first_far, first_far + far_edges)

    def ready(r):
        rs = slice(r * rb, (r + 1) * rb)
        got(shared_part(near, r, 1 - core), tab_r.at[0, r])
        wide[rs, :] = tn(near[r], feat[...])
        if groups == 1:
            got(shared_part(far, r, 1 - core), tab_r.at[1, r])
            turned[rs, :] = far[r].T

    def arrived(q):
        peers(lambda s: got(incg.at[q, s], in_r.at[q, s]))

    def piece_of(owner, q, r):
        return merged.at[owner, q, pl.ds(r * rb, rb)]

    def aggregate(q, r):
        rs = slice(r * rb, (r + 1) * rb)
        total = wide[rs, q * quarter : (q + 1) * quarter]
        if groups == 1:
            total = total + nn(turned[rs, :], incg[q].reshape(gs, quarter))
        merged[col, q, rs] = total.astype(bf16)
        piece = piece_of(col, q, r)
        put(piece, piece, mx_s.at[q, r], mx_r.at[q, r], (me, xcol))
        put(piece, piece, mc_s.at[q, r], mc_r.at[q, r], (me, pair))

    build(0)
    build(1)
    ready(0)
    if groups > 1:
        for r in range(2, BLOCKS):
            build(r)
        for r in range(1, BLOCKS):
            ready(r)
        for q in range(QUARTERS):
            arrived(q)
        for g in range(groups):
            far_group(g)
            for r in range(BLOCKS):
                rs = slice(r * rb, (r + 1) * rb)
                turned[...] = far[r].T
                for q in range(QUARTERS):
                    pooled = incg[q, g * gd : (g + 1) * gd].reshape(gs, quarter)
                    wide[rs, q * quarter : (q + 1) * quarter] += nn(turned[...], pooled)
        for q, r in ORDER:
            aggregate(q, r)
    else:
        arrived(0)
        aggregate(0, 0)
        ready(1)
        aggregate(0, 1)
        build(2)
        arrived(1)
        aggregate(1, 0)
        aggregate(1, 1)
        ready(2)
        aggregate(0, 2)
        aggregate(1, 2)
        build(3)
        arrived(2)
        for r in range(3):
            aggregate(2, r)
        ready(3)
        arrived(3)
        for q, r in ORDER[9:]:
            aggregate(q, r)

    load_w.wait()
    load_c.wait()

    def cross(count):
        for q, r in [crossing.pop(0) for _ in range(count)]:
            piece = piece_of(xcol, q, r)
            got(piece, mx_r.at[q, r])
            put(piece, piece, mf_s.at[q, r], mf_r.at[q, r], (me, pair))

    def whole_rows(h, r):
        for q in range(h * per_half, (h + 1) * per_half):
            got(piece_of(pair, q, r), mc_r.at[q, r])
            got(piece_of(dcol, q, r), mf_r.at[q, r])

    crossing = list(ORDER)

    def products(h, r):
        total = None
        for q in range(ncol):
            k0 = q * part + h * half
            term = nn(half_of(merged.at[q], h, slice(r * rb, (r + 1) * rb)), w_v[k0 : k0 + half, :])
            total = term if total is None else total + term
        return total

    def first_half(r):
        whole_rows(0, r)
        wide[r * rb : (r + 1) * rb, :] = products(0, r) + bias[...].astype(f32).reshape(1, part)

    def second_half(r):
        whole_rows(1, r)
        wide[r * rb : (r + 1) * rb, :] += products(1, r)

    tall = 32

    def smooth(r, total):
        def step(b, total):
            rs = pl.ds(pl.multiple_of(r * rb + b * tall, tall), tall)
            v = wide[rs, :]
            cdf = 0.5 + 0.5 * lax.erf(v * (1.0 / math.sqrt(2.0)))
            act[col, rs, :] = (v * cdf).astype(bf16)
            density = jnp.exp(v * v * -0.5) * (1.0 / math.sqrt(2.0 * math.pi))
            low = (cot_v[rs, :].astype(f32) * (cdf + v * density)).astype(bf16)
            glow[rs, :] = low
            return total + jnp.sum(low.astype(f32).reshape(tall // 8, 8, part), axis=0)

        return lax.fori_loop(0, rb // tall, step, total)

    def grads(r):
        rs = slice(r * rb, (r + 1) * rb)
        low = glow[rs, :]

        def term(q):
            return nt(low, w_v[pl.ds(pl.multiple_of(q * part, part), part), :])

        csend[r, 0] = term(pair).astype(bf16)
        csend[r, 1] = term(dcol).astype(bf16)
        put(csend.at[r], crecv.at[r], rc_s.at[r], rc_r.at[r], (me, pair))
        keep_own[rs, :] = term(col)
        keep_far[rs, :] = term(xcol)

    def grads_over(r):
        rs = slice(r * rb, (r + 1) * rb)
        got(crecv.at[r], rc_r.at[r])
        xsend[r] = (keep_far[rs, :] + crecv[r, 1].astype(f32)).astype(bf16)
        put(xsend.at[r], xrecv.at[r], rx_s.at[r], rx_r.at[r], (me, xcol))
        keep_own[rs, :] += crecv[r, 0].astype(f32)

    def grads_in(r):
        rs = slice(r * rb, (r + 1) * rb)
        got(xrecv.at[r], rx_r.at[r])
        gm[rs, :] = (keep_own[rs, :] + xrecv[r].astype(f32)).astype(bf16)

    total = jnp.zeros((8, part), f32)
    cross(4)
    first_half(0)
    cross(2)
    first_half(1)
    cross(3)
    first_half(2)
    cross(2)
    second_half(0)
    total = smooth(0, total)
    cross(2)
    second_half(1)
    total = smooth(1, total)
    first_half(3)
    cross(2)
    second_half(2)
    total = smooth(2, total)
    grads(0)
    cross(1)
    second_half(3)
    total = smooth(3, total)

    bsend[...] = jnp.sum(total, axis=0, keepdims=True)

    def cols(h):
        return slice(h * half, (h + 1) * half)

    def weight_chunk(chunk, h):
        q, at = lax.div(chunk, HALVES), lax.rem(chunk, HALVES) * per_half
        rows_in = jnp.concatenate([merged[q, at + p] for p in range(per_half)], axis=1)
        return tn(rows_in, glow[:, cols(h)])

    fine = kb == half
    if not fine:
        for chunk in range(ncol * HALVES):
            rows_in = half_of(merged.at[chunk // HALVES], chunk % HALVES)
            wacc[chunk * half : (chunk + 1) * half, :] = tn(rows_in, glow[...])

    def block_rows(b):
        return pl.ds(pl.multiple_of(b * kb, kb), kb)

    low = zz < depth // 2
    ahead = jnp.where(low, depth - 1 - zz, zz)

    def place(k):
        up = jnp.where(k < ahead, depth - 1 - k, k - ahead)
        return jnp.where(low, up, depth - 1 - up)

    def weight_out(h, k):
        z = place(k)
        theirs, mine = z * 2 + 1 - yy, z * 2 + yy
        if fine:
            ysend[h, z] = weight_chunk(theirs, h).astype(bf16)
        else:
            ysend[h, z] = wacc[block_rows(theirs), cols(h)].astype(bf16)
        put(ysend.at[h, z], yrecv.at[h, z], y_s.at[h, z], y_r.at[h, z], ypeer)
        if fine:
            wacc[block_rows(mine), cols(h)] = weight_chunk(mine, h)

    before, after = me - 2, me + 2

    def weight_sum(h, k):
        z = place(k)
        got(yrecv.at[h, z], y_r.at[h, z])
        total = wacc[block_rows(z * 2 + yy), cols(h)] + yrecv[h, z].astype(f32)
        if k == depth - 1:
            wacc[block_rows(me), cols(h)] = total

            @pl.when(zz > 0)
            def _():
                got(from_before.at[h, zz], fb_r.at[h, zz])
                wacc[block_rows(me), cols(h)] += from_before[h, zz].astype(f32)

            @pl.when(zz < depth - 1)
            def _():
                got(from_after.at[h, zz], fa_r.at[h, zz])
                wacc[block_rows(me), cols(h)] += from_after[h, zz].astype(f32)

            wfin[h, me] = wacc[block_rows(me), cols(h)].astype(bf16)
            weight_share(h, me)
            return
        zsend[h, z] = total.astype(bf16)

        @pl.when(z > zz)
        def _():
            @pl.when(zz > 0)
            def _():
                got(from_before.at[h, z], fb_r.at[h, z])
                zsend[h, z] = (total + from_before[h, z].astype(f32)).astype(bf16)

            start(zsend.at[h, z], from_before.at[h, z], z_s.at[h, z], fb_r.at[h, z], (after, col))

        @pl.when(z < zz)
        def _():
            @pl.when(zz < depth - 1)
            def _():
                got(from_after.at[h, z], fa_r.at[h, z])
                zsend[h, z] = (total + from_after[h, z].astype(f32)).astype(bf16)

            start(zsend.at[h, z], from_after.at[h, z], z_s.at[h, z], fa_r.at[h, z], (before, col))

    def weight_share(h, b, up=True, down=True):
        z = lax.div(b, 2)
        block = wfin.at[h, b]
        if up:
            @pl.when(zz < depth - 1)
            def _():
                start(block, block, zu_s.at[h, z], zg_r.at[h, z], (after, col))
        if down:
            @pl.when(zz > 0)
            def _():
                start(block, block, zd_s.at[h, z], zg_r.at[h, z], (before, col))
        start(block, block, yg_s.at[h, z], yg_r.at[h, z], ypeer)

    def weight_on(h, d):
        @pl.when(zz >= d)
        def _():
            got(wfin.at[h, me - 2 * d], zg_r.at[h, zz - d])
            weight_share(h, me - 2 * d, down=False)

        @pl.when(zz + d < depth)
        def _():
            got(wfin.at[h, me + 2 * d], zg_r.at[h, zz + d])
            weight_share(h, me + 2 * d, up=False)

    def weight_end(h):
        for z in range(depth):
            got(wfin.at[h, z * 2 + 1 - yy], yg_r.at[h, z])
            sent(wfin.at[h, z * 2 + yy], yg_s.at[h, z])

            @pl.when(z != zz)
            def _():
                sent(zsend.at[h, z], z_s.at[h, z])

            @pl.when((z <= zz) & (zz < depth - 1))
            def _():
                sent(wfin.at[h, z * 2 + yy], zu_s.at[h, z])

            @pl.when((z >= zz) & (zz > 0))
            def _():
                sent(wfin.at[h, z * 2 + yy], zd_s.at[h, z])

    rest = [functools.partial(weight_out, h, k) for h in range(HALVES) for k in range(depth)]
    for r in range(1, BLOCKS):
        rest.pop(0)()
        grads_over(r - 1)
        grads(r)
    rest.pop(0)()
    grads_over(BLOCKS - 1)
    for step in rest:
        step()

    def bias_copy(t):
        pltpu.make_async_remote_copy(
            src_ref=bsend, dst_ref=brecv.at[me], send_sem=b_s.at[t], recv_sem=b_r.at[me],
            device_id=(t, col), device_id_type=MESH,
        ).start()

    peers(bias_copy)

    def act_over(r):
        piece = act.at[col, pl.ds(r * rb, rb)]
        put(piece, piece, ax_s.at[r], ax_r.at[r], (me, xcol))

    own_act = act.at[col]
    put(own_act, own_act, ac_s.at[0], ac_r.at[0], (me, pair))

    steps = [functools.partial(weight_sum, h, k) for h in range(HALVES) for k in range(depth)]
    steps.pop(0)()
    grads_in(0)
    steps.pop(0)()
    grads_in(1)
    for _ in range(depth - 2):
        steps.pop(0)()
    grads_in(2)
    act_over(0)
    steps.pop(0)()
    grads_in(3)
    for r in range(1, BLOCKS):
        act_over(r)

    def sent_in(q):
        peers(lambda t: sent(outg.at[q, t], in_s.at[q, t]))

    for q in range(QUARTERS):
        sent_in(q)

    def back_copy(q, t):
        pltpu.make_async_remote_copy(
            src_ref=outg.at[q, t], dst_ref=ret.at[q, me],
            send_sem=ret_s.at[q, t], recv_sem=ret_r.at[q, me], device_id=(t, col), device_id_type=MESH,
        ).start()

    for g in range(groups):
        if groups > 1:
            far_group(g)
        pool_grad = nn(jnp.concatenate([far[r] for r in range(BLOCKS)], axis=1), gm[...]).astype(bf16)
        for q in range(QUARTERS):
            outg[q, g * gd : (g + 1) * gd] = pool_grad[:, q * quarter : (q + 1) * quarter].reshape(gd, slots, quarter)
    for q in range(QUARTERS):
        peers(functools.partial(back_copy, q))
        ret[q, me] = jnp.zeros((slots, quarter), bf16)
    for k in range(1, depth - 1):
        steps.pop(0)()
        weight_on(0, k)
    for r in range(BLOCKS):
        rs = slice(r * rb, (r + 1) * rb)
        wide[rs, :] = nn(jnp.concatenate([near[b, rs] for b in range(BLOCKS)], axis=1), gm[...])
    steps.pop(0)()
    weight_on(0, depth - 1)
    weight_on(1, 1)

    for d in range(2, depth):
        weight_on(1, d)

    for h in range(HALVES):
        hs = slice(h * half, (h + 1) * half)
        for q in range(h * per_half, (h + 1) * per_half):
            peers(lambda s: got(ret.at[q, s], ret_r.at[q, s]))
        for g in range(groups):
            if groups > 1:
                put_selector(g)
            back = half_of(ret, h, slice(g * gd, (g + 1) * gd)).reshape(gs, half)
            for r in range(BLOCKS):
                rs = slice(r * rb, (r + 1) * rb)
                wide[rs, hs] += tn(sel[:, rs], back)
        ig_out[:, hs] = wide[:, hs].astype(bf16)

    for r in range(BLOCKS):
        piece = act.at[xcol, pl.ds(r * rb, rb)]
        got(piece, ax_r.at[r])
        put(piece, piece, af_s.at[r], af_r.at[r], (me, pair))
    got(act.at[pair], ac_r.at[0])
    peers(lambda s: got(brecv.at[s], b_r.at[s]))
    brecv[me] = bsend[...]
    bg_out[...] = jnp.sum(brecv[...], axis=0)
    for r in range(BLOCKS):
        got(act.at[dcol, pl.ds(r * rb, rb)], af_r.at[r])
    for h in range(HALVES):
        weight_end(h)

    peers(lambda t: sent(bsend, b_s.at[t]))
    for q in range(QUARTERS):
        peers(lambda t: sent(outg.at[q, t], ret_s.at[q, t]))
    for copy in pending:
        copy.wait_send()


WRITES = 8


def store(act, ig, wg, bg, act_out, ig_out, wg_out, bg_out, wide, some_s, wg_s):
    ncol, part = act.shape[0], act.shape[2]
    copies = []
    for q in range(ncol):
        copies.append(pltpu.make_async_copy(act.at[q], act_out.at[:, q * part : (q + 1) * part], some_s.at[q]))
        copies[-1].start()
    copies.append(pltpu.make_async_copy(ig, ig_out, some_s.at[ncol]))
    copies[-1].start()
    tall = wide.shape[0] // WRITES
    group, half = wg.shape[1] // WRITES, wg.shape[3]
    for p in range(WRITES):
        rs = slice(p * tall, (p + 1) * tall)
        for h in range(HALVES):
            wide[rs, h * half : (h + 1) * half] = wg[h, p * group : (p + 1) * group].reshape(tall, half).astype(f32)
        copies.append(pltpu.make_async_copy(wide.at[rs], wg_out.at[rs], wg_s.at[p]))
        copies[-1].start()
    bg_out[...] = bg[...]
    for copy in copies:
        copy.wait()


def local(
    features, weight, layer_bias, cotangent, self_weight, local_index, local_weight, send_index, remote_slot, remote_weight,
    *, n, ncol,
):
    rows, part = features.shape
    width = weight.shape[0]
    slots = send_index.shape[2]
    half, quarter, rb = part // HALVES, part // QUARTERS, rows // BLOCKS
    gs = min(8, n) * slots
    depth, kb = n // 2, width // n
    edges = local_index.shape[1] + 1 + remote_slot.shape[1]
    vmem = pl.BlockSpec(memory_space=pltpu.VMEM)
    hbm = pl.BlockSpec(memory_space=pl.ANY)
    V = pltpu.VMEM
    S = lambda *shape: pltpu.SemaphoreType.DMA(shape)
    buffers = [
        V((width, part), bf16), V((rows, part), bf16), V((gs, rows), bf16), V((BLOCKS, rows, rb), bf16), V((BLOCKS, gs, rb), bf16),
        V((rows if n <= 8 else rb, gs), bf16),
        V((edges, 8, rows), i32), V((edges, 8, rows), f32),
        V((QUARTERS, n, slots, quarter), bf16), V((QUARTERS, n, slots, quarter), bf16), V((rows, part), f32),
        V((ncol, QUARTERS, rows, quarter), bf16), V((rows, part), bf16),
        V((rows, part), f32), V((rows, part), f32),
        V((BLOCKS, 2, rb, part), bf16), V((BLOCKS, 2, rb, part), bf16), V((BLOCKS, rb, part), bf16), V((BLOCKS, rb, part), bf16),
        V((rows, part), bf16), V((width, part), f32),
        *[V((HALVES, depth, kb, half), bf16) for _ in range(5)],
        V((1, part), f32), V((n, 1, part), f32), V((QUARTERS, n, slots, quarter), bf16),
    ]
    semaphores = [
        S(2), S(QUARTERS, n), S(QUARTERS, n), S(2, BLOCKS), S(2, BLOCKS),
        *[S(QUARTERS, BLOCKS) for _ in range(6)],
        S(BLOCKS), S(BLOCKS), S(BLOCKS), S(BLOCKS),
        *[S(HALVES, depth) for _ in range(10)],
        S(n), S(n), S(QUARTERS, n), S(QUARTERS, n),
        S(BLOCKS), S(BLOCKS), S(1), S(1), S(BLOCKS), S(BLOCKS),
    ]
    results = pl.pallas_call(
        functools.partial(layer, n=n, ncol=ncol),
        out_shape=(
            V((ncol, rows, part), bf16),
            V((rows, part), bf16),
            V((HALVES, n, kb, half), bf16),
            V((1, part), f32),
        ),
        in_specs=[vmem, hbm, vmem, hbm, vmem, vmem, vmem, vmem, vmem, vmem],
        out_specs=(vmem,) * 4,
        scratch_shapes=buffers + semaphores,
        compiler_params=pltpu.CompilerParams(
            collective_id=0, has_side_effects=True, vmem_limit_bytes=54 << 20
        ),
        cost_estimate=pl.CostEstimate(flops=11 << 30, bytes_accessed=16 << 20, transcendentals=1 << 20),
    )(
        features, weight, layer_bias, cotangent, self_weight[None, :], local_index.T, local_weight.T,
        send_index[0], remote_slot.T, remote_weight.T,
    )
    output, input_grad, weight_grad, bias_grad = pl.pallas_call(
        store,
        out_shape=(
            jax.ShapeDtypeStruct((rows, ncol * part), bf16),
            jax.ShapeDtypeStruct((rows, part), bf16),
            jax.ShapeDtypeStruct((width, part), f32),
            jax.ShapeDtypeStruct((1, part), f32),
        ),
        in_specs=[vmem] * 4,
        out_specs=(hbm, hbm, hbm, vmem),
        scratch_shapes=[V((width, part), f32), S(ncol + 1), S(WRITES)],
        compiler_params=pltpu.CompilerParams(vmem_limit_bytes=6 << 20),
        cost_estimate=pl.CostEstimate(flops=0, bytes_accessed=10 << 20, transcendentals=0),
    )(*results)
    return output, input_grad, weight_grad, bias_grad[0]


def solution(mesh):
    placed = (
        P("clu", "col"),
        P(None, "col"),
        P("col"),
        P("clu", "col"),
        P("clu"),
        P("clu", None),
        P("clu", None),
        P("clu", None, None),
        P("clu", None),
        P("clu", None),
    )
    return jax.shard_map(
        functools.partial(local, n=mesh.shape["clu"], ncol=mesh.shape["col"]),
        mesh=mesh,
        in_specs=placed,
        out_specs=(P("clu", None), P("clu", "col"), P(None, "col"), P("col")),
        check_vma=False,
    )
```

```python
import functools
import math

import jax
import jax.numpy as jnp
from jax import lax
from jax.experimental import pallas as pl
from jax.experimental.pallas import tpu as pltpu
from jax.sharding import PartitionSpec as P

enhance = 1.0
f32, bf16, i32 = jnp.float32, jnp.bfloat16, jnp.int32
MESH = pl.DeviceIdType.MESH
BLOCKS = 4
HALVES = 2
QUARTERS = 4
ALONG = QUARTERS - 1
UNROLL = 8
ORDER = (
    (0, 0), (0, 1), (1, 0), (1, 1), (0, 2), (1, 2), (2, 0), (2, 1), (2, 2),
    (3, 0), (0, 3), (3, 1), (1, 3), (3, 2), (2, 3), (3, 3),
)


def tn(a, b):
    return lax.dot_general(a, b, (((0,), (0,)), ((), ())), preferred_element_type=f32)


def nt(a, b):
    return lax.dot_general(a, b, (((1,), (1,)), ((), ())), preferred_element_type=f32)


def nn(a, b):
    return jnp.dot(a, b, preferred_element_type=f32)


def layer(
    feat, weight_in, bias, cot_in, selfw, lidx, lwgt, send, ridx, rwgt,
    act, ig_out, wfin, bg_out,
    w_v, cot_v, sel, near, far, turned, edge_pos, edge_w, outg, incg, wide, merged, glow, keep_own, keep_far,
    csend, crecv, xsend, xrecv, gm, wacc, ysend, yrecv, zsend, from_before, from_after,
    pair_send, pair_before, pair_after, bsend, brecv, ret,
    load_s, in_s, in_r, tab_s, tab_r, mx_s, mx_r, mc_s, mc_r, mf_s, mf_r, rc_s, rc_r, rx_s, rx_r,
    y_s, y_r, z_s, fb_r, fa_r, zu_s, zd_s, zg_r, yg_s, yg_r, b_s, b_r, ret_s, ret_r, ax_s, ax_r, ac_s, ac_r, af_s, af_r,
    *, n, ncol,
):
    rows, part = feat.shape
    half, quarter = part // HALVES, part // QUARTERS
    per_half = QUARTERS // HALVES
    rb = rows // BLOCKS
    slots = send.shape[1]
    gd = min(8, n)
    groups = n // gd
    gs = gd * slots
    depth = n // 2
    kb = wacc.shape[0] // n

    me = lax.axis_index("clu")
    col = lax.axis_index("col")
    zz, yy = lax.div(me, 2), lax.rem(me, 2)
    core = lax.rem(col, 2)
    pair = col + 1 - 2 * core
    xcol = lax.rem(col + ncol // 2, ncol)
    dcol = lax.rem(pair + ncol // 2, ncol)
    ypeer = (me + 1 - 2 * yy, col)
    pending = []

    def start(src, dst, ss, rs, dev):
        copy = pltpu.make_async_remote_copy(
            src_ref=src, dst_ref=dst, send_sem=ss, recv_sem=rs, device_id=dev, device_id_type=MESH
        )
        copy.start()
        return copy

    def put(*args):
        pending.append(start(*args))

    def got(dst, rs):
        pltpu.make_async_remote_copy(
            src_ref=dst, dst_ref=dst, send_sem=rs, recv_sem=rs, device_id=(me, pair), device_id_type=MESH
        ).wait_recv()

    def sent(src, ss):
        pltpu.make_async_remote_copy(
            src_ref=src, dst_ref=src, send_sem=ss, recv_sem=ss, device_id=(me, pair), device_id_type=MESH
        ).wait_send()

    def peers(step):
        def body(k, carry):
            step(lax.rem(me + k, n))
            return carry

        lax.fori_loop(1, n, body, 0)

    load_w = pltpu.make_async_copy(weight_in, w_v, load_s.at[0])
    load_c = pltpu.make_async_copy(cot_in, cot_v, load_s.at[1])
    load_w.start()
    load_c.start()
    barrier = pltpu.get_barrier_semaphore()
    peers(lambda t: pl.semaphore_signal(barrier, inc=1, device_id=(t, col), device_id_type=MESH))
    for other in (pair, xcol):
        pl.semaphore_signal(barrier, inc=1, device_id=(me, other), device_id_type=MESH)

    lane = lax.broadcasted_iota(i32, (slots, rows), 1)

    def put_selector(g):
        ids = send[g * gd : (g + 1) * gd, :].T
        for d in range(gd):
            sel[d * slots : (d + 1) * slots, :] = jnp.where(ids[:, d : d + 1] == lane, 1.0, 0.0).astype(bf16)

    def half_of(ref, h, *at):
        return jnp.concatenate([ref[(h * per_half + p, *at)] for p in range(per_half)], axis=-1)

    def in_copy(q, t):
        pltpu.make_async_remote_copy(
            src_ref=outg.at[q, t], dst_ref=incg.at[q, me], send_sem=in_s.at[q, t], recv_sem=in_r.at[q, me],
            device_id=(t, col), device_id_type=MESH,
        ).start()

    for q in range(QUARTERS):
        if q % per_half == 0:
            for g in range(groups):
                if groups > 1 or q == 0:
                    put_selector(g)
                at = q // per_half * half
                rows_out = nn(sel[...], feat[:, at : at + half]).astype(bf16)
                for p in range(per_half):
                    piece = rows_out[:, p * quarter : (p + 1) * quarter].reshape(gd, slots, quarter)
                    outg[q // per_half * per_half + p, g * gd : (g + 1) * gd] = piece
        if q == 0:
            pl.semaphore_wait(barrier, n + 1)
        peers(functools.partial(in_copy, q))
        incg[q, me] = jnp.zeros((slots, quarter), bf16)

    local_edges, far_edges = lidx.shape[0], ridx.shape[0]
    first_far = local_edges + 1

    def put_edges(at, idx, w):
        for k in range(idx.shape[0]):
            edge_pos[at + k] = jnp.broadcast_to(idx[k : k + 1, :], (8, rows))
            edge_w[at + k] = jnp.broadcast_to(w[k : k + 1, :], (8, rows))

    put_edges(0, lidx[...], lwgt[...])
    put_edges(local_edges, lax.broadcasted_iota(i32, (1, rows), 1), (1.0 + enhance) * selfw[...])
    put_edges(first_far, ridx[...], rwgt[...])
    sub = lax.broadcasted_iota(i32, (8, 128), 0)

    def table(dst, block, first, count, base, edge_from, edge_to):
        tall = 16 * UNROLL

        def lanes(l, carry):
            ls = pl.ds(pl.multiple_of(l * 128, 128), 128)

            def step(b, carry):
                r0 = first + b * tall
                places = [sub + (base + r0 + 8 * u) for u in range(2 * UNROLL)]
                sums = [jnp.zeros((8, 128), f32)] * (2 * UNROLL)
                for k in range(edge_from, edge_to):
                    at, w = edge_pos[k, :, ls], edge_w[k, :, ls]
                    sums = [s + jnp.where(at == p, w, 0.0) for s, p in zip(sums, places)]
                inner = pl.ds(pl.multiple_of(l * 128 - block * rb, 128), 128)
                dst[block, pl.ds(pl.multiple_of(r0, 16), tall), inner] = jnp.concatenate(sums, 0).astype(bf16)
                return carry

            return lax.fori_loop(0, count // tall, step, carry)

        lax.fori_loop(block * rb // 128, (block + 1) * rb // 128, lanes, 0)

    def shared_part(dst, r, whose):
        count = dst.shape[1] // 2
        return dst.at[r, pl.ds(pl.multiple_of(whose * count, count), count)]

    def shared_table(dst, which, r, edge_from, edge_to):
        count = dst.shape[1] // 2
        table(dst, r, core * count, count, 0, edge_from, edge_to)
        piece = shared_part(dst, r, core)
        put(piece, piece, tab_s.at[which, r], tab_r.at[which, r], (me, pair))

    def far_group(g):
        for r in range(BLOCKS):
            table(far, r, 0, gs, g * gs, first_far, first_far + far_edges)

    def build(r):
        shared_table(near, 0, r, 0, first_far)
        if groups == 1:
            shared_table(far, 1, r, first_far, first_far + far_edges)

    def ready(r):
        rs = slice(r * rb, (r + 1) * rb)
        got(shared_part(near, r, 1 - core), tab_r.at[0, r])
        wide[rs, :] = tn(near[r], feat[...])
        if groups == 1:
            got(shared_part(far, r, 1 - core), tab_r.at[1, r])
            turned[rs, :] = far[r].T

    def arrived(q):
        peers(lambda s: got(incg.at[q, s], in_r.at[q, s]))

    def piece_of(owner, q, r):
        return merged.at[owner, q, pl.ds(r * rb, rb)]

    def aggregate(q, r):
        rs = slice(r * rb, (r + 1) * rb)
        total = wide[rs, q * quarter : (q + 1) * quarter]
        if groups == 1:
            total = total + nn(turned[rs, :], incg[q].reshape(gs, quarter))
        merged[col, q, rs] = total.astype(bf16)
        piece = piece_of(col, q, r)
        put(piece, piece, mx_s.at[q, r], mx_r.at[q, r], (me, xcol))
        put(piece, piece, mc_s.at[q, r], mc_r.at[q, r], (me, pair))

    build(0)
    build(1)
    ready(0)
    if groups > 1:
        for r in range(2, BLOCKS):
            build(r)
        for r in range(1, BLOCKS):
            ready(r)
        for q in range(QUARTERS):
            arrived(q)
        for g in range(groups):
            far_group(g)
            for r in range(BLOCKS):
                rs = slice(r * rb, (r + 1) * rb)
                turned[...] = far[r].T
                for q in range(QUARTERS):
                    pooled = incg[q, g * gd : (g + 1) * gd].reshape(gs, quarter)
                    wide[rs, q * quarter : (q + 1) * quarter] += nn(turned[...], pooled)
        for q, r in ORDER:
            aggregate(q, r)
    else:
        arrived(0)
        aggregate(0, 0)
        ready(1)
        aggregate(0, 1)
        build(2)
        arrived(1)
        aggregate(1, 0)
        aggregate(1, 1)
        ready(2)
        aggregate(0, 2)
        aggregate(1, 2)
        build(3)
        arrived(2)
        for r in range(3):
            aggregate(2, r)
        ready(3)
        arrived(3)
        for q, r in ORDER[9:]:
            aggregate(q, r)

    load_w.wait()
    load_c.wait()

    def cross(count):
        for q, r in [crossing.pop(0) for _ in range(count)]:
            piece = piece_of(xcol, q, r)
            got(piece, mx_r.at[q, r])
            put(piece, piece, mf_s.at[q, r], mf_r.at[q, r], (me, pair))

    def whole_rows(h, r):
        for q in range(h * per_half, (h + 1) * per_half):
            got(piece_of(pair, q, r), mc_r.at[q, r])
            got(piece_of(dcol, q, r), mf_r.at[q, r])

    crossing = list(ORDER)

    def products(h, r):
        total = None
        for q in range(ncol):
            k0 = q * part + h * half
            term = nn(half_of(merged.at[q], h, slice(r * rb, (r + 1) * rb)), w_v[k0 : k0 + half, :])
            total = term if total is None else total + term
        return total

    def first_half(r):
        whole_rows(0, r)
        wide[r * rb : (r + 1) * rb, :] = products(0, r) + bias[...].astype(f32).reshape(1, part)

    def second_half(r):
        whole_rows(1, r)
        wide[r * rb : (r + 1) * rb, :] += products(1, r)

    tall = 32

    def smooth(r, total):
        def step(b, total):
            rs = pl.ds(pl.multiple_of(r * rb + b * tall, tall), tall)
            v = wide[rs, :]
            cdf = 0.5 + 0.5 * lax.erf(v * (1.0 / math.sqrt(2.0)))
            act[col, rs, :] = (v * cdf).astype(bf16)
            density = jnp.exp(v * v * -0.5) * (1.0 / math.sqrt(2.0 * math.pi))
            low = (cot_v[rs, :].astype(f32) * (cdf + v * density)).astype(bf16)
            glow[rs, :] = low
            return total + jnp.sum(low.astype(f32).reshape(tall // 8, 8, part), axis=0)

        return lax.fori_loop(0, rb // tall, step, total)

    def grads(r):
        rs = slice(r * rb, (r + 1) * rb)
        low = glow[rs, :]

        def term(q):
            return nt(low, w_v[pl.ds(pl.multiple_of(q * part, part), part), :])

        csend[r, 0] = term(pair).astype(bf16)
        csend[r, 1] = term(dcol).astype(bf16)
        put(csend.at[r], crecv.at[r], rc_s.at[r], rc_r.at[r], (me, pair))
        keep_own[rs, :] = term(col)
        keep_far[rs, :] = term(xcol)

    def grads_over(r):
        rs = slice(r * rb, (r + 1) * rb)
        got(crecv.at[r], rc_r.at[r])
        xsend[r] = (keep_far[rs, :] + crecv[r, 1].astype(f32)).astype(bf16)
        put(xsend.at[r], xrecv.at[r], rx_s.at[r], rx_r.at[r], (me, xcol))
        keep_own[rs, :] += crecv[r, 0].astype(f32)

    def grads_in(r):
        rs = slice(r * rb, (r + 1) * rb)
        got(xrecv.at[r], rx_r.at[r])
        gm[rs, :] = (keep_own[rs, :] + xrecv[r].astype(f32)).astype(bf16)

    total = jnp.zeros((8, part), f32)
    cross(4)
    first_half(0)
    cross(2)
    first_half(1)
    cross(3)
    first_half(2)
    cross(2)
    second_half(0)
    total = smooth(0, total)
    cross(2)
    grads(0)
    second_half(1)
    total = smooth(1, total)
    first_half(3)
    cross(2)
    grads_over(0)
    grads(1)
    cross(1)
    second_half(2)
    total = smooth(2, total)
    second_half(3)
    total = smooth(3, total)

    bsend[...] = jnp.sum(total, axis=0, keepdims=True)

    def cols(p):
        return slice(p * quarter, (p + 1) * quarter)

    fine = kb == half
    if not fine:
        for chunk in range(ncol * HALVES):
            rows_in = half_of(merged.at[chunk // HALVES], chunk % HALVES)
            wacc[chunk * half : (chunk + 1) * half, :] = tn(rows_in, glow[...])

    def block_rows(b, count=1):
        return pl.ds(pl.multiple_of(b * kb, kb), count * kb)

    def weight_chunk(b, h):
        hs = slice(h * half, (h + 1) * half)
        if not fine:
            return wacc[block_rows(b), hs]
        q, at = lax.div(b, HALVES), lax.rem(b, HALVES) * per_half
        rows_in = jnp.concatenate([merged[q, at + p] for p in range(per_half)], axis=1)
        return tn(rows_in, glow[:, hs])

    low = zz < depth // 2
    ahead = jnp.where(low, depth - 1 - zz, zz)

    def place(k):
        up = jnp.where(k < ahead, depth - 1 - k, k - ahead)
        return jnp.where(low, up, depth - 1 - up)

    def weight_out(h, k):
        z = place(k)
        theirs, mine = z * 2 + 1 - yy, z * 2 + yy
        term = weight_chunk(theirs, h)
        for p in range(h * per_half, (h + 1) * per_half):
            piece = term[:, (p - h * per_half) * quarter : (p - h * per_half + 1) * quarter]
            if p == ALONG:
                wacc[block_rows(theirs), cols(p)] = piece
            else:
                ysend[p, z] = piece.astype(bf16)
                put(ysend.at[p, z], yrecv.at[p, z], y_s.at[p, z], y_r.at[p, z], ypeer)
        if fine:
            wacc[block_rows(mine), h * half : (h + 1) * half] = weight_chunk(mine, h)

    before, after = me - 2, me + 2

    def line_sum(p, z, total, out, came_before, came_after):
        out[z] = total.astype(bf16)

        @pl.when(z > zz)
        def _():
            @pl.when(zz > 0)
            def _():
                got(came_before.at[z], fb_r.at[p, z])
                out[z] = (total + came_before[z].astype(f32)).astype(bf16)

            start(out.at[z], came_before.at[z], z_s.at[p, z], fb_r.at[p, z], (after, col))

        @pl.when(z < zz)
        def _():
            @pl.when(zz < depth - 1)
            def _():
                got(came_after.at[z], fa_r.at[p, z])
                out[z] = (total + came_after[z].astype(f32)).astype(bf16)

            start(out.at[z], came_after.at[z], z_s.at[p, z], fa_r.at[p, z], (before, col))

    def line_end(p, rows_in, came_before, came_after):
        @pl.when(zz > 0)
        def _():
            got(came_before.at[zz], fb_r.at[p, zz])
            wacc[rows_in, cols(p)] += came_before[zz].astype(f32)

        @pl.when(zz < depth - 1)
        def _():
            got(came_after.at[zz], fa_r.at[p, zz])
            wacc[rows_in, cols(p)] += came_after[zz].astype(f32)

    def line_share(p, z, block, up=True, down=True):
        if up:
            @pl.when(zz < depth - 1)
            def _():
                start(block, block, zu_s.at[p, z], zg_r.at[p, z], (after, col))
        if down:
            @pl.when(zz > 0)
            def _():
                start(block, block, zd_s.at[p, z], zg_r.at[p, z], (before, col))

    def sent_line(p, z, out, block):
        @pl.when(z != zz)
        def _():
            sent(out.at[z], z_s.at[p, z])

        @pl.when((z <= zz) & (zz < depth - 1))
        def _():
            sent(block, zu_s.at[p, z])

        @pl.when((z >= zz) & (zz > 0))
        def _():
            sent(block, zd_s.at[p, z])

    def weight_sum(p, k):
        z = place(k)
        got(yrecv.at[p, z], y_r.at[p, z])
        rows_in = block_rows(z * 2 + yy)
        total = wacc[rows_in, cols(p)] + yrecv[p, z].astype(f32)
        if k < depth - 1:
            line_sum(p, z, total, zsend.at[p], from_before.at[p], from_after.at[p])
            return
        wacc[rows_in, cols(p)] = total
        line_end(p, rows_in, from_before.at[p], from_after.at[p])
        wfin[p, me] = wacc[rows_in, cols(p)].astype(bf16)
        line_share(p, zz, wfin.at[p, me])
        across(p, zz)

    def across(p, z):
        block = wfin.at[p, z * 2 + yy]
        start(block, block, yg_s.at[p, z], yg_r.at[p, z], ypeer)

    def weight_on(p, d):
        @pl.when(zz >= d)
        def _():
            block = wfin.at[p, me - 2 * d]
            got(block, zg_r.at[p, zz - d])
            line_share(p, zz - d, block, down=False)
            across(p, zz - d)

        @pl.when(zz + d < depth)
        def _():
            block = wfin.at[p, me + 2 * d]
            got(block, zg_r.at[p, zz + d])
            line_share(p, zz + d, block, up=False)
            across(p, zz + d)

    def weight_end(p):
        for z in range(depth):
            got(wfin.at[p, z * 2 + 1 - yy], yg_r.at[p, z])
            sent(wfin.at[p, z * 2 + yy], yg_s.at[p, z])
            sent_line(p, z, zsend.at[p], wfin.at[p, z * 2 + yy])

    def both(z):
        return wfin.at[ALONG, pl.ds(z * 2, 2)]

    def along_sum(k):
        z = place(k)
        total = wacc[block_rows(z * 2, 2), cols(ALONG)]
        line_sum(ALONG, z, total, pair_send, pair_before, pair_after)

    end = (zz == 0) | (zz == depth - 1)

    def along_from_end(k):
        @pl.when(end)
        def _():
            along_sum(k)

    def along_inside(k):
        @pl.when(jnp.logical_not(end))
        def _():
            along_sum(k)

    def along_own():
        line_end(ALONG, block_rows(zz * 2, 2), pair_before, pair_after)
        ysend[ALONG, zz] = wacc[block_rows(zz * 2 + 1 - yy), cols(ALONG)].astype(bf16)
        put(ysend.at[ALONG, zz], yrecv.at[ALONG, zz], y_s.at[ALONG, zz], y_r.at[ALONG, zz], ypeer)

    def along_across():
        got(yrecv.at[ALONG, zz], y_r.at[ALONG, zz])
        total = wacc[block_rows(me), cols(ALONG)] + yrecv[ALONG, zz].astype(f32)
        wfin[ALONG, me] = total.astype(bf16)
        across(ALONG, zz)

    def along_share():
        got(wfin.at[ALONG, zz * 2 + 1 - yy], yg_r.at[ALONG, zz])
        line_share(ALONG, zz, both(zz))

    def along_on(d):
        @pl.when(zz >= d)
        def _():
            got(both(zz - d), zg_r.at[ALONG, zz - d])
            line_share(ALONG, zz - d, both(zz - d), down=False)

        @pl.when(zz + d < depth)
        def _():
            got(both(zz + d), zg_r.at[ALONG, zz + d])
            line_share(ALONG, zz + d, both(zz + d), up=False)

    def along_end():
        sent(wfin.at[ALONG, me], yg_s.at[ALONG, zz])
        for z in range(depth):
            sent_line(ALONG, z, pair_send, both(z))

    def out_along(k):
        weight_out(HALVES - 1, k)
        if k < depth - 1:
            along_from_end(k)

    out_along(0)
    out_along(1)
    grads_over(1)
    grads(2)
    for k in range(2, depth):
        out_along(k)
    weight_out(0, 0)
    grads_over(2)
    grads(3)
    along_inside(0)
    weight_out(0, 1)
    grads_over(3)
    for k in range(1, depth - 2):
        along_inside(k)
    for k in range(2, depth):
        weight_out(0, k)
    if depth > 2:
        along_inside(depth - 2)

    def bias_copy(t):
        pltpu.make_async_remote_copy(
            src_ref=bsend, dst_ref=brecv.at[me], send_sem=b_s.at[t], recv_sem=b_r.at[me],
            device_id=(t, col), device_id_type=MESH,
        ).start()

    peers(bias_copy)

    def act_over(r):
        piece = act.at[col, pl.ds(r * rb, rb)]
        put(piece, piece, ax_s.at[r], ax_r.at[r], (me, xcol))

    own_act = act.at[col]
    put(own_act, own_act, ac_s.at[0], ac_r.at[0], (me, pair))

    def back_copy(q, t):
        pltpu.make_async_remote_copy(
            src_ref=outg.at[q, t], dst_ref=ret.at[q, me],
            send_sem=ret_s.at[q, t], recv_sem=ret_r.at[q, me], device_id=(t, col), device_id_type=MESH,
        ).start()

    def send_back():
        for q in range(QUARTERS):
            peers(lambda t: sent(outg.at[q, t], in_s.at[q, t]))
        for g in range(groups):
            if groups > 1:
                far_group(g)
            pool_grad = nn(jnp.concatenate([far[r] for r in range(BLOCKS)], axis=1), gm[...]).astype(bf16)
            for q in range(QUARTERS):
                piece = pool_grad[:, q * quarter : (q + 1) * quarter]
                outg[q, g * gd : (g + 1) * gd] = piece.reshape(gd, slots, quarter)
        for q in range(QUARTERS):
            peers(functools.partial(back_copy, q))
            ret[q, me] = jnp.zeros((slots, quarter), bf16)

    def near_back(r):
        rs = slice(r * rb, (r + 1) * rb)
        wide[rs, :] = nn(jnp.concatenate([near[b, rs] for b in range(BLOCKS)], axis=1), gm[...])

    def input_grad(h):
        hs = slice(h * half, (h + 1) * half)
        for q in range(h * per_half, (h + 1) * per_half):
            peers(lambda s: got(ret.at[q, s], ret_r.at[q, s]))
        for g in range(groups):
            if groups > 1:
                put_selector(g)
            back = half_of(ret, h, slice(g * gd, (g + 1) * gd)).reshape(gs, half)
            for r in range(BLOCKS):
                rs = slice(r * rb, (r + 1) * rb)
                wide[rs, hs] += tn(sel[:, rs], back)
        ig_out[:, hs] = wide[:, hs].astype(bf16)

    def act_on(r):
        piece = act.at[xcol, pl.ds(r * rb, rb)]
        got(piece, ax_r.at[r])
        put(piece, piece, af_s.at[r], af_r.at[r], (me, pair))

    events = []

    def at(when, step, *args):
        events.append((when, len(events), functools.partial(step, *args)))

    unit = 4.0 / depth
    first, *others = [p for p in reversed(range(QUARTERS)) if p != ALONG]
    for k in range(depth):
        last = 2.0 if k == depth - 1 else 0.0
        at(3.1 + 1.4 * unit * k + last, weight_sum, first, k)
        for p in others:
            at(10.5 + 2.8 * unit * k + last, weight_sum, p, k)
    at(12.0, along_own)
    at(14.5, along_across)
    at(17.0, along_share)
    for d in range(1, depth):
        at(12.0 + 2.7 * d, weight_on, first, d)
        at(17.0 + 4.0 * d, along_on, d)
        for p in others:
            at(21.5 + 2.8 * d, weight_on, p, d)
    for r in range(BLOCKS):
        at(2.6 + 5.7 * r, grads_in, r)
        at(25.5 + 5.7 * r, act_on, r)
        at(20.5 + 0.01 * r, near_back, r)
        at(14.3 if r == 0 else 20.3, act_over, r)
    at(20.4, send_back)
    at(36.0, input_grad, 0)
    at(37.0, input_grad, 1)
    for _, _, step in sorted(events, key=lambda event: event[:2]):
        step()

    got(act.at[pair], ac_r.at[0])
    peers(lambda s: got(brecv.at[s], b_r.at[s]))
    brecv[me] = bsend[...]
    bg_out[...] = jnp.sum(brecv[...], axis=0)
    for r in range(BLOCKS):
        got(act.at[dcol, pl.ds(r * rb, rb)], af_r.at[r])
    for p in range(QUARTERS):
        if p != ALONG:
            weight_end(p)
    along_end()

    peers(lambda t: sent(bsend, b_s.at[t]))
    for q in range(QUARTERS):
        peers(lambda t: sent(outg.at[q, t], ret_s.at[q, t]))
    for copy in pending:
        copy.wait_send()


WRITES = 8


def store(act, ig, wg, bg, act_out, ig_out, wg_out, bg_out, wide, some_s, wg_s):
    ncol, part = act.shape[0], act.shape[2]
    copies = []
    for q in range(ncol):
        copies.append(pltpu.make_async_copy(act.at[q], act_out.at[:, q * part : (q + 1) * part], some_s.at[q]))
        copies[-1].start()
    copies.append(pltpu.make_async_copy(ig, ig_out, some_s.at[ncol]))
    copies[-1].start()
    tall = wide.shape[0] // WRITES
    group, quarter = wg.shape[1] // WRITES, wg.shape[3]
    for p in range(WRITES):
        rs = slice(p * tall, (p + 1) * tall)
        for c in range(QUARTERS):
            piece = wg[c, p * group : (p + 1) * group].reshape(tall, quarter)
            wide[rs, c * quarter : (c + 1) * quarter] = piece.astype(f32)
        copies.append(pltpu.make_async_copy(wide.at[rs], wg_out.at[rs], wg_s.at[p]))
        copies[-1].start()
    bg_out[...] = bg[...]
    for copy in copies:
        copy.wait()


def local(
    features, weight, layer_bias, cotangent, self_weight, local_index, local_weight, send_index, remote_slot, remote_weight,
    *, n, ncol,
):
    rows, part = features.shape
    width = weight.shape[0]
    slots = send_index.shape[2]
    half, quarter, rb = part // HALVES, part // QUARTERS, rows // BLOCKS
    gs = min(8, n) * slots
    depth, kb = n // 2, width // n
    edges = local_index.shape[1] + 1 + remote_slot.shape[1]
    vmem = pl.BlockSpec(memory_space=pltpu.VMEM)
    hbm = pl.BlockSpec(memory_space=pl.ANY)
    V = pltpu.VMEM
    S = lambda *shape: pltpu.SemaphoreType.DMA(shape)
    buffers = [
        V((width, part), bf16), V((rows, part), bf16), V((gs, rows), bf16), V((BLOCKS, rows, rb), bf16), V((BLOCKS, gs, rb), bf16),
        V((rows if n <= 8 else rb, gs), bf16),
        V((edges, 8, rows), i32), V((edges, 8, rows), f32),
        V((QUARTERS, n, slots, quarter), bf16), V((QUARTERS, n, slots, quarter), bf16), V((rows, part), f32),
        V((ncol, QUARTERS, rows, quarter), bf16), V((rows, part), bf16),
        V((rows, part), f32), V((rows, part), f32),
        V((BLOCKS, 2, rb, part), bf16), V((BLOCKS, 2, rb, part), bf16), V((BLOCKS, rb, part), bf16), V((BLOCKS, rb, part), bf16),
        V((rows, part), bf16), V((width, part), f32),
        *[V((QUARTERS, depth, kb, quarter), bf16) for _ in range(2)],
        *[V((ALONG, depth, kb, quarter), bf16) for _ in range(3)],
        *[V((depth, 2 * kb, quarter), bf16) for _ in range(3)],
        V((1, part), f32), V((n, 1, part), f32), V((QUARTERS, n, slots, quarter), bf16),
    ]
    semaphores = [
        S(2), S(QUARTERS, n), S(QUARTERS, n), S(2, BLOCKS), S(2, BLOCKS),
        *[S(QUARTERS, BLOCKS) for _ in range(6)],
        S(BLOCKS), S(BLOCKS), S(BLOCKS), S(BLOCKS),
        *[S(QUARTERS, depth) for _ in range(10)],
        S(n), S(n), S(QUARTERS, n), S(QUARTERS, n),
        S(BLOCKS), S(BLOCKS), S(1), S(1), S(BLOCKS), S(BLOCKS),
    ]
    results = pl.pallas_call(
        functools.partial(layer, n=n, ncol=ncol),
        out_shape=(
            V((ncol, rows, part), bf16),
            V((rows, part), bf16),
            V((QUARTERS, n, kb, quarter), bf16),
            V((1, part), f32),
        ),
        in_specs=[vmem, hbm, vmem, hbm, vmem, vmem, vmem, vmem, vmem, vmem],
        out_specs=(vmem,) * 4,
        scratch_shapes=buffers + semaphores,
        compiler_params=pltpu.CompilerParams(
            collective_id=0, has_side_effects=True, vmem_limit_bytes=54 << 20
        ),
        cost_estimate=pl.CostEstimate(flops=11 << 30, bytes_accessed=16 << 20, transcendentals=1 << 20),
    )(
        features, weight, layer_bias, cotangent, self_weight[None, :], local_index.T, local_weight.T,
        send_index[0], remote_slot.T, remote_weight.T,
    )
    output, input_grad, weight_grad, bias_grad = pl.pallas_call(
        store,
        out_shape=(
            jax.ShapeDtypeStruct((rows, ncol * part), bf16),
            jax.ShapeDtypeStruct((rows, part), bf16),
            jax.ShapeDtypeStruct((width, part), f32),
            jax.ShapeDtypeStruct((1, part), f32),
        ),
        in_specs=[vmem] * 4,
        out_specs=(hbm, hbm, hbm, vmem),
        scratch_shapes=[V((width, part), f32), S(ncol + 1), S(WRITES)],
        compiler_params=pltpu.CompilerParams(vmem_limit_bytes=6 << 20),
        cost_estimate=pl.CostEstimate(flops=0, bytes_accessed=10 << 20, transcendentals=0),
    )(*results)
    return output, input_grad, weight_grad, bias_grad[0]


def solution(mesh):
    placed = (
        P("clu", "col"),
        P(None, "col"),
        P("col"),
        P("clu", "col"),
        P("clu"),
        P("clu", None),
        P("clu", None),
        P("clu", None, None),
        P("clu", None),
        P("clu", None),
    )
    return jax.shard_map(
        functools.partial(local, n=mesh.shape["clu"], ncol=mesh.shape["col"]),
        mesh=mesh,
        in_specs=placed,
        out_specs=(P("clu", None), P("clu", "col"), P(None, "col"), P("col")),
        check_vma=False,
    )
```

```python
import functools
import math

import jax
import jax.numpy as jnp
from jax import lax
from jax.experimental import pallas as pl
from jax.experimental.pallas import tpu as pltpu
from jax.sharding import PartitionSpec as P

enhance = 1.0
f32, bf16, i32 = jnp.float32, jnp.bfloat16, jnp.int32
MESH = pl.DeviceIdType.MESH
BLOCKS = 4
HALVES = 2
QUARTERS = 4
ALONG = QUARTERS - 1
TIMES = {"in": (0.5, 3.0, 6.0, 10.0, 13.0, 16.0, 18.5, 21.3), "act": 27.0, "near": 21.6, "over": (18.6, 21.4), "back": (13.2, 21.5), "input": (31.0, 37.0)}
UNROLL = 8
ORDER = (
    (0, 0), (0, 1), (1, 0), (1, 1), (0, 2), (1, 2), (2, 0), (2, 1), (2, 2),
    (3, 0), (0, 3), (3, 1), (1, 3), (3, 2), (2, 3), (3, 3),
)


def tn(a, b):
    return lax.dot_general(a, b, (((0,), (0,)), ((), ())), preferred_element_type=f32)


def nt(a, b):
    return lax.dot_general(a, b, (((1,), (1,)), ((), ())), preferred_element_type=f32)


def nn(a, b):
    return jnp.dot(a, b, preferred_element_type=f32)


def layer(
    feat_in, weight_in, bias_in, cot_in, selfw_in, lidx_in, lwgt_in, send_in, ridx_in, rwgt_in,
    act, ig_out, wfin, bg_out,
    feat, w_v, bias, cot_v, selfw, lidx, lwgt, send, ridx, rwgt, sel, near, far, turned, edge_pos, edge_w, outg, incg, wide, merged, glow, keep_own, keep_far,
    csend, crecv, xsend, xrecv, gm, wacc, ysend, yrecv, zsend, from_before, from_after,
    pair_send, pair_before, pair_after, bsend, brecv, ret,
    load_s, in_s, in_r, tab_s, tab_r, mx_s, mx_r, mc_s, mc_r, mf_s, mf_r, rc_s, rc_r, rx_s, rx_r,
    y_s, y_r, z_s, fb_r, fa_r, zu_s, zd_s, zg_r, yg_s, yg_r, b_s, b_r, ret_s, ret_r, ax_s, ax_r, ac_s, ac_r, af_s, af_r,
    *, n, ncol,
):
    rows, part = feat_in.shape
    half, quarter = part // HALVES, part // QUARTERS
    per_half = QUARTERS // HALVES
    rb = rows // BLOCKS
    slots = send.shape[1]
    gd = min(8, n)
    groups = n // gd
    gs = gd * slots
    depth = n // 2
    kb = wacc.shape[0] // n

    me = lax.axis_index("clu")
    col = lax.axis_index("col")
    zz, yy = lax.div(me, 2), lax.rem(me, 2)
    core = lax.rem(col, 2)
    pair = col + 1 - 2 * core
    xcol = lax.rem(col + ncol // 2, ncol)
    dcol = lax.rem(pair + ncol // 2, ncol)
    ypeer = (me + 1 - 2 * yy, col)
    pending = []

    def start(src, dst, ss, rs, dev):
        copy = pltpu.make_async_remote_copy(
            src_ref=src, dst_ref=dst, send_sem=ss, recv_sem=rs, device_id=dev, device_id_type=MESH
        )
        copy.start()
        return copy

    def put(*args):
        pending.append(start(*args))

    def got(dst, rs):
        pltpu.make_async_remote_copy(
            src_ref=dst, dst_ref=dst, send_sem=rs, recv_sem=rs, device_id=(me, pair), device_id_type=MESH
        ).wait_recv()

    def sent(src, ss):
        pltpu.make_async_remote_copy(
            src_ref=src, dst_ref=src, send_sem=ss, recv_sem=ss, device_id=(me, pair), device_id_type=MESH
        ).wait_send()

    def peers(step):
        def body(k, carry):
            step(lax.rem(me + k, n))
            return carry

        lax.fori_loop(1, n, body, 0)

    loads = [
        pltpu.make_async_copy(src, dst, load_s.at[at])
        for at, (src, dst) in enumerate((
            (send_in, send), (feat_in, feat), (lidx_in, lidx), (lwgt_in, lwgt), (selfw_in, selfw), (ridx_in, ridx),
            (rwgt_in, rwgt), (bias_in, bias), (weight_in, w_v), (cot_in, cot_v),
        ))
    ]
    barrier = pltpu.get_barrier_semaphore()
    peers(lambda t: pl.semaphore_signal(barrier, inc=1, device_id=(t, col), device_id_type=MESH))
    for other in (pair, xcol):
        pl.semaphore_signal(barrier, inc=1, device_id=(me, other), device_id_type=MESH)
    for load in loads:
        load.start()
    for load in loads[:2]:
        load.wait()

    lane = lax.broadcasted_iota(i32, (slots, rows), 1)

    def put_selector(g):
        ids = send[g * gd : (g + 1) * gd, :].T
        for d in range(gd):
            sel[d * slots : (d + 1) * slots, :] = jnp.where(ids[:, d : d + 1] == lane, 1.0, 0.0).astype(bf16)

    def half_of(ref, h, *at):
        return jnp.concatenate([ref[(h * per_half + p, *at)] for p in range(per_half)], axis=-1)

    def in_copy(q, t):
        pltpu.make_async_remote_copy(
            src_ref=outg.at[q, t], dst_ref=incg.at[q, me], send_sem=in_s.at[q, t], recv_sem=in_r.at[q, me],
            device_id=(t, col), device_id_type=MESH,
        ).start()

    for q in range(QUARTERS):
        if q % per_half == 0:
            for g in range(groups):
                if groups > 1 or q == 0:
                    put_selector(g)
                at = q // per_half * half
                rows_out = nn(sel[...], feat[:, at : at + half]).astype(bf16)
                for p in range(per_half):
                    piece = rows_out[:, p * quarter : (p + 1) * quarter].reshape(gd, slots, quarter)
                    outg[q // per_half * per_half + p, g * gd : (g + 1) * gd] = piece
        if q == 0:
            pl.semaphore_wait(barrier, n + 1)
        peers(functools.partial(in_copy, q))
        incg[q, me] = jnp.zeros((slots, quarter), bf16)

    local_edges, far_edges = lidx.shape[0], ridx.shape[0]
    first_far = local_edges + 1

    def put_edges(at, idx, w):
        for k in range(idx.shape[0]):
            edge_pos[at + k] = jnp.broadcast_to(idx[k : k + 1, :], (8, rows))
            edge_w[at + k] = jnp.broadcast_to(w[k : k + 1, :], (8, rows))

    for load in loads[2:7]:
        load.wait()
    put_edges(0, lidx[...], lwgt[...])
    put_edges(local_edges, lax.broadcasted_iota(i32, (1, rows), 1), (1.0 + enhance) * selfw[...])
    put_edges(first_far, ridx[...], rwgt[...])
    sub = lax.broadcasted_iota(i32, (8, 128), 0)

    def table(dst, block, first, count, base, edge_from, edge_to):
        tall = 16 * UNROLL

        def lanes(l, carry):
            ls = pl.ds(pl.multiple_of(l * 128, 128), 128)

            def step(b, carry):
                r0 = first + b * tall
                places = [sub + (base + r0 + 8 * u) for u in range(2 * UNROLL)]
                sums = [jnp.zeros((8, 128), f32)] * (2 * UNROLL)
                for k in range(edge_from, edge_to):
                    at, w = edge_pos[k, :, ls], edge_w[k, :, ls]
                    sums = [s + jnp.where(at == p, w, 0.0) for s, p in zip(sums, places)]
                inner = pl.ds(pl.multiple_of(l * 128 - block * rb, 128), 128)
                dst[block, pl.ds(pl.multiple_of(r0, 16), tall), inner] = jnp.concatenate(sums, 0).astype(bf16)
                return carry

            return lax.fori_loop(0, count // tall, step, carry)

        lax.fori_loop(block * rb // 128, (block + 1) * rb // 128, lanes, 0)

    def shared_part(dst, r, whose):
        count = dst.shape[1] // 2
        return dst.at[r, pl.ds(pl.multiple_of(whose * count, count), count)]

    def shared_table(dst, which, r, edge_from, edge_to):
        count = dst.shape[1] // 2
        table(dst, r, core * count, count, 0, edge_from, edge_to)
        piece = shared_part(dst, r, core)
        put(piece, piece, tab_s.at[which, r], tab_r.at[which, r], (me, pair))

    def far_group(g):
        for r in range(BLOCKS):
            table(far, r, 0, gs, g * gs, first_far, first_far + far_edges)

    def build(r):
        shared_table(near, 0, r, 0, first_far)
        if groups == 1:
            shared_table(far, 1, r, first_far, first_far + far_edges)

    def ready(r):
        rs = slice(r * rb, (r + 1) * rb)
        got(shared_part(near, r, 1 - core), tab_r.at[0, r])
        wide[rs, :] = tn(near[r], feat[...])
        if groups == 1:
            got(shared_part(far, r, 1 - core), tab_r.at[1, r])
            turned[rs, :] = far[r].T

    def arrived(q):
        peers(lambda s: got(incg.at[q, s], in_r.at[q, s]))

    def piece_of(owner, q, r):
        return merged.at[owner, q, pl.ds(r * rb, rb)]

    def aggregate(q, r):
        rs = slice(r * rb, (r + 1) * rb)
        total = wide[rs, q * quarter : (q + 1) * quarter]
        if groups == 1:
            total = total + nn(turned[rs, :], incg[q].reshape(gs, quarter))
        merged[col, q, rs] = total.astype(bf16)
        piece = piece_of(col, q, r)
        put(piece, piece, mx_s.at[q, r], mx_r.at[q, r], (me, xcol))
        put(piece, piece, mc_s.at[q, r], mc_r.at[q, r], (me, pair))

    build(0)
    build(1)
    ready(0)
    if groups > 1:
        for r in range(2, BLOCKS):
            build(r)
        for r in range(1, BLOCKS):
            ready(r)
        for q in range(QUARTERS):
            arrived(q)
        for g in range(groups):
            far_group(g)
            for r in range(BLOCKS):
                rs = slice(r * rb, (r + 1) * rb)
                turned[...] = far[r].T
                for q in range(QUARTERS):
                    pooled = incg[q, g * gd : (g + 1) * gd].reshape(gs, quarter)
                    wide[rs, q * quarter : (q + 1) * quarter] += nn(turned[...], pooled)
        for q, r in ORDER:
            aggregate(q, r)
    else:
        arrived(0)
        aggregate(0, 0)
        ready(1)
        aggregate(0, 1)
        build(2)
        arrived(1)
        aggregate(1, 0)
        aggregate(1, 1)
        ready(2)
        aggregate(0, 2)
        aggregate(1, 2)
        build(3)
        arrived(2)
        for r in range(3):
            aggregate(2, r)
        ready(3)
        arrived(3)
        for q, r in ORDER[9:]:
            aggregate(q, r)

    for load in loads[7:]:
        load.wait()

    def cross(count):
        for q, r in [crossing.pop(0) for _ in range(count)]:
            piece = piece_of(xcol, q, r)
            got(piece, mx_r.at[q, r])
            put(piece, piece, mf_s.at[q, r], mf_r.at[q, r], (me, pair))

    def whole_rows(h, r):
        for q in range(h * per_half, (h + 1) * per_half):
            got(piece_of(pair, q, r), mc_r.at[q, r])
            got(piece_of(dcol, q, r), mf_r.at[q, r])

    crossing = list(ORDER)

    def products(h, r):
        total = None
        for q in range(ncol):
            k0 = q * part + h * half
            term = nn(half_of(merged.at[q], h, slice(r * rb, (r + 1) * rb)), w_v[k0 : k0 + half, :])
            total = term if total is None else total + term
        return total

    def first_half(r):
        whole_rows(0, r)
        wide[r * rb : (r + 1) * rb, :] = products(0, r) + bias[...].astype(f32).reshape(1, part)

    def second_half(r):
        whole_rows(1, r)
        wide[r * rb : (r + 1) * rb, :] += products(1, r)

    tall = 32

    def smooth(r, total):
        def step(b, total):
            rs = pl.ds(pl.multiple_of(r * rb + b * tall, tall), tall)
            v = wide[rs, :]
            cdf = 0.5 + 0.5 * lax.erf(v * (1.0 / math.sqrt(2.0)))
            act[col, rs, :] = (v * cdf).astype(bf16)
            density = jnp.exp(v * v * -0.5) * (1.0 / math.sqrt(2.0 * math.pi))
            low = (cot_v[rs, :].astype(f32) * (cdf + v * density)).astype(bf16)
            glow[rs, :] = low
            return total + jnp.sum(low.astype(f32).reshape(tall // 8, 8, part), axis=0)

        return lax.fori_loop(0, rb // tall, step, total)

    def grads(r):
        rs = slice(r * rb, (r + 1) * rb)
        low = glow[rs, :]

        def term(q):
            return nt(low, w_v[pl.ds(pl.multiple_of(q * part, part), part), :])

        csend[r, 0] = term(pair).astype(bf16)
        csend[r, 1] = term(dcol).astype(bf16)
        put(csend.at[r], crecv.at[r], rc_s.at[r], rc_r.at[r], (me, pair))
        keep_own[rs, :] = term(col)
        keep_far[rs, :] = term(xcol)

    def grads_over(r):
        rs = slice(r * rb, (r + 1) * rb)
        got(crecv.at[r], rc_r.at[r])
        both_halves = (keep_far[rs, :] + crecv[r, 1].astype(f32)).astype(bf16)
        for h in range(HALVES):
            xsend[h, r] = both_halves[:, h * half : (h + 1) * half]
        grads_cross(0, r)
        keep_own[rs, :] += crecv[r, 0].astype(f32)

    def grads_cross(h, r):
        put(xsend.at[h, r], xrecv.at[h, r], rx_s.at[h, r], rx_r.at[h, r], (me, xcol))

    def grads_in(h, r):
        rs, hs = slice(r * rb, (r + 1) * rb), slice(h * half, (h + 1) * half)
        got(xrecv.at[h, r], rx_r.at[h, r])
        gm[rs, hs] = (keep_own[rs, hs] + xrecv[h, r].astype(f32)).astype(bf16)

    total = jnp.zeros((8, part), f32)
    cross(4)
    first_half(0)
    cross(2)
    first_half(1)
    cross(3)
    first_half(2)
    cross(2)
    second_half(0)
    total = smooth(0, total)
    cross(2)
    grads(0)
    second_half(1)
    total = smooth(1, total)
    first_half(3)
    cross(2)
    grads_over(0)
    grads_cross(1, 0)
    grads(1)
    cross(1)
    second_half(2)
    total = smooth(2, total)
    second_half(3)
    total = smooth(3, total)

    bsend[...] = jnp.sum(total, axis=0, keepdims=True)

    def cols(p):
        return slice(p * quarter, (p + 1) * quarter)

    fine = kb == half
    if not fine:
        for chunk in range(ncol * HALVES):
            rows_in = half_of(merged.at[chunk // HALVES], chunk % HALVES)
            wacc[chunk * half : (chunk + 1) * half, :] = tn(rows_in, glow[...])

    def block_rows(b, count=1):
        return pl.ds(pl.multiple_of(b * kb, kb), count * kb)

    def weight_chunk(b, h):
        hs = slice(h * half, (h + 1) * half)
        if not fine:
            return wacc[block_rows(b), hs]
        q, at = lax.div(b, HALVES), lax.rem(b, HALVES) * per_half
        rows_in = jnp.concatenate([merged[q, at + p] for p in range(per_half)], axis=1)
        return tn(rows_in, glow[:, hs])

    low = zz < depth // 2
    ahead = jnp.where(low, depth - 1 - zz, zz)

    def place(k):
        up = jnp.where(k < ahead, depth - 1 - k, k - ahead)
        return jnp.where(low, up, depth - 1 - up)

    def weight_out(h, k):
        z = place(k)
        theirs, mine = z * 2 + 1 - yy, z * 2 + yy
        term = weight_chunk(theirs, h)
        for p in range(h * per_half, (h + 1) * per_half):
            piece = term[:, (p - h * per_half) * quarter : (p - h * per_half + 1) * quarter]
            if p == ALONG:
                wacc[block_rows(theirs), cols(p)] = piece
            else:
                ysend[p, z] = piece.astype(bf16)
                put(ysend.at[p, z], yrecv.at[p, z], y_s.at[p, z], y_r.at[p, z], ypeer)
        if fine:
            wacc[block_rows(mine), h * half : (h + 1) * half] = weight_chunk(mine, h)

    before, after = me - 2, me + 2

    def line_sum(p, z, total, out, came_before, came_after):
        out[z] = total.astype(bf16)

        @pl.when(z > zz)
        def _():
            @pl.when(zz > 0)
            def _():
                got(came_before.at[z], fb_r.at[p, z])
                out[z] = (total + came_before[z].astype(f32)).astype(bf16)

            start(out.at[z], came_before.at[z], z_s.at[p, z], fb_r.at[p, z], (after, col))

        @pl.when(z < zz)
        def _():
            @pl.when(zz < depth - 1)
            def _():
                got(came_after.at[z], fa_r.at[p, z])
                out[z] = (total + came_after[z].astype(f32)).astype(bf16)

            start(out.at[z], came_after.at[z], z_s.at[p, z], fa_r.at[p, z], (before, col))

    def line_end(p, rows_in, came_before, came_after):
        @pl.when(zz > 0)
        def _():
            got(came_before.at[zz], fb_r.at[p, zz])
            wacc[rows_in, cols(p)] += came_before[zz].astype(f32)

        @pl.when(zz < depth - 1)
        def _():
            got(came_after.at[zz], fa_r.at[p, zz])
            wacc[rows_in, cols(p)] += came_after[zz].astype(f32)

    def line_share(p, z, block, up=True, down=True):
        if up:
            @pl.when(zz < depth - 1)
            def _():
                start(block, block, zu_s.at[p, z], zg_r.at[p, z], (after, col))
        if down:
            @pl.when(zz > 0)
            def _():
                start(block, block, zd_s.at[p, z], zg_r.at[p, z], (before, col))

    def sent_line(p, z, out, block):
        @pl.when(z != zz)
        def _():
            sent(out.at[z], z_s.at[p, z])

        @pl.when((z <= zz) & (zz < depth - 1))
        def _():
            sent(block, zu_s.at[p, z])

        @pl.when((z >= zz) & (zz > 0))
        def _():
            sent(block, zd_s.at[p, z])

    def weight_sum(p, k):
        z = place(k)
        got(yrecv.at[p, z], y_r.at[p, z])
        rows_in = block_rows(z * 2 + yy)
        total = wacc[rows_in, cols(p)] + yrecv[p, z].astype(f32)
        if k < depth - 1:
            line_sum(p, z, total, zsend.at[p], from_before.at[p], from_after.at[p])
            return
        wacc[rows_in, cols(p)] = total
        line_end(p, rows_in, from_before.at[p], from_after.at[p])
        wfin[p, me] = wacc[rows_in, cols(p)].astype(bf16)
        line_share(p, zz, wfin.at[p, me])
        across(p, zz)

    def across(p, z):
        block = wfin.at[p, z * 2 + yy]
        start(block, block, yg_s.at[p, z], yg_r.at[p, z], ypeer)

    def weight_on(p, d):
        @pl.when(zz >= d)
        def _():
            block = wfin.at[p, me - 2 * d]
            got(block, zg_r.at[p, zz - d])
            line_share(p, zz - d, block, down=False)
            across(p, zz - d)

        @pl.when(zz + d < depth)
        def _():
            block = wfin.at[p, me + 2 * d]
            got(block, zg_r.at[p, zz + d])
            line_share(p, zz + d, block, up=False)
            across(p, zz + d)

    def weight_end(p):
        for z in range(depth):
            got(wfin.at[p, z * 2 + 1 - yy], yg_r.at[p, z])
            sent(wfin.at[p, z * 2 + yy], yg_s.at[p, z])
            sent_line(p, z, zsend.at[p], wfin.at[p, z * 2 + yy])

    def both(z):
        return wfin.at[ALONG, pl.ds(z * 2, 2)]

    def along_sum(k):
        z = place(k)
        total = wacc[block_rows(z * 2, 2), cols(ALONG)]
        line_sum(ALONG, z, total, pair_send, pair_before, pair_after)

    end = (zz == 0) | (zz == depth - 1)

    def along_from_end(k):
        @pl.when(end)
        def _():
            along_sum(k)

    def along_inside(k):
        @pl.when(jnp.logical_not(end))
        def _():
            along_sum(k)

    def along_own():
        line_end(ALONG, block_rows(zz * 2, 2), pair_before, pair_after)
        ysend[ALONG, zz] = wacc[block_rows(zz * 2 + 1 - yy), cols(ALONG)].astype(bf16)
        put(ysend.at[ALONG, zz], yrecv.at[ALONG, zz], y_s.at[ALONG, zz], y_r.at[ALONG, zz], ypeer)

    def along_across():
        got(yrecv.at[ALONG, zz], y_r.at[ALONG, zz])
        total = wacc[block_rows(me), cols(ALONG)] + yrecv[ALONG, zz].astype(f32)
        wfin[ALONG, me] = total.astype(bf16)
        across(ALONG, zz)

    def along_share():
        got(wfin.at[ALONG, zz * 2 + 1 - yy], yg_r.at[ALONG, zz])
        line_share(ALONG, zz, both(zz))

    def along_on(d):
        @pl.when(zz >= d)
        def _():
            got(both(zz - d), zg_r.at[ALONG, zz - d])
            line_share(ALONG, zz - d, both(zz - d), down=False)

        @pl.when(zz + d < depth)
        def _():
            got(both(zz + d), zg_r.at[ALONG, zz + d])
            line_share(ALONG, zz + d, both(zz + d), up=False)

    def along_end():
        sent(wfin.at[ALONG, me], yg_s.at[ALONG, zz])
        for z in range(depth):
            sent_line(ALONG, z, pair_send, both(z))

    def out_along(k):
        weight_out(HALVES - 1, k)
        if k < depth - 1:
            along_from_end(k)

    out_along(0)
    out_along(1)
    grads_over(1)
    grads(2)
    for k in range(2, depth):
        out_along(k)
    weight_out(0, 0)
    grads_over(2)
    grads(3)
    along_inside(0)
    weight_out(0, 1)
    grads_over(3)
    for r in range(1, BLOCKS):
        grads_cross(1, r)
    for k in range(1, depth - 2):
        along_inside(k)
    for k in range(2, depth):
        weight_out(0, k)
    if depth > 2:
        along_inside(depth - 2)

    def bias_copy(t):
        pltpu.make_async_remote_copy(
            src_ref=bsend, dst_ref=brecv.at[me], send_sem=b_s.at[t], recv_sem=b_r.at[me],
            device_id=(t, col), device_id_type=MESH,
        ).start()

    peers(bias_copy)

    def act_over(r):
        piece = act.at[col, pl.ds(r * rb, rb)]
        put(piece, piece, ax_s.at[r], ax_r.at[r], (me, xcol))

    own_act = act.at[col]
    put(own_act, own_act, ac_s.at[0], ac_r.at[0], (me, pair))

    def back_copy(q, t):
        pltpu.make_async_remote_copy(
            src_ref=outg.at[q, t], dst_ref=ret.at[q, me],
            send_sem=ret_s.at[q, t], recv_sem=ret_r.at[q, me], device_id=(t, col), device_id_type=MESH,
        ).start()

    def send_back(h):
        quarters = range(h * per_half, (h + 1) * per_half)
        for q in quarters:
            peers(lambda t: sent(outg.at[q, t], in_s.at[q, t]))
        for g in range(groups):
            if groups > 1:
                far_group(g)
            whole = jnp.concatenate([far[r] for r in range(BLOCKS)], axis=1)
            pool_grad = nn(whole, gm[:, h * half : (h + 1) * half]).astype(bf16)
            for i, q in enumerate(quarters):
                piece = pool_grad[:, i * quarter : (i + 1) * quarter]
                outg[q, g * gd : (g + 1) * gd] = piece.reshape(gd, slots, quarter)
        for q in quarters:
            peers(functools.partial(back_copy, q))
            ret[q, me] = jnp.zeros((slots, quarter), bf16)

    def near_back(r):
        rs = slice(r * rb, (r + 1) * rb)
        wide[rs, :] = nn(jnp.concatenate([near[b, rs] for b in range(BLOCKS)], axis=1), gm[...])

    def input_grad(h):
        hs = slice(h * half, (h + 1) * half)
        for q in range(h * per_half, (h + 1) * per_half):
            peers(lambda s: got(ret.at[q, s], ret_r.at[q, s]))
        for g in range(groups):
            if groups > 1:
                put_selector(g)
            back = half_of(ret, h, slice(g * gd, (g + 1) * gd)).reshape(gs, half)
            for r in range(BLOCKS):
                rs = slice(r * rb, (r + 1) * rb)
                wide[rs, hs] += tn(sel[:, rs], back)
        ig_out[:, hs] = wide[:, hs].astype(bf16)

    def act_on(r):
        piece = act.at[xcol, pl.ds(r * rb, rb)]
        got(piece, ax_r.at[r])
        put(piece, piece, af_s.at[r], af_r.at[r], (me, pair))

    events = []

    def at(when, step, *args):
        events.append((when, len(events), functools.partial(step, *args)))

    unit = 4.0 / depth
    first, *others = [p for p in reversed(range(QUARTERS)) if p != ALONG]
    for k in range(depth):
        last = 2.0 if k == depth - 1 else 0.0
        at(3.1 + 1.4 * unit * k + last, weight_sum, first, k)
        for p in others:
            at(10.5 + 2.8 * unit * k + last, weight_sum, p, k)
    at(12.0, along_own)
    at(14.5, along_across)
    at(17.0, along_share)
    for d in range(1, depth):
        at(12.0 + 2.7 * d, weight_on, first, d)
        at(17.0 + 4.0 * d, along_on, d)
        for p in others:
            at(21.5 + 2.8 * d, weight_on, p, d)
    crossed = ((0, 0), (1, 0), (0, 1), (0, 2), (0, 3), (1, 1), (1, 2), (1, 3))
    for when, (h, r) in zip(TIMES["in"], crossed):
        at(when, grads_in, h, r)
    for r in range(BLOCKS):
        at(TIMES["act"] + 5.7 * r, act_on, r)
        at(TIMES["near"] + 0.01 * r, near_back, r)
        at(TIMES["over"][0 if r == 0 else 1], act_over, r)
    for h in range(HALVES):
        at(TIMES["back"][h], send_back, h)
        at(TIMES["input"][h], input_grad, h)
    for _, _, step in sorted(events, key=lambda event: event[:2]):
        step()

    got(act.at[pair], ac_r.at[0])
    peers(lambda s: got(brecv.at[s], b_r.at[s]))
    brecv[me] = bsend[...]
    bg_out[...] = jnp.sum(brecv[...], axis=0)
    for r in range(BLOCKS):
        got(act.at[dcol, pl.ds(r * rb, rb)], af_r.at[r])
    for p in range(QUARTERS):
        if p != ALONG:
            weight_end(p)
    along_end()

    peers(lambda t: sent(bsend, b_s.at[t]))
    for q in range(QUARTERS):
        peers(lambda t: sent(outg.at[q, t], ret_s.at[q, t]))
    for copy in pending:
        copy.wait_send()


WRITES = 8


def store(act, ig, wg, bg, act_out, ig_out, wg_out, bg_out, wide, some_s, wg_s):
    ncol, part = act.shape[0], act.shape[2]
    copies = []
    for q in range(ncol):
        copies.append(pltpu.make_async_copy(act.at[q], act_out.at[:, q * part : (q + 1) * part], some_s.at[q]))
        copies[-1].start()
    copies.append(pltpu.make_async_copy(ig, ig_out, some_s.at[ncol]))
    copies[-1].start()
    tall = wide.shape[0] // WRITES
    group, quarter = wg.shape[1] // WRITES, wg.shape[3]
    for p in range(WRITES):
        rs = slice(p * tall, (p + 1) * tall)
        for c in range(QUARTERS):
            piece = wg[c, p * group : (p + 1) * group].reshape(tall, quarter)
            wide[rs, c * quarter : (c + 1) * quarter] = piece.astype(f32)
        copies.append(pltpu.make_async_copy(wide.at[rs], wg_out.at[rs], wg_s.at[p]))
        copies[-1].start()
    bg_out[...] = bg[...]
    for copy in copies:
        copy.wait()


def local(
    features, weight, layer_bias, cotangent, self_weight, local_index, local_weight, send_index, remote_slot, remote_weight,
    *, n, ncol,
):
    rows, part = features.shape
    width = weight.shape[0]
    slots = send_index.shape[2]
    half, quarter, rb = part // HALVES, part // QUARTERS, rows // BLOCKS
    gs = min(8, n) * slots
    depth, kb = n // 2, width // n
    edges_near, edges_far = local_index.shape[1], remote_slot.shape[1]
    edges = edges_near + 1 + edges_far
    vmem = pl.BlockSpec(memory_space=pltpu.VMEM)
    hbm = pl.BlockSpec(memory_space=pl.ANY)
    V = pltpu.VMEM
    S = lambda *shape: pltpu.SemaphoreType.DMA(shape)
    buffers = [
        V((rows, part), bf16), V((width, part), bf16), V((part,), bf16), V((rows, part), bf16), V((1, rows), f32),
        V((edges_near, rows), i32), V((edges_near, rows), f32), V((n, slots), i32), V((edges_far, rows), i32), V((edges_far, rows), f32),
        V((gs, rows), bf16), V((BLOCKS, rows, rb), bf16), V((BLOCKS, gs, rb), bf16),
        V((rows if n <= 8 else rb, gs), bf16),
        V((edges, 8, rows), i32), V((edges, 8, rows), f32),
        V((QUARTERS, n, slots, quarter), bf16), V((QUARTERS, n, slots, quarter), bf16), V((rows, part), f32),
        V((ncol, QUARTERS, rows, quarter), bf16), V((rows, part), bf16),
        V((rows, part), f32), V((rows, part), f32),
        V((BLOCKS, 2, rb, part), bf16), V((BLOCKS, 2, rb, part), bf16), *[V((HALVES, BLOCKS, rb, half), bf16) for _ in range(2)],
        V((rows, part), bf16), V((width, part), f32),
        *[V((QUARTERS, depth, kb, quarter), bf16) for _ in range(2)],
        *[V((ALONG, depth, kb, quarter), bf16) for _ in range(3)],
        *[V((depth, 2 * kb, quarter), bf16) for _ in range(3)],
        V((1, part), f32), V((n, 1, part), f32), V((QUARTERS, n, slots, quarter), bf16),
    ]
    semaphores = [
        S(10), S(QUARTERS, n), S(QUARTERS, n), S(2, BLOCKS), S(2, BLOCKS),
        *[S(QUARTERS, BLOCKS) for _ in range(6)],
        S(BLOCKS), S(BLOCKS), S(HALVES, BLOCKS), S(HALVES, BLOCKS),
        *[S(QUARTERS, depth) for _ in range(10)],
        S(n), S(n), S(QUARTERS, n), S(QUARTERS, n),
        S(BLOCKS), S(BLOCKS), S(1), S(1), S(BLOCKS), S(BLOCKS),
    ]
    results = pl.pallas_call(
        functools.partial(layer, n=n, ncol=ncol),
        out_shape=(
            V((ncol, rows, part), bf16),
            V((rows, part), bf16),
            V((QUARTERS, n, kb, quarter), bf16),
            V((1, part), f32),
        ),
        in_specs=[hbm] * 10,
        out_specs=(vmem,) * 4,
        scratch_shapes=buffers + semaphores,
        compiler_params=pltpu.CompilerParams(
            collective_id=0, has_side_effects=True, vmem_limit_bytes=54 << 20
        ),
        cost_estimate=pl.CostEstimate(flops=11 << 30, bytes_accessed=16 << 20, transcendentals=1 << 20),
    )(
        features, weight, layer_bias, cotangent, self_weight[None, :], local_index.T, local_weight.T,
        send_index[0], remote_slot.T, remote_weight.T,
    )
    output, input_grad, weight_grad, bias_grad = pl.pallas_call(
        store,
        out_shape=(
            jax.ShapeDtypeStruct((rows, ncol * part), bf16),
            jax.ShapeDtypeStruct((rows, part), bf16),
            jax.ShapeDtypeStruct((width, part), f32),
            jax.ShapeDtypeStruct((1, part), f32),
        ),
        in_specs=[vmem] * 4,
        out_specs=(hbm, hbm, hbm, vmem),
        scratch_shapes=[V((width, part), f32), S(ncol + 1), S(WRITES)],
        compiler_params=pltpu.CompilerParams(vmem_limit_bytes=6 << 20),
        cost_estimate=pl.CostEstimate(flops=0, bytes_accessed=10 << 20, transcendentals=0),
    )(*results)
    return output, input_grad, weight_grad, bias_grad[0]


def solution(mesh):
    placed = (
        P("clu", "col"),
        P(None, "col"),
        P("col"),
        P("clu", "col"),
        P("clu"),
        P("clu", None),
        P("clu", None),
        P("clu", None, None),
        P("clu", None),
        P("clu", None),
    )
    return jax.shard_map(
        functools.partial(local, n=mesh.shape["clu"], ncol=mesh.shape["col"]),
        mesh=mesh,
        in_specs=placed,
        out_specs=(P("clu", None), P("clu", "col"), P(None, "col"), P("col")),
        check_vma=False,
    )
```

```python
import functools
import math

import jax
import jax.numpy as jnp
from jax import lax
from jax.experimental import pallas as pl
from jax.experimental.pallas import tpu as pltpu
from jax.sharding import PartitionSpec as P

enhance = 1.0
f32, bf16, i32 = jnp.float32, jnp.bfloat16, jnp.int32
MESH = pl.DeviceIdType.MESH
BLOCKS = 4
HALVES = 2
QUARTERS = 4
PIECES = (3, 2, 1, 0)
TIMES = {"sum": 3.8, "own": 2.0, "on": 17.5, "hop": 3.3, "in": (0.5, 3.0, 6.0, 10.0, 13.0, 16.0, 18.5, 21.3), "act": 27.0, "near": 21.6, "over": (18.6, 21.4), "back": (13.2, 21.5), "input": (31.0, 37.0)}
UNROLL = 8
ORDER = (
    (0, 0), (0, 1), (1, 0), (1, 1), (0, 2), (1, 2), (2, 0), (2, 1), (2, 2),
    (3, 0), (0, 3), (3, 1), (1, 3), (3, 2), (2, 3), (3, 3),
)


def tn(a, b):
    return lax.dot_general(a, b, (((0,), (0,)), ((), ())), preferred_element_type=f32)


def nt(a, b):
    return lax.dot_general(a, b, (((1,), (1,)), ((), ())), preferred_element_type=f32)


def nn(a, b):
    return jnp.dot(a, b, preferred_element_type=f32)


def layer(
    feat_in, weight_in, bias_in, cot_in, selfw_in, lidx_in, lwgt_in, send_in, ridx_in, rwgt_in,
    act, ig_out, wfin, bg_out,
    feat, w_v, bias, cot_v, selfw, lidx, lwgt, send, ridx, rwgt, sel, near, far, turned, edge_pos, edge_w, outg, incg, wide, merged, glow, keep_own, keep_far,
    csend, crecv, xsend, xrecv, gm, wacc, ysend, yrecv, zsend, from_before, from_after, bsend, brecv, ret,
    load_s, in_s, in_r, tab_s, tab_r, mx_s, mx_r, mc_s, mc_r, mf_s, mf_r, rc_s, rc_r, rx_s, rx_r,
    y_s, y_r, z_s, fb_r, fa_r, zu_s, zd_s, zg_r, yg_s, yg_r, b_s, b_r, ret_s, ret_r, ax_s, ax_r, ac_s, ac_r, af_s, af_r,
    *, n, ncol,
):
    rows, part = feat_in.shape
    half, quarter = part // HALVES, part // QUARTERS
    per_half = QUARTERS // HALVES
    rb = rows // BLOCKS
    slots = send.shape[1]
    gd = min(8, n)
    groups = n // gd
    gs = gd * slots
    depth = n // 2
    kb = wacc.shape[0] // n

    me = lax.axis_index("clu")
    col = lax.axis_index("col")
    zz, yy = lax.div(me, 2), lax.rem(me, 2)
    core = lax.rem(col, 2)
    pair = col + 1 - 2 * core
    xcol = lax.rem(col + ncol // 2, ncol)
    dcol = lax.rem(pair + ncol // 2, ncol)
    ypeer = (me + 1 - 2 * yy, col)
    pending = []

    def start(src, dst, ss, rs, dev):
        copy = pltpu.make_async_remote_copy(
            src_ref=src, dst_ref=dst, send_sem=ss, recv_sem=rs, device_id=dev, device_id_type=MESH
        )
        copy.start()
        return copy

    def put(*args):
        pending.append(start(*args))

    def got(dst, rs):
        pltpu.make_async_remote_copy(
            src_ref=dst, dst_ref=dst, send_sem=rs, recv_sem=rs, device_id=(me, pair), device_id_type=MESH
        ).wait_recv()

    def sent(src, ss):
        pltpu.make_async_remote_copy(
            src_ref=src, dst_ref=src, send_sem=ss, recv_sem=ss, device_id=(me, pair), device_id_type=MESH
        ).wait_send()

    def peers(step):
        def body(k, carry):
            step(lax.rem(me + k, n))
            return carry

        lax.fori_loop(1, n, body, 0)

    loads = [
        pltpu.make_async_copy(src, dst, load_s.at[at])
        for at, (src, dst) in enumerate((
            (send_in, send), (feat_in, feat), (lidx_in, lidx), (lwgt_in, lwgt), (selfw_in, selfw), (ridx_in, ridx),
            (rwgt_in, rwgt), (bias_in, bias), (weight_in, w_v), (cot_in, cot_v),
        ))
    ]
    barrier = pltpu.get_barrier_semaphore()
    peers(lambda t: pl.semaphore_signal(barrier, inc=1, device_id=(t, col), device_id_type=MESH))
    for other in (pair, xcol):
        pl.semaphore_signal(barrier, inc=1, device_id=(me, other), device_id_type=MESH)
    for load in loads:
        load.start()
    for load in loads[:2]:
        load.wait()

    lane = lax.broadcasted_iota(i32, (slots, rows), 1)

    def put_selector(g):
        ids = send[g * gd : (g + 1) * gd, :].T
        for d in range(gd):
            sel[d * slots : (d + 1) * slots, :] = jnp.where(ids[:, d : d + 1] == lane, 1.0, 0.0).astype(bf16)

    def half_of(ref, h, *at):
        return jnp.concatenate([ref[(h * per_half + p, *at)] for p in range(per_half)], axis=-1)

    def in_copy(q, t):
        pltpu.make_async_remote_copy(
            src_ref=outg.at[q, t], dst_ref=incg.at[q, me], send_sem=in_s.at[q, t], recv_sem=in_r.at[q, me],
            device_id=(t, col), device_id_type=MESH,
        ).start()

    for q in range(QUARTERS):
        if q % per_half == 0:
            for g in range(groups):
                if groups > 1 or q == 0:
                    put_selector(g)
                at = q // per_half * half
                rows_out = nn(sel[...], feat[:, at : at + half]).astype(bf16)
                for p in range(per_half):
                    piece = rows_out[:, p * quarter : (p + 1) * quarter].reshape(gd, slots, quarter)
                    outg[q // per_half * per_half + p, g * gd : (g + 1) * gd] = piece
        if q == 0:
            pl.semaphore_wait(barrier, n + 1)
        peers(functools.partial(in_copy, q))
        incg[q, me] = jnp.zeros((slots, quarter), bf16)

    local_edges, far_edges = lidx.shape[0], ridx.shape[0]
    first_far = local_edges + 1

    def put_edges(at, idx, w):
        for k in range(idx.shape[0]):
            edge_pos[at + k] = jnp.broadcast_to(idx[k : k + 1, :], (8, rows))
            edge_w[at + k] = jnp.broadcast_to(w[k : k + 1, :], (8, rows))

    for load in loads[2:7]:
        load.wait()
    put_edges(0, lidx[...], lwgt[...])
    put_edges(local_edges, lax.broadcasted_iota(i32, (1, rows), 1), (1.0 + enhance) * selfw[...])
    put_edges(first_far, ridx[...], rwgt[...])
    sub = lax.broadcasted_iota(i32, (8, 128), 0)

    def table(dst, block, first, count, base, edge_from, edge_to):
        tall = 16 * UNROLL

        def lanes(l, carry):
            ls = pl.ds(pl.multiple_of(l * 128, 128), 128)

            def step(b, carry):
                r0 = first + b * tall
                places = [sub + (base + r0 + 8 * u) for u in range(2 * UNROLL)]
                sums = [jnp.zeros((8, 128), f32)] * (2 * UNROLL)
                for k in range(edge_from, edge_to):
                    at, w = edge_pos[k, :, ls], edge_w[k, :, ls]
                    sums = [s + jnp.where(at == p, w, 0.0) for s, p in zip(sums, places)]
                inner = pl.ds(pl.multiple_of(l * 128 - block * rb, 128), 128)
                dst[block, pl.ds(pl.multiple_of(r0, 16), tall), inner] = jnp.concatenate(sums, 0).astype(bf16)
                return carry

            return lax.fori_loop(0, count // tall, step, carry)

        lax.fori_loop(block * rb // 128, (block + 1) * rb // 128, lanes, 0)

    def shared_part(dst, r, whose):
        count = dst.shape[1] // 2
        return dst.at[r, pl.ds(pl.multiple_of(whose * count, count), count)]

    def shared_table(dst, which, r, edge_from, edge_to):
        count = dst.shape[1] // 2
        table(dst, r, core * count, count, 0, edge_from, edge_to)
        piece = shared_part(dst, r, core)
        put(piece, piece, tab_s.at[which, r], tab_r.at[which, r], (me, pair))

    def far_group(g):
        for r in range(BLOCKS):
            table(far, r, 0, gs, g * gs, first_far, first_far + far_edges)

    def build(r):
        shared_table(near, 0, r, 0, first_far)
        if groups == 1:
            shared_table(far, 1, r, first_far, first_far + far_edges)

    def ready(r):
        rs = slice(r * rb, (r + 1) * rb)
        got(shared_part(near, r, 1 - core), tab_r.at[0, r])
        wide[rs, :] = tn(near[r], feat[...])
        if groups == 1:
            got(shared_part(far, r, 1 - core), tab_r.at[1, r])
            turned[rs, :] = far[r].T

    def arrived(q):
        peers(lambda s: got(incg.at[q, s], in_r.at[q, s]))

    def piece_of(owner, q, r):
        return merged.at[owner, q, pl.ds(r * rb, rb)]

    def aggregate(q, r):
        rs = slice(r * rb, (r + 1) * rb)
        total = wide[rs, q * quarter : (q + 1) * quarter]
        if groups == 1:
            total = total + nn(turned[rs, :], incg[q].reshape(gs, quarter))
        merged[col, q, rs] = total.astype(bf16)
        piece = piece_of(col, q, r)
        put(piece, piece, mx_s.at[q, r], mx_r.at[q, r], (me, xcol))
        put(piece, piece, mc_s.at[q, r], mc_r.at[q, r], (me, pair))

    build(0)
    build(1)
    ready(0)
    if groups > 1:
        for r in range(2, BLOCKS):
            build(r)
        for r in range(1, BLOCKS):
            ready(r)
        for q in range(QUARTERS):
            arrived(q)
        for g in range(groups):
            far_group(g)
            for r in range(BLOCKS):
                rs = slice(r * rb, (r + 1) * rb)
                turned[...] = far[r].T
                for q in range(QUARTERS):
                    pooled = incg[q, g * gd : (g + 1) * gd].reshape(gs, quarter)
                    wide[rs, q * quarter : (q + 1) * quarter] += nn(turned[...], pooled)
        for q, r in ORDER:
            aggregate(q, r)
    else:
        arrived(0)
        aggregate(0, 0)
        ready(1)
        aggregate(0, 1)
        build(2)
        arrived(1)
        aggregate(1, 0)
        aggregate(1, 1)
        ready(2)
        aggregate(0, 2)
        aggregate(1, 2)
        build(3)
        arrived(2)
        for r in range(3):
            aggregate(2, r)
        ready(3)
        arrived(3)
        for q, r in ORDER[9:]:
            aggregate(q, r)

    for load in loads[7:]:
        load.wait()

    def cross(count):
        for q, r in [crossing.pop(0) for _ in range(count)]:
            piece = piece_of(xcol, q, r)
            got(piece, mx_r.at[q, r])
            put(piece, piece, mf_s.at[q, r], mf_r.at[q, r], (me, pair))

    def whole_rows(h, r):
        for q in range(h * per_half, (h + 1) * per_half):
            got(piece_of(pair, q, r), mc_r.at[q, r])
            got(piece_of(dcol, q, r), mf_r.at[q, r])

    crossing = list(ORDER)

    def products(h, r):
        total = None
        for q in range(ncol):
            k0 = q * part + h * half
            term = nn(half_of(merged.at[q], h, slice(r * rb, (r + 1) * rb)), w_v[k0 : k0 + half, :])
            total = term if total is None else total + term
        return total

    def first_half(r):
        whole_rows(0, r)
        wide[r * rb : (r + 1) * rb, :] = products(0, r) + bias[...].astype(f32).reshape(1, part)

    def second_half(r):
        whole_rows(1, r)
        wide[r * rb : (r + 1) * rb, :] += products(1, r)

    tall = 32

    def smooth(r, total):
        def step(b, total):
            rs = pl.ds(pl.multiple_of(r * rb + b * tall, tall), tall)
            v = wide[rs, :]
            cdf = 0.5 + 0.5 * lax.erf(v * (1.0 / math.sqrt(2.0)))
            act[col, rs, :] = (v * cdf).astype(bf16)
            density = jnp.exp(v * v * -0.5) * (1.0 / math.sqrt(2.0 * math.pi))
            low = (cot_v[rs, :].astype(f32) * (cdf + v * density)).astype(bf16)
            glow[rs, :] = low
            return total + jnp.sum(low.astype(f32).reshape(tall // 8, 8, part), axis=0)

        return lax.fori_loop(0, rb // tall, step, total)

    def grads(r):
        rs = slice(r * rb, (r + 1) * rb)
        low = glow[rs, :]

        def term(q):
            return nt(low, w_v[pl.ds(pl.multiple_of(q * part, part), part), :])

        csend[r, 0] = term(pair).astype(bf16)
        csend[r, 1] = term(dcol).astype(bf16)
        put(csend.at[r], crecv.at[r], rc_s.at[r], rc_r.at[r], (me, pair))
        keep_own[rs, :] = term(col)
        keep_far[rs, :] = term(xcol)

    def grads_over(r):
        rs = slice(r * rb, (r + 1) * rb)
        got(crecv.at[r], rc_r.at[r])
        both_halves = (keep_far[rs, :] + crecv[r, 1].astype(f32)).astype(bf16)
        for h in range(HALVES):
            xsend[h, r] = both_halves[:, h * half : (h + 1) * half]
        grads_cross(0, r)
        keep_own[rs, :] += crecv[r, 0].astype(f32)

    def grads_cross(h, r):
        put(xsend.at[h, r], xrecv.at[h, r], rx_s.at[h, r], rx_r.at[h, r], (me, xcol))

    def grads_in(h, r):
        rs, hs = slice(r * rb, (r + 1) * rb), slice(h * half, (h + 1) * half)
        got(xrecv.at[h, r], rx_r.at[h, r])
        gm[rs, hs] = (keep_own[rs, hs] + xrecv[h, r].astype(f32)).astype(bf16)

    total = jnp.zeros((8, part), f32)
    cross(4)
    first_half(0)
    cross(2)
    first_half(1)
    cross(3)
    first_half(2)
    cross(2)
    second_half(0)
    total = smooth(0, total)
    cross(2)
    grads(0)
    second_half(1)
    total = smooth(1, total)
    first_half(3)
    cross(2)
    grads_over(0)
    grads_cross(1, 0)
    grads(1)
    cross(1)
    second_half(2)
    total = smooth(2, total)
    second_half(3)
    total = smooth(3, total)

    bsend[...] = jnp.sum(total, axis=0, keepdims=True)

    def cols(p):
        return slice(p * quarter, (p + 1) * quarter)

    fine = kb == half
    if not fine:
        for chunk in range(ncol * HALVES):
            rows_in = half_of(merged.at[chunk // HALVES], chunk % HALVES)
            wacc[chunk * half : (chunk + 1) * half, :] = tn(rows_in, glow[...])

    def block_rows(b, count=1):
        return pl.ds(pl.multiple_of(b * kb, kb), count * kb)

    def weight_chunk(b, h):
        hs = slice(h * half, (h + 1) * half)
        if not fine:
            return wacc[block_rows(b), hs]
        q, at = lax.div(b, HALVES), lax.rem(b, HALVES) * per_half
        rows_in = jnp.concatenate([merged[q, at + p] for p in range(per_half)], axis=1)
        return tn(rows_in, glow[:, hs])

    low = zz < depth // 2
    ahead = jnp.where(low, depth - 1 - zz, zz)

    def place(k):
        up = jnp.where(k < ahead, depth - 1 - k, k - ahead)
        return jnp.where(low, up, depth - 1 - up)

    def weight_out(h, k):
        z = place(k)
        theirs, mine = z * 2 + 1 - yy, z * 2 + yy
        term = weight_chunk(theirs, h)
        for p in range(h * per_half, (h + 1) * per_half):
            piece = term[:, (p - h * per_half) * quarter : (p - h * per_half + 1) * quarter]
            ysend[p, z] = piece.astype(bf16)
            put(ysend.at[p, z], yrecv.at[p, z], y_s.at[p, z], y_r.at[p, z], ypeer)
        if fine:
            wacc[block_rows(mine), h * half : (h + 1) * half] = weight_chunk(mine, h)

    before, after = me - 2, me + 2

    def line_sum(p, z, total, out, came_before, came_after):
        out[z] = total.astype(bf16)

        @pl.when(z > zz)
        def _():
            @pl.when(zz > 0)
            def _():
                got(came_before.at[z], fb_r.at[p, z])
                out[z] = (total + came_before[z].astype(f32)).astype(bf16)

            start(out.at[z], came_before.at[z], z_s.at[p, z], fb_r.at[p, z], (after, col))

        @pl.when(z < zz)
        def _():
            @pl.when(zz < depth - 1)
            def _():
                got(came_after.at[z], fa_r.at[p, z])
                out[z] = (total + came_after[z].astype(f32)).astype(bf16)

            start(out.at[z], came_after.at[z], z_s.at[p, z], fa_r.at[p, z], (before, col))

    def line_end(p, rows_in, came_before, came_after):
        @pl.when(zz > 0)
        def _():
            got(came_before.at[zz], fb_r.at[p, zz])
            wacc[rows_in, cols(p)] += came_before[zz].astype(f32)

        @pl.when(zz < depth - 1)
        def _():
            got(came_after.at[zz], fa_r.at[p, zz])
            wacc[rows_in, cols(p)] += came_after[zz].astype(f32)

    def line_share(p, z, block, up=True, down=True):
        if up:
            @pl.when(zz < depth - 1)
            def _():
                start(block, block, zu_s.at[p, z], zg_r.at[p, z], (after, col))
        if down:
            @pl.when(zz > 0)
            def _():
                start(block, block, zd_s.at[p, z], zg_r.at[p, z], (before, col))

    def sent_line(p, z, out, block):
        @pl.when(z != zz)
        def _():
            sent(out.at[z], z_s.at[p, z])

        @pl.when((z <= zz) & (zz < depth - 1))
        def _():
            sent(block, zu_s.at[p, z])

        @pl.when((z >= zz) & (zz > 0))
        def _():
            sent(block, zd_s.at[p, z])

    def weight_sum(p, k):
        z = place(k)
        got(yrecv.at[p, z], y_r.at[p, z])
        rows_in = block_rows(z * 2 + yy)
        total = wacc[rows_in, cols(p)] + yrecv[p, z].astype(f32)
        if k < depth - 1:
            line_sum(p, z, total, zsend.at[p], from_before.at[p], from_after.at[p])
            return
        wacc[rows_in, cols(p)] = total
        line_end(p, rows_in, from_before.at[p], from_after.at[p])
        wfin[p, me] = wacc[rows_in, cols(p)].astype(bf16)
        line_share(p, zz, wfin.at[p, me])
        across(p, zz)

    def across(p, z):
        block = wfin.at[p, z * 2 + yy]
        start(block, block, yg_s.at[p, z], yg_r.at[p, z], ypeer)

    def weight_on(p, d):
        @pl.when(zz >= d)
        def _():
            block = wfin.at[p, me - 2 * d]
            got(block, zg_r.at[p, zz - d])
            line_share(p, zz - d, block, down=False)
            across(p, zz - d)

        @pl.when(zz + d < depth)
        def _():
            block = wfin.at[p, me + 2 * d]
            got(block, zg_r.at[p, zz + d])
            line_share(p, zz + d, block, up=False)
            across(p, zz + d)

    def weight_end(p):
        for z in range(depth):
            got(wfin.at[p, z * 2 + 1 - yy], yg_r.at[p, z])
            sent(wfin.at[p, z * 2 + yy], yg_s.at[p, z])
            sent_line(p, z, zsend.at[p], wfin.at[p, z * 2 + yy])

    for k in range(depth):
        weight_out(HALVES - 1, k)
        if k == 1:
            grads_over(1)
            grads(2)
    weight_out(0, 0)
    grads_over(2)
    grads(3)
    weight_out(0, 1)
    grads_over(3)
    for k in range(2, depth):
        weight_out(0, k)
    for r in range(1, BLOCKS):
        grads_cross(1, r)

    def bias_copy(t):
        pltpu.make_async_remote_copy(
            src_ref=bsend, dst_ref=brecv.at[me], send_sem=b_s.at[t], recv_sem=b_r.at[me],
            device_id=(t, col), device_id_type=MESH,
        ).start()

    peers(bias_copy)

    def act_over(r):
        piece = act.at[col, pl.ds(r * rb, rb)]
        put(piece, piece, ax_s.at[r], ax_r.at[r], (me, xcol))

    own_act = act.at[col]
    put(own_act, own_act, ac_s.at[0], ac_r.at[0], (me, pair))

    def back_copy(q, t):
        pltpu.make_async_remote_copy(
            src_ref=outg.at[q, t], dst_ref=ret.at[q, me],
            send_sem=ret_s.at[q, t], recv_sem=ret_r.at[q, me], device_id=(t, col), device_id_type=MESH,
        ).start()

    def send_back(h):
        quarters = range(h * per_half, (h + 1) * per_half)
        for q in quarters:
            peers(lambda t: sent(outg.at[q, t], in_s.at[q, t]))
        for g in range(groups):
            if groups > 1:
                far_group(g)
            whole = jnp.concatenate([far[r] for r in range(BLOCKS)], axis=1)
            pool_grad = nn(whole, gm[:, h * half : (h + 1) * half]).astype(bf16)
            for i, q in enumerate(quarters):
                piece = pool_grad[:, i * quarter : (i + 1) * quarter]
                outg[q, g * gd : (g + 1) * gd] = piece.reshape(gd, slots, quarter)
        for q in quarters:
            peers(functools.partial(back_copy, q))
            ret[q, me] = jnp.zeros((slots, quarter), bf16)

    def near_back(r):
        rs = slice(r * rb, (r + 1) * rb)
        wide[rs, :] = nn(jnp.concatenate([near[b, rs] for b in range(BLOCKS)], axis=1), gm[...])

    def input_grad(h):
        hs = slice(h * half, (h + 1) * half)
        for q in range(h * per_half, (h + 1) * per_half):
            peers(lambda s: got(ret.at[q, s], ret_r.at[q, s]))
        for g in range(groups):
            if groups > 1:
                put_selector(g)
            back = half_of(ret, h, slice(g * gd, (g + 1) * gd)).reshape(gs, half)
            for r in range(BLOCKS):
                rs = slice(r * rb, (r + 1) * rb)
                wide[rs, hs] += tn(sel[:, rs], back)
        ig_out[:, hs] = wide[:, hs].astype(bf16)

    def act_on(r):
        piece = act.at[xcol, pl.ds(r * rb, rb)]
        got(piece, ax_r.at[r])
        put(piece, piece, af_s.at[r], af_r.at[r], (me, pair))

    events = []

    def at(when, step, *args):
        events.append((when, len(events), functools.partial(step, *args)))

    unit = 4.0 / depth
    for k in range(depth):
        for i, p in enumerate(PIECES):
            at(TIMES["sum"] + 11.2 * (i // 2) + 2.8 * unit * k + (TIMES["own"] if k == depth - 1 else 0.0), weight_sum, p, k)
    for d in range(1, depth):
        for i, p in enumerate(PIECES):
            at(TIMES["on"] + 11.2 * (i // 2) + TIMES["hop"] * d, weight_on, p, d)
    crossed = ((0, 0), (1, 0), (0, 1), (0, 2), (0, 3), (1, 1), (1, 2), (1, 3))
    for when, (h, r) in zip(TIMES["in"], crossed):
        at(when, grads_in, h, r)
    for r in range(BLOCKS):
        at(TIMES["act"] + 5.7 * r, act_on, r)
        at(TIMES["near"] + 0.01 * r, near_back, r)
        at(TIMES["over"][0 if r == 0 else 1], act_over, r)
    for h in range(HALVES):
        at(TIMES["back"][h], send_back, h)
        at(TIMES["input"][h], input_grad, h)
    for _, _, step in sorted(events, key=lambda event: event[:2]):
        step()

    got(act.at[pair], ac_r.at[0])
    peers(lambda s: got(brecv.at[s], b_r.at[s]))
    brecv[me] = bsend[...]
    bg_out[...] = jnp.sum(brecv[...], axis=0)
    for r in range(BLOCKS):
        got(act.at[dcol, pl.ds(r * rb, rb)], af_r.at[r])
    for p in PIECES:
        weight_end(p)

    peers(lambda t: sent(bsend, b_s.at[t]))
    for q in range(QUARTERS):
        peers(lambda t: sent(outg.at[q, t], ret_s.at[q, t]))
    for copy in pending:
        copy.wait_send()


WRITES = 8


def store(act, ig, wg, bg, act_out, ig_out, wg_out, bg_out, wide, some_s, wg_s):
    ncol, part = act.shape[0], act.shape[2]
    copies = []
    for q in range(ncol):
        copies.append(pltpu.make_async_copy(act.at[q], act_out.at[:, q * part : (q + 1) * part], some_s.at[q]))
        copies[-1].start()
    copies.append(pltpu.make_async_copy(ig, ig_out, some_s.at[ncol]))
    copies[-1].start()
    tall = wide.shape[0] // WRITES
    group, quarter = wg.shape[1] // WRITES, wg.shape[3]
    for p in range(WRITES):
        rs = slice(p * tall, (p + 1) * tall)
        for c in range(QUARTERS):
            piece = wg[c, p * group : (p + 1) * group].reshape(tall, quarter)
            wide[rs, c * quarter : (c + 1) * quarter] = piece.astype(f32)
        copies.append(pltpu.make_async_copy(wide.at[rs], wg_out.at[rs], wg_s.at[p]))
        copies[-1].start()
    bg_out[...] = bg[...]
    for copy in copies:
        copy.wait()


def local(
    features, weight, layer_bias, cotangent, self_weight, local_index, local_weight, send_index, remote_slot, remote_weight,
    *, n, ncol,
):
    rows, part = features.shape
    width = weight.shape[0]
    slots = send_index.shape[2]
    half, quarter, rb = part // HALVES, part // QUARTERS, rows // BLOCKS
    gs = min(8, n) * slots
    depth, kb = n // 2, width // n
    edges_near, edges_far = local_index.shape[1], remote_slot.shape[1]
    edges = edges_near + 1 + edges_far
    vmem = pl.BlockSpec(memory_space=pltpu.VMEM)
    hbm = pl.BlockSpec(memory_space=pl.ANY)
    V = pltpu.VMEM
    S = lambda *shape: pltpu.SemaphoreType.DMA(shape)
    buffers = [
        V((rows, part), bf16), V((width, part), bf16), V((part,), bf16), V((rows, part), bf16), V((1, rows), f32),
        V((edges_near, rows), i32), V((edges_near, rows), f32), V((n, slots), i32), V((edges_far, rows), i32), V((edges_far, rows), f32),
        V((gs, rows), bf16), V((BLOCKS, rows, rb), bf16), V((BLOCKS, gs, rb), bf16),
        V((rows if n <= 8 else rb, gs), bf16),
        V((edges, 8, rows), i32), V((edges, 8, rows), f32),
        V((QUARTERS, n, slots, quarter), bf16), V((QUARTERS, n, slots, quarter), bf16), V((rows, part), f32),
        V((ncol, QUARTERS, rows, quarter), bf16), V((rows, part), bf16),
        V((rows, part), f32), V((rows, part), f32),
        V((BLOCKS, 2, rb, part), bf16), V((BLOCKS, 2, rb, part), bf16), *[V((HALVES, BLOCKS, rb, half), bf16) for _ in range(2)],
        V((rows, part), bf16), V((width, part), f32),
        *[V((QUARTERS, depth, kb, quarter), bf16) for _ in range(2)],
        *[V((len(PIECES), depth, kb, quarter), bf16) for _ in range(3)],
        V((1, part), f32), V((n, 1, part), f32), V((QUARTERS, n, slots, quarter), bf16),
    ]
    semaphores = [
        S(10), S(QUARTERS, n), S(QUARTERS, n), S(2, BLOCKS), S(2, BLOCKS),
        *[S(QUARTERS, BLOCKS) for _ in range(6)],
        S(BLOCKS), S(BLOCKS), S(HALVES, BLOCKS), S(HALVES, BLOCKS),
        *[S(QUARTERS, depth) for _ in range(10)],
        S(n), S(n), S(QUARTERS, n), S(QUARTERS, n),
        S(BLOCKS), S(BLOCKS), S(1), S(1), S(BLOCKS), S(BLOCKS),
    ]
    results = pl.pallas_call(
        functools.partial(layer, n=n, ncol=ncol),
        out_shape=(
            V((ncol, rows, part), bf16),
            V((rows, part), bf16),
            V((QUARTERS, n, kb, quarter), bf16),
            V((1, part), f32),
        ),
        in_specs=[hbm] * 10,
        out_specs=(vmem,) * 4,
        scratch_shapes=buffers + semaphores,
        compiler_params=pltpu.CompilerParams(
            collective_id=0, has_side_effects=True, vmem_limit_bytes=54 << 20
        ),
        cost_estimate=pl.CostEstimate(flops=11 << 30, bytes_accessed=16 << 20, transcendentals=1 << 20),
    )(
        features, weight, layer_bias, cotangent, self_weight[None, :], local_index.T, local_weight.T,
        send_index[0], remote_slot.T, remote_weight.T,
    )
    output, input_grad, weight_grad, bias_grad = pl.pallas_call(
        store,
        out_shape=(
            jax.ShapeDtypeStruct((rows, ncol * part), bf16),
            jax.ShapeDtypeStruct((rows, part), bf16),
            jax.ShapeDtypeStruct((width, part), f32),
            jax.ShapeDtypeStruct((1, part), f32),
        ),
        in_specs=[vmem] * 4,
        out_specs=(hbm, hbm, hbm, vmem),
        scratch_shapes=[V((width, part), f32), S(ncol + 1), S(WRITES)],
        compiler_params=pltpu.CompilerParams(vmem_limit_bytes=6 << 20),
        cost_estimate=pl.CostEstimate(flops=0, bytes_accessed=10 << 20, transcendentals=0),
    )(*results)
    return output, input_grad, weight_grad, bias_grad[0]


def solution(mesh):
    placed = (
        P("clu", "col"),
        P(None, "col"),
        P("col"),
        P("clu", "col"),
        P("clu"),
        P("clu", None),
        P("clu", None),
        P("clu", None, None),
        P("clu", None),
        P("clu", None),
    )
    return jax.shard_map(
        functools.partial(local, n=mesh.shape["clu"], ncol=mesh.shape["col"]),
        mesh=mesh,
        in_specs=placed,
        out_specs=(P("clu", None), P("clu", "col"), P(None, "col"), P("col")),
        check_vma=False,
    )
```

```python
import functools
import math

import jax
import jax.numpy as jnp
from jax import lax
from jax.experimental import pallas as pl
from jax.experimental.pallas import tpu as pltpu
from jax.sharding import PartitionSpec as P

enhance = 1.0
f32, bf16, i32 = jnp.float32, jnp.bfloat16, jnp.int32
MESH = pl.DeviceIdType.MESH
BLOCKS = 4
HALVES = 2
QUARTERS = 4
PIECES = (3, 2, 1, 0)
TIMES = {"sum": 3.8, "own": 2.0, "on": (17.5, 26.5), "hop": 3.3, "in": (0.5, 3.0, 6.0, 10.0, 13.0, 16.0, 18.5, 21.3), "act": 27.0, "near": 21.6, "over": (18.6, 21.4), "back": (13.2, 21.5), "input": (31.0, 37.0)}
UNROLL = 8
ORDER = (
    (0, 0), (0, 1), (1, 0), (1, 1), (0, 2), (1, 2), (2, 0), (2, 1), (2, 2),
    (3, 0), (0, 3), (3, 1), (1, 3), (3, 2), (2, 3), (3, 3),
)


def tn(a, b):
    return lax.dot_general(a, b, (((0,), (0,)), ((), ())), preferred_element_type=f32)


def nt(a, b):
    return lax.dot_general(a, b, (((1,), (1,)), ((), ())), preferred_element_type=f32)


def nn(a, b):
    return jnp.dot(a, b, preferred_element_type=f32)


def layer(
    feat_in, weight_in, bias_in, cot_in, selfw_in, lidx_in, lwgt_in, send_in, ridx_in, rwgt_in,
    act, ig_out, wfin, bg_out,
    feat, w_v, bias, cot_v, selfw, lidx, lwgt, send, ridx, rwgt, sel, near, far, turned, edge_pos, edge_w, outg, incg, wide, merged, glow, keep_own, keep_far,
    csend, crecv, xsend, xrecv, gm, wacc, ysend, yrecv, zsend, from_before, from_after, bsend, brecv, ret,
    load_s, in_s, in_r, tab_s, tab_r, mx_s, mx_r, mc_s, mc_r, mf_s, mf_r, rc_s, rc_r, rx_s, rx_r,
    y_s, y_r, z_s, fb_r, fa_r, zu_s, zd_s, zg_r, yg_s, yg_r, b_s, b_r, ret_s, ret_r, ax_s, ax_r, ac_s, ac_r, af_s, af_r,
    *, n, ncol,
):
    rows, part = feat_in.shape
    half, quarter = part // HALVES, part // QUARTERS
    per_half = QUARTERS // HALVES
    rb = rows // BLOCKS
    slots = send.shape[1]
    gd = min(8, n)
    groups = n // gd
    gs = gd * slots
    depth = n // 2
    kb = wacc.shape[0] // n

    me = lax.axis_index("clu")
    col = lax.axis_index("col")
    zz, yy = lax.div(me, 2), lax.rem(me, 2)
    core = lax.rem(col, 2)
    pair = col + 1 - 2 * core
    xcol = lax.rem(col + ncol // 2, ncol)
    dcol = lax.rem(pair + ncol // 2, ncol)
    ypeer = (me + 1 - 2 * yy, col)
    pending = []

    def start(src, dst, ss, rs, dev):
        copy = pltpu.make_async_remote_copy(
            src_ref=src, dst_ref=dst, send_sem=ss, recv_sem=rs, device_id=dev, device_id_type=MESH
        )
        copy.start()
        return copy

    def put(*args):
        pending.append(start(*args))

    def got(dst, rs):
        pltpu.make_async_remote_copy(
            src_ref=dst, dst_ref=dst, send_sem=rs, recv_sem=rs, device_id=(me, pair), device_id_type=MESH
        ).wait_recv()

    def sent(src, ss):
        pltpu.make_async_remote_copy(
            src_ref=src, dst_ref=src, send_sem=ss, recv_sem=ss, device_id=(me, pair), device_id_type=MESH
        ).wait_send()

    def peers(step):
        def body(k, carry):
            step(lax.rem(me + k, n))
            return carry

        lax.fori_loop(1, n, body, 0)

    loads = [
        pltpu.make_async_copy(src, dst, load_s.at[at])
        for at, (src, dst) in enumerate((
            (send_in, send), (feat_in, feat), (lidx_in, lidx), (lwgt_in, lwgt), (selfw_in, selfw), (ridx_in, ridx),
            (rwgt_in, rwgt), (bias_in, bias), (weight_in, w_v), (cot_in, cot_v),
        ))
    ]
    barrier = pltpu.get_barrier_semaphore()
    peers(lambda t: pl.semaphore_signal(barrier, inc=1, device_id=(t, col), device_id_type=MESH))
    for other in (pair, xcol):
        pl.semaphore_signal(barrier, inc=1, device_id=(me, other), device_id_type=MESH)
    for load in loads:
        load.start()
    for load in loads[:2]:
        load.wait()

    lane = lax.broadcasted_iota(i32, (slots, rows), 1)

    def put_selector(g):
        ids = send[g * gd : (g + 1) * gd, :].T
        for d in range(gd):
            sel[d * slots : (d + 1) * slots, :] = jnp.where(ids[:, d : d + 1] == lane, 1.0, 0.0).astype(bf16)

    def half_of(ref, h, *at):
        return jnp.concatenate([ref[(h * per_half + p, *at)] for p in range(per_half)], axis=-1)

    def in_copy(q, t):
        pltpu.make_async_remote_copy(
            src_ref=outg.at[q, t], dst_ref=incg.at[q, me], send_sem=in_s.at[q, t], recv_sem=in_r.at[q, me],
            device_id=(t, col), device_id_type=MESH,
        ).start()

    for q in range(QUARTERS):
        if q % per_half == 0:
            for g in range(groups):
                if groups > 1 or q == 0:
                    put_selector(g)
                at = q // per_half * half
                rows_out = nn(sel[...], feat[:, at : at + half]).astype(bf16)
                for p in range(per_half):
                    piece = rows_out[:, p * quarter : (p + 1) * quarter].reshape(gd, slots, quarter)
                    outg[q // per_half * per_half + p, g * gd : (g + 1) * gd] = piece
        if q == 0:
            pl.semaphore_wait(barrier, n + 1)
        peers(functools.partial(in_copy, q))
        incg[q, me] = jnp.zeros((slots, quarter), bf16)

    local_edges, far_edges = lidx.shape[0], ridx.shape[0]
    first_far = local_edges + 1

    def put_edges(at, idx, w):
        for k in range(idx.shape[0]):
            edge_pos[at + k] = jnp.broadcast_to(idx[k : k + 1, :], (8, rows))
            edge_w[at + k] = jnp.broadcast_to(w[k : k + 1, :], (8, rows))

    for load in loads[2:7]:
        load.wait()
    put_edges(0, lidx[...], lwgt[...])
    put_edges(local_edges, lax.broadcasted_iota(i32, (1, rows), 1), (1.0 + enhance) * selfw[...])
    put_edges(first_far, ridx[...], rwgt[...])
    sub = lax.broadcasted_iota(i32, (8, 128), 0)

    def table(dst, block, first, count, base, edge_from, edge_to):
        tall = 16 * UNROLL

        def lanes(l, carry):
            ls = pl.ds(pl.multiple_of(l * 128, 128), 128)

            def step(b, carry):
                r0 = first + b * tall
                places = [sub + (base + r0 + 8 * u) for u in range(2 * UNROLL)]
                sums = [jnp.zeros((8, 128), f32)] * (2 * UNROLL)
                for k in range(edge_from, edge_to):
                    at, w = edge_pos[k, :, ls], edge_w[k, :, ls]
                    sums = [s + jnp.where(at == p, w, 0.0) for s, p in zip(sums, places)]
                inner = pl.ds(pl.multiple_of(l * 128 - block * rb, 128), 128)
                dst[block, pl.ds(pl.multiple_of(r0, 16), tall), inner] = jnp.concatenate(sums, 0).astype(bf16)
                return carry

            return lax.fori_loop(0, count // tall, step, carry)

        lax.fori_loop(block * rb // 128, (block + 1) * rb // 128, lanes, 0)

    def shared_part(dst, r, whose):
        count = dst.shape[1] // 2
        return dst.at[r, pl.ds(pl.multiple_of(whose * count, count), count)]

    def shared_table(dst, which, r, edge_from, edge_to):
        count = dst.shape[1] // 2
        table(dst, r, core * count, count, 0, edge_from, edge_to)
        piece = shared_part(dst, r, core)
        put(piece, piece, tab_s.at[which, r], tab_r.at[which, r], (me, pair))

    def far_group(g):
        for r in range(BLOCKS):
            table(far, r, 0, gs, g * gs, first_far, first_far + far_edges)

    def build(r):
        shared_table(near, 0, r, 0, first_far)
        if groups == 1:
            shared_table(far, 1, r, first_far, first_far + far_edges)

    def ready(r):
        rs = slice(r * rb, (r + 1) * rb)
        got(shared_part(near, r, 1 - core), tab_r.at[0, r])
        wide[rs, :] = tn(near[r], feat[...])
        if groups == 1:
            got(shared_part(far, r, 1 - core), tab_r.at[1, r])
            turned[rs, :] = far[r].T

    def arrived(q):
        peers(lambda s: got(incg.at[q, s], in_r.at[q, s]))

    def piece_of(owner, q, r):
        return merged.at[owner, q, pl.ds(r * rb, rb)]

    def aggregate(q, r):
        rs = slice(r * rb, (r + 1) * rb)
        total = wide[rs, q * quarter : (q + 1) * quarter]
        if groups == 1:
            total = total + nn(turned[rs, :], incg[q].reshape(gs, quarter))
        merged[col, q, rs] = total.astype(bf16)
        piece = piece_of(col, q, r)
        put(piece, piece, mx_s.at[q, r], mx_r.at[q, r], (me, xcol))
        put(piece, piece, mc_s.at[q, r], mc_r.at[q, r], (me, pair))

    build(0)
    build(1)
    ready(0)
    if groups > 1:
        for r in range(2, BLOCKS):
            build(r)
        for r in range(1, BLOCKS):
            ready(r)
        for q in range(QUARTERS):
            arrived(q)
        for g in range(groups):
            far_group(g)
            for r in range(BLOCKS):
                rs = slice(r * rb, (r + 1) * rb)
                turned[...] = far[r].T
                for q in range(QUARTERS):
                    pooled = incg[q, g * gd : (g + 1) * gd].reshape(gs, quarter)
                    wide[rs, q * quarter : (q + 1) * quarter] += nn(turned[...], pooled)
        for q, r in ORDER:
            aggregate(q, r)
    else:
        arrived(0)
        aggregate(0, 0)
        ready(1)
        aggregate(0, 1)
        build(2)
        arrived(1)
        aggregate(1, 0)
        aggregate(1, 1)
        ready(2)
        aggregate(0, 2)
        aggregate(1, 2)
        build(3)
        arrived(2)
        for r in range(3):
            aggregate(2, r)
        ready(3)
        arrived(3)
        for q, r in ORDER[9:]:
            aggregate(q, r)

    for load in loads[7:]:
        load.wait()

    def cross(count):
        for q, r in [crossing.pop(0) for _ in range(count)]:
            piece = piece_of(xcol, q, r)
            got(piece, mx_r.at[q, r])
            put(piece, piece, mf_s.at[q, r], mf_r.at[q, r], (me, pair))

    def whole_rows(h, r):
        for q in range(h * per_half, (h + 1) * per_half):
            got(piece_of(pair, q, r), mc_r.at[q, r])
            got(piece_of(dcol, q, r), mf_r.at[q, r])

    crossing = list(ORDER)

    def products(h, r):
        total = None
        for q in range(ncol):
            k0 = q * part + h * half
            term = nn(half_of(merged.at[q], h, slice(r * rb, (r + 1) * rb)), w_v[k0 : k0 + half, :])
            total = term if total is None else total + term
        return total

    def first_half(r):
        whole_rows(0, r)
        wide[r * rb : (r + 1) * rb, :] = products(0, r) + bias[...].astype(f32).reshape(1, part)

    def second_half(r):
        whole_rows(1, r)
        wide[r * rb : (r + 1) * rb, :] += products(1, r)

    tall = 32

    def smooth(r, total):
        def step(b, total):
            rs = pl.ds(pl.multiple_of(r * rb + b * tall, tall), tall)
            v = wide[rs, :]
            cdf = 0.5 + 0.5 * lax.erf(v * (1.0 / math.sqrt(2.0)))
            act[col, rs, :] = (v * cdf).astype(bf16)
            density = jnp.exp(v * v * -0.5) * (1.0 / math.sqrt(2.0 * math.pi))
            low = (cot_v[rs, :].astype(f32) * (cdf + v * density)).astype(bf16)
            glow[rs, :] = low
            return total + jnp.sum(low.astype(f32).reshape(tall // 8, 8, part), axis=0)

        return lax.fori_loop(0, rb // tall, step, total)

    def grads(r):
        rs = slice(r * rb, (r + 1) * rb)
        low = glow[rs, :]

        def term(q):
            return nt(low, w_v[pl.ds(pl.multiple_of(q * part, part), part), :])

        csend[r, 0] = term(pair).astype(bf16)
        csend[r, 1] = term(dcol).astype(bf16)
        put(csend.at[r], crecv.at[r], rc_s.at[r], rc_r.at[r], (me, pair))
        keep_own[rs, :] = term(col)
        keep_far[rs, :] = term(xcol)

    def grads_over(r):
        rs = slice(r * rb, (r + 1) * rb)
        got(crecv.at[r], rc_r.at[r])
        both_halves = (keep_far[rs, :] + crecv[r, 1].astype(f32)).astype(bf16)
        for h in range(HALVES):
            xsend[h, r] = both_halves[:, h * half : (h + 1) * half]
        grads_cross(0, r)
        keep_own[rs, :] += crecv[r, 0].astype(f32)

    def grads_cross(h, r):
        put(xsend.at[h, r], xrecv.at[h, r], rx_s.at[h, r], rx_r.at[h, r], (me, xcol))

    def grads_in(h, r):
        rs, hs = slice(r * rb, (r + 1) * rb), slice(h * half, (h + 1) * half)
        got(xrecv.at[h, r], rx_r.at[h, r])
        gm[rs, hs] = (keep_own[rs, hs] + xrecv[h, r].astype(f32)).astype(bf16)

    total = jnp.zeros((8, part), f32)
    cross(4)
    first_half(0)
    cross(2)
    first_half(1)
    cross(3)
    first_half(2)
    cross(2)
    second_half(0)
    total = smooth(0, total)
    cross(2)
    grads(0)
    second_half(1)
    total = smooth(1, total)
    first_half(3)
    cross(2)
    grads_over(0)
    grads_cross(1, 0)
    grads(1)
    cross(1)
    second_half(2)
    total = smooth(2, total)
    second_half(3)
    total = smooth(3, total)

    bsend[...] = jnp.sum(total, axis=0, keepdims=True)

    def cols(p):
        return slice(p * quarter, (p + 1) * quarter)

    fine = kb == half
    if not fine:
        for chunk in range(ncol * HALVES):
            rows_in = half_of(merged.at[chunk // HALVES], chunk % HALVES)
            wacc[chunk * half : (chunk + 1) * half, :] = tn(rows_in, glow[...])

    def block_rows(b, count=1):
        return pl.ds(pl.multiple_of(b * kb, kb), count * kb)

    def weight_chunk(b, h):
        hs = slice(h * half, (h + 1) * half)
        if not fine:
            return wacc[block_rows(b), hs]
        q, at = lax.div(b, HALVES), lax.rem(b, HALVES) * per_half
        rows_in = jnp.concatenate([merged[q, at + p] for p in range(per_half)], axis=1)
        return tn(rows_in, glow[:, hs])

    low = zz < depth // 2
    ahead = jnp.where(low, depth - 1 - zz, zz)

    def place(k):
        up = jnp.where(k < ahead, depth - 1 - k, k - ahead)
        return jnp.where(low, up, depth - 1 - up)

    def weight_out(h, k):
        z = place(k)
        theirs, mine = z * 2 + 1 - yy, z * 2 + yy
        term = weight_chunk(theirs, h)
        for p in range(h * per_half, (h + 1) * per_half):
            piece = term[:, (p - h * per_half) * quarter : (p - h * per_half + 1) * quarter]
            ysend[p, z] = piece.astype(bf16)
            put(ysend.at[p, z], yrecv.at[p, z], y_s.at[p, z], y_r.at[p, z], ypeer)
        if fine:
            wacc[block_rows(mine), h * half : (h + 1) * half] = weight_chunk(mine, h)

    before, after = me - 2, me + 2

    def line_sum(p, z, total, out, came_before, came_after):
        out[z] = total.astype(bf16)

        @pl.when(z > zz)
        def _():
            @pl.when(zz > 0)
            def _():
                got(came_before.at[z], fb_r.at[p, z])
                out[z] = (total + came_before[z].astype(f32)).astype(bf16)

            start(out.at[z], came_before.at[z], z_s.at[p, z], fb_r.at[p, z], (after, col))

        @pl.when(z < zz)
        def _():
            @pl.when(zz < depth - 1)
            def _():
                got(came_after.at[z], fa_r.at[p, z])
                out[z] = (total + came_after[z].astype(f32)).astype(bf16)

            start(out.at[z], came_after.at[z], z_s.at[p, z], fa_r.at[p, z], (before, col))

    def line_end(p, rows_in, came_before, came_after):
        @pl.when(zz > 0)
        def _():
            got(came_before.at[zz], fb_r.at[p, zz])
            wacc[rows_in, cols(p)] += came_before[zz].astype(f32)

        @pl.when(zz < depth - 1)
        def _():
            got(came_after.at[zz], fa_r.at[p, zz])
            wacc[rows_in, cols(p)] += came_after[zz].astype(f32)

    def line_share(p, z, block, up=True, down=True):
        if up:
            @pl.when(zz < depth - 1)
            def _():
                start(block, block, zu_s.at[p, z], zg_r.at[p, z], (after, col))
        if down:
            @pl.when(zz > 0)
            def _():
                start(block, block, zd_s.at[p, z], zg_r.at[p, z], (before, col))

    def sent_line(p, z, out, block):
        @pl.when(z != zz)
        def _():
            sent(out.at[z], z_s.at[p, z])

        @pl.when((z <= zz) & (zz < depth - 1))
        def _():
            sent(block, zu_s.at[p, z])

        @pl.when((z >= zz) & (zz > 0))
        def _():
            sent(block, zd_s.at[p, z])

    def weight_sum(p, k):
        z = place(k)
        got(yrecv.at[p, z], y_r.at[p, z])
        rows_in = block_rows(z * 2 + yy)
        total = wacc[rows_in, cols(p)] + yrecv[p, z].astype(f32)
        if k < depth - 1:
            line_sum(p, z, total, zsend.at[p], from_before.at[p], from_after.at[p])
            return
        wacc[rows_in, cols(p)] = total
        line_end(p, rows_in, from_before.at[p], from_after.at[p])
        wfin[p, me] = wacc[rows_in, cols(p)].astype(bf16)
        line_share(p, zz, wfin.at[p, me])
        across(p, zz)

    def across(p, z):
        block = wfin.at[p, z * 2 + yy]
        start(block, block, yg_s.at[p, z], yg_r.at[p, z], ypeer)

    def weight_on(p, d):
        @pl.when(zz >= d)
        def _():
            block = wfin.at[p, me - 2 * d]
            got(block, zg_r.at[p, zz - d])
            line_share(p, zz - d, block, down=False)
            across(p, zz - d)

        @pl.when(zz + d < depth)
        def _():
            block = wfin.at[p, me + 2 * d]
            got(block, zg_r.at[p, zz + d])
            line_share(p, zz + d, block, up=False)
            across(p, zz + d)

    def weight_end(p):
        for z in range(depth):
            got(wfin.at[p, z * 2 + 1 - yy], yg_r.at[p, z])
            sent(wfin.at[p, z * 2 + yy], yg_s.at[p, z])
            sent_line(p, z, zsend.at[p], wfin.at[p, z * 2 + yy])

    for k in range(depth):
        weight_out(HALVES - 1, k)
        if k == 1:
            grads_over(1)
            grads(2)
    weight_out(0, 0)
    grads_over(2)
    grads(3)
    weight_out(0, 1)
    grads_over(3)
    for k in range(2, depth):
        weight_out(0, k)
    for r in range(1, BLOCKS):
        grads_cross(1, r)

    def bias_copy(t):
        pltpu.make_async_remote_copy(
            src_ref=bsend, dst_ref=brecv.at[me], send_sem=b_s.at[t], recv_sem=b_r.at[me],
            device_id=(t, col), device_id_type=MESH,
        ).start()

    peers(bias_copy)

    def act_over(r):
        piece = act.at[col, pl.ds(r * rb, rb)]
        put(piece, piece, ax_s.at[r], ax_r.at[r], (me, xcol))

    own_act = act.at[col]
    put(own_act, own_act, ac_s.at[0], ac_r.at[0], (me, pair))

    def back_copy(q, t):
        pltpu.make_async_remote_copy(
            src_ref=outg.at[q, t], dst_ref=ret.at[q, me],
            send_sem=ret_s.at[q, t], recv_sem=ret_r.at[q, me], device_id=(t, col), device_id_type=MESH,
        ).start()

    def send_back(h):
        quarters = range(h * per_half, (h + 1) * per_half)
        for q in quarters:
            peers(lambda t: sent(outg.at[q, t], in_s.at[q, t]))
        for g in range(groups):
            if groups > 1:
                far_group(g)
            whole = jnp.concatenate([far[r] for r in range(BLOCKS)], axis=1)
            pool_grad = nn(whole, gm[:, h * half : (h + 1) * half]).astype(bf16)
            for i, q in enumerate(quarters):
                piece = pool_grad[:, i * quarter : (i + 1) * quarter]
                outg[q, g * gd : (g + 1) * gd] = piece.reshape(gd, slots, quarter)
        for q in quarters:
            peers(functools.partial(back_copy, q))
            ret[q, me] = jnp.zeros((slots, quarter), bf16)

    def near_back(r):
        rs = slice(r * rb, (r + 1) * rb)
        wide[rs, :] = nn(jnp.concatenate([near[b, rs] for b in range(BLOCKS)], axis=1), gm[...])

    def input_grad(h):
        hs = slice(h * half, (h + 1) * half)
        for q in range(h * per_half, (h + 1) * per_half):
            peers(lambda s: got(ret.at[q, s], ret_r.at[q, s]))
        for g in range(groups):
            if groups > 1:
                put_selector(g)
            back = half_of(ret, h, slice(g * gd, (g + 1) * gd)).reshape(gs, half)
            for r in range(BLOCKS):
                rs = slice(r * rb, (r + 1) * rb)
                wide[rs, hs] += tn(sel[:, rs], back)
        ig_out[:, hs] = wide[:, hs].astype(bf16)

    def act_on(r):
        piece = act.at[xcol, pl.ds(r * rb, rb)]
        got(piece, ax_r.at[r])
        put(piece, piece, af_s.at[r], af_r.at[r], (me, pair))

    events = []

    def at(when, step, *args):
        events.append((when, len(events), functools.partial(step, *args)))

    unit = 4.0 / depth
    for k in range(depth):
        for i, p in enumerate(PIECES):
            at(TIMES["sum"] + 11.2 * (i // 2) + 2.8 * unit * k + (TIMES["own"] if k == depth - 1 else 0.0), weight_sum, p, k)
    for d in range(1, depth):
        for i, p in enumerate(PIECES):
            at(TIMES["on"][i // 2] + TIMES["hop"] * d, weight_on, p, d)
    crossed = ((0, 0), (1, 0), (0, 1), (0, 2), (0, 3), (1, 1), (1, 2), (1, 3))
    for when, (h, r) in zip(TIMES["in"], crossed):
        at(when, grads_in, h, r)
    for r in range(BLOCKS):
        at(TIMES["act"] + 5.7 * r, act_on, r)
        at(TIMES["near"] + 0.01 * r, near_back, r)
        at(TIMES["over"][0 if r == 0 else 1], act_over, r)
    for h in range(HALVES):
        at(TIMES["back"][h], send_back, h)
        at(TIMES["input"][h], input_grad, h)
    for _, _, step in sorted(events, key=lambda event: event[:2]):
        step()

    got(act.at[pair], ac_r.at[0])
    peers(lambda s: got(brecv.at[s], b_r.at[s]))
    brecv[me] = bsend[...]
    bg_out[...] = jnp.sum(brecv[...], axis=0)
    for r in range(BLOCKS):
        got(act.at[dcol, pl.ds(r * rb, rb)], af_r.at[r])
    for p in PIECES:
        weight_end(p)

    peers(lambda t: sent(bsend, b_s.at[t]))
    for q in range(QUARTERS):
        peers(lambda t: sent(outg.at[q, t], ret_s.at[q, t]))
    for copy in pending:
        copy.wait_send()


WRITES = 8


def store(act, ig, wg, bg, act_out, ig_out, wg_out, bg_out, wide, some_s, wg_s):
    ncol, part = act.shape[0], act.shape[2]
    copies = []
    rb = act.shape[1] // BLOCKS
    for r in range(BLOCKS):
        rs = slice(r * rb, (r + 1) * rb)
        for q in range(ncol):
            out = act_out.at[rs, q * part : (q + 1) * part]
            copies.append(pltpu.make_async_copy(act.at[q, rs], out, some_s.at[r * ncol + q]))
            copies[-1].start()
    copies.append(pltpu.make_async_copy(ig, ig_out, some_s.at[BLOCKS * ncol]))
    copies[-1].start()
    tall = wide.shape[0] // WRITES
    group, quarter = wg.shape[1] // WRITES, wg.shape[3]
    for p in range(WRITES):
        rs = slice(p * tall, (p + 1) * tall)
        for c in range(QUARTERS):
            piece = wg[c, p * group : (p + 1) * group].reshape(tall, quarter)
            wide[rs, c * quarter : (c + 1) * quarter] = piece.astype(f32)
        copies.append(pltpu.make_async_copy(wide.at[rs], wg_out.at[rs], wg_s.at[p]))
        copies[-1].start()
    bg_out[...] = bg[...]
    for copy in copies:
        copy.wait()


def local(
    features, weight, layer_bias, cotangent, self_weight, local_index, local_weight, send_index, remote_slot, remote_weight,
    *, n, ncol,
):
    rows, part = features.shape
    width = weight.shape[0]
    slots = send_index.shape[2]
    half, quarter, rb = part // HALVES, part // QUARTERS, rows // BLOCKS
    gs = min(8, n) * slots
    depth, kb = n // 2, width // n
    edges_near, edges_far = local_index.shape[1], remote_slot.shape[1]
    edges = edges_near + 1 + edges_far
    vmem = pl.BlockSpec(memory_space=pltpu.VMEM)
    hbm = pl.BlockSpec(memory_space=pl.ANY)
    V = pltpu.VMEM
    S = lambda *shape: pltpu.SemaphoreType.DMA(shape)
    buffers = [
        V((rows, part), bf16), V((width, part), bf16), V((part,), bf16), V((rows, part), bf16), V((1, rows), f32),
        V((edges_near, rows), i32), V((edges_near, rows), f32), V((n, slots), i32), V((edges_far, rows), i32), V((edges_far, rows), f32),
        V((gs, rows), bf16), V((BLOCKS, rows, rb), bf16), V((BLOCKS, gs, rb), bf16),
        V((rows if n <= 8 else rb, gs), bf16),
        V((edges, 8, rows), i32), V((edges, 8, rows), f32),
        V((QUARTERS, n, slots, quarter), bf16), V((QUARTERS, n, slots, quarter), bf16), V((rows, part), f32),
        V((ncol, QUARTERS, rows, quarter), bf16), V((rows, part), bf16),
        V((rows, part), f32), V((rows, part), f32),
        V((BLOCKS, 2, rb, part), bf16), V((BLOCKS, 2, rb, part), bf16), *[V((HALVES, BLOCKS, rb, half), bf16) for _ in range(2)],
        V((rows, part), bf16), V((width, part), f32),
        *[V((QUARTERS, depth, kb, quarter), bf16) for _ in range(2)],
        *[V((len(PIECES), depth, kb, quarter), bf16) for _ in range(3)],
        V((1, part), f32), V((n, 1, part), f32), V((QUARTERS, n, slots, quarter), bf16),
    ]
    semaphores = [
        S(10), S(QUARTERS, n), S(QUARTERS, n), S(2, BLOCKS), S(2, BLOCKS),
        *[S(QUARTERS, BLOCKS) for _ in range(6)],
        S(BLOCKS), S(BLOCKS), S(HALVES, BLOCKS), S(HALVES, BLOCKS),
        *[S(QUARTERS, depth) for _ in range(10)],
        S(n), S(n), S(QUARTERS, n), S(QUARTERS, n),
        S(BLOCKS), S(BLOCKS), S(1), S(1), S(BLOCKS), S(BLOCKS),
    ]
    results = pl.pallas_call(
        functools.partial(layer, n=n, ncol=ncol),
        out_shape=(
            V((ncol, rows, part), bf16),
            V((rows, part), bf16),
            V((QUARTERS, n, kb, quarter), bf16),
            V((1, part), f32),
        ),
        in_specs=[hbm] * 10,
        out_specs=(vmem,) * 4,
        scratch_shapes=buffers + semaphores,
        compiler_params=pltpu.CompilerParams(
            collective_id=0, has_side_effects=True, vmem_limit_bytes=54 << 20
        ),
        cost_estimate=pl.CostEstimate(flops=11 << 30, bytes_accessed=16 << 20, transcendentals=1 << 20),
    )(
        features, weight, layer_bias, cotangent, self_weight[None, :], local_index.T, local_weight.T,
        send_index[0], remote_slot.T, remote_weight.T,
    )
    output, input_grad, weight_grad, bias_grad = pl.pallas_call(
        store,
        out_shape=(
            jax.ShapeDtypeStruct((rows, ncol * part), bf16),
            jax.ShapeDtypeStruct((rows, part), bf16),
            jax.ShapeDtypeStruct((width, part), f32),
            jax.ShapeDtypeStruct((1, part), f32),
        ),
        in_specs=[vmem] * 4,
        out_specs=(hbm, hbm, hbm, vmem),
        scratch_shapes=[V((width, part), f32), S(BLOCKS * ncol + 1), S(WRITES)],
        compiler_params=pltpu.CompilerParams(vmem_limit_bytes=6 << 20),
        cost_estimate=pl.CostEstimate(flops=0, bytes_accessed=10 << 20, transcendentals=0),
    )(*results)
    return output, input_grad, weight_grad, bias_grad[0]


def solution(mesh):
    placed = (
        P("clu", "col"),
        P(None, "col"),
        P("col"),
        P("clu", "col"),
        P("clu"),
        P("clu", None),
        P("clu", None),
        P("clu", None, None),
        P("clu", None),
        P("clu", None),
    )
    return jax.shard_map(
        functools.partial(local, n=mesh.shape["clu"], ncol=mesh.shape["col"]),
        mesh=mesh,
        in_specs=placed,
        out_specs=(P("clu", None), P("clu", "col"), P(None, "col"), P("col")),
        check_vma=False,
    )
```
